32 devices in a mesh: dp: 2 (over core), seq: 16 (over z, y, x).
Axes of the slice: x: 2, y: 2, z: 4, core: 2. Of those that a mesh axis runs over, the one named last changes fastest.
Arguments:
- features: bfloat16 [2, 2048, 512], P('dp', 'seq'), may hold values from -40 to 40
- score_cotangent: float32 [2, 2048], P('dp', 'seq'), may hold values from -24 to 24
- projection_weight: bfloat16 [512, 768], replicated, may hold values from -0.25 to 0.25
- squeeze_weight: bfloat16 [64, 768], replicated, may hold values from -0.21875 to 0.21875
- first_weight: bfloat16 [320, 128], replicated, may hold values from -0.3125 to 0.3125
- second_weight: bfloat16 [640, 256], replicated, may hold values from -0.25 to 0.25
- third_weight: bfloat16 [1280, 256], replicated, may hold values from -0.15625 to 0.15625
- final_weight: bfloat16 [768], replicated, may hold values from -0.875 to 0.875
Outputs:
- scores: float32 [2, 2048], P('dp', 'seq')
- feature_grad: float32 [2, 2048, 512], P('dp', 'seq')
- squeeze_grad: float32 [64, 768], P('seq')
- first_grad: float32 [320, 128], P('seq')
- second_grad: float32 [640, 256], P('seq')
- third_grad: float32 [1280, 256], P('seq')
- final_grad: float32 [768], P('seq')
The draws below stay inside these ranges and needn't reach their ends.
All inputs are finite; a program needn't handle non-finite values.
Results may differ from the reference program's by a relative error of at most 0.025.
Values may be sent and summed in bfloat16 or wider, within the bound.
No kernel may reach another device: no remote copies, remote signals or barrier semaphores. Data moves between devices by JAX's collectives and lax.ppermute only.
A program may use at most 64 MiB of HBM per device.

```python
import math
import jax
import jax.numpy as jnp
from jax import lax

D = 768
FEAT = 512
C0 = 64
C1 = 128
C2 = 256
HK = 5
PK = 3
FRAMES = 2048
UTTS = 2


def draw_features(key, part):
    noise_key, row_key, column_key = jax.random.split(key, 3)
    array_shape = (UTTS, FRAMES, FEAT)
    base_values = jnp.clip(jax.random.normal(noise_key, array_shape, jnp.float32), -4.0, 4.0)
    row_scale = jnp.exp(jax.random.uniform(row_key, (UTTS, FRAMES, 1), jnp.float32, math.log(0.3), math.log(3.0)))
    columns = jnp.exp(jax.random.uniform(column_key, (1, 1, FEAT), jnp.float32, math.log(0.3), math.log(3.0)))
    values = base_values * row_scale * columns
    return values.astype(jnp.bfloat16)


def level_of(key, extent, cuts, low, high):
    gain = 1.0
    for dim, parts in cuts:
        draws = jax.random.uniform(jax.random.fold_in(jax.random.fold_in(key, 6), dim), (parts,), jnp.float32, low / len(cuts), high / len(cuts))
        gain = gain * jnp.repeat(jnp.exp(draws), extent[dim] // parts).reshape((-1,) + (1,) * (len(extent) - 1 - dim))
    return gain


def bell_draw(key, extent, width, bound, cuts=(), held_as=jnp.bfloat16):
    result = width * jax.random.normal(key, extent, jnp.float32)
    if cuts:
        result = result * level_of(key, extent, cuts, -0.22, 0.18)
    return jnp.clip(result, -bound, bound).astype(held_as)


def setup_inputs(seed: int = 0) -> dict:
    keys = jax.random.split(jax.random.key(seed), 9)
    return {
        "features": draw_features(jax.random.fold_in(keys[8], 71), 0),
        "score_cotangent": bell_draw(keys[1], (UTTS, FRAMES), 4.0, 24.0, ((0, 2), (1, 16)), jnp.float32),
        "projection_weight": bell_draw(keys[2], (FEAT, D), FEAT ** -0.5, 0.25),
        "squeeze_weight": bell_draw(keys[3], (C0, D), D ** -0.5, 0.21875),
        "first_weight": bell_draw(keys[4], (HK * C0, C1), (HK * C0) ** -0.5, 0.3125),
        "second_weight": bell_draw(keys[5], (HK * C1, C2), (HK * C1) ** -0.5, 0.25),
        "third_weight": bell_draw(keys[6], (HK * C2, C2), (HK * C2) ** -0.5, 0.15625),
        "final_weight": bell_draw(keys[7], (PK * C2,), (PK * C2 // 16) ** -0.5, 0.875),
    }


EPSILON = 1e-05
SLOPE = 0.1

def normalize(values):
    average = lax.optimization_barrier(jnp.mean(values, axis=-1, keepdims=True))
    centred = values - average
    variance = lax.optimization_barrier(jnp.mean(centred * centred, axis=-1, keepdims=True))
    inverse = lax.rsqrt(variance + EPSILON)
    return (centred * inverse, inverse)

def normalize_back(upstream, normed, inverse):
    first_mean = lax.optimization_barrier(jnp.mean(upstream, axis=-1, keepdims=True))
    second_mean = lax.optimization_barrier(jnp.mean(upstream * normed, axis=-1, keepdims=True))
    return (upstream - first_mean - normed * second_mean) * inverse

def gelu_slope(values):
    cumulative = 0.5 * (1.0 + lax.erf(values * math.sqrt(0.5)))
    density = jnp.exp(-0.5 * values * values) / math.sqrt(2.0 * math.pi)
    return cumulative + values * density

def leaky_unit(values):
    return SLOPE * values + (1.0 - SLOPE) * jax.nn.gelu(values, approximate=False)

def leaky_slope(values):
    return SLOPE + (1.0 - SLOPE) * gelu_slope(values)

def convolve(extended, weights):
    return lax.conv_general_dilated(extended, weights, (1,), 'VALID', dimension_numbers=('NWC', 'WIO', 'NWC'), preferred_element_type=jnp.float32)

def flipped_plain(weights):
    return jnp.swapaxes(weights, 1, 2)[::-1]

def tap_gradients(extended, delta, tap_count):
    length = delta.shape[0]
    pieces = [jnp.dot(extended[offset:offset + length].T, delta, preferred_element_type=jnp.float32) for offset in range(tap_count)]
    return jnp.concatenate(pieces, axis=0)

def reference(features, score_cotangent, projection_weight, squeeze_weight, first_weight, second_weight, third_weight, final_weight):
    kernels = [first_weight.reshape(HK, C0, C1), second_weight.reshape(HK, C1, C2), third_weight.reshape(HK, C2, C2)]
    final_kernel = final_weight.reshape(PK, C2, 1)
    final_taps = final_weight.astype(jnp.float32).reshape(PK, C2)
    head_pad = (HK - 1) // 2
    final_pad = (PK - 1) // 2

    def single(inputs):
        feature_rows, cotangent = inputs
        frames = cotangent.shape[0]
        normed_in, inverse_in = normalize(feature_rows.astype(jnp.float32))
        rounded_in = normed_in.astype(jnp.bfloat16)
        projected = jnp.dot(rounded_in, projection_weight, preferred_element_type=jnp.float32).astype(jnp.bfloat16)
        hidden_normed, hidden_inverse = normalize(projected.astype(jnp.float32))
        hidden = hidden_normed.astype(jnp.bfloat16)
        squeezed = lax.dot_general(hidden, squeeze_weight, (((1,), (1,)), ((), ())), preferred_element_type=jnp.float32)
        layer_input = leaky_unit(squeezed).astype(jnp.bfloat16)
        extended_list = []
        action_list = []
        for kernel in kernels:
            extended = jnp.pad(layer_input, ((head_pad, head_pad), (0, 0)))
            action = convolve(extended[None], kernel)[0]
            extended_list.append(extended)
            action_list.append(action)
            layer_input = leaky_unit(action).astype(jnp.bfloat16)
        final_ext = jnp.pad(layer_input, ((final_pad, final_pad), (0, 0)))
        scores = convolve(final_ext[None], final_kernel)[0, :, 0]
        cotangent_ext = jnp.pad(cotangent, (final_pad, final_pad))
        upstream = jnp.zeros((frames, C2), jnp.float32)
        for offset in range(PK):
            upstream = upstream + cotangent_ext[offset:offset + frames, None] * final_taps[PK - 1 - offset][None, :]
        final_grad = jnp.concatenate([jnp.dot(cotangent, final_ext[offset:offset + frames].astype(jnp.float32), precision=lax.Precision.HIGHEST) for offset in range(PK)], axis=0)
        layer_grads = [None, None, None]
        for layer_index in (2, 1, 0):
            delta = (upstream * leaky_slope(action_list[layer_index])).astype(jnp.bfloat16)
            layer_grads[layer_index] = tap_gradients(extended_list[layer_index], delta, HK)
            delta_ext = jnp.pad(delta, ((head_pad, head_pad), (0, 0)))
            upstream = convolve(delta_ext[None], flipped_plain(kernels[layer_index]))[0]
        delta_squeeze = (upstream * leaky_slope(squeezed)).astype(jnp.bfloat16)
        squeeze_grad = jnp.dot(delta_squeeze.T, hidden, preferred_element_type=jnp.float32)
        hidden_upstream = jnp.dot(delta_squeeze, squeeze_weight, preferred_element_type=jnp.float32)
        projected_grad = normalize_back(hidden_upstream, hidden_normed, hidden_inverse).astype(jnp.bfloat16)
        normed_grad = lax.dot_general(projected_grad, projection_weight, (((1,), (1,)), ((), ())), preferred_element_type=jnp.float32)
        feature_grad = normalize_back(normed_grad, normed_in, inverse_in)
        return (scores, feature_grad, squeeze_grad, layer_grads[0], layer_grads[1], layer_grads[2], final_grad)
    results = lax.map(single, (features, score_cotangent))
    factor = 1.0 / math.sqrt(UTTS * FRAMES)
    return (results[0], results[1], lax.optimization_barrier(jnp.sum(results[2], axis=0)) * factor, lax.optimization_barrier(jnp.sum(results[3], axis=0)) * factor, lax.optimization_barrier(jnp.sum(results[4], axis=0)) * factor, lax.optimization_barrier(jnp.sum(results[5], axis=0)) * factor, lax.optimization_barrier(jnp.sum(results[6], axis=0)) * factor)
```

```python
import functools
import math

import jax
import jax.numpy as jnp
from jax import lax
from jax.experimental import pallas as pl
from jax.experimental.pallas import tpu as pltpu
from jax.sharding import PartitionSpec as P

C0 = 64
C1 = 128
C2 = 256
HK = 5
PK = 3
EDGE = 16
LANES = 128

EPSILON = 1e-05
SLOPE = 0.1
BF16 = jnp.bfloat16
F32 = jnp.float32
NT = (((1,), (1,)), ((), ()))
TN = (((0,), (0,)), ((), ()))


def normalize(values):
    average = jnp.mean(values, axis=-1, keepdims=True)
    centred = values - average
    variance = jnp.mean(centred * centred, axis=-1, keepdims=True)
    inverse = lax.rsqrt(variance + EPSILON)
    return (centred * inverse, inverse)


def normalize_back(upstream, normed, inverse):
    first_mean = jnp.mean(upstream, axis=-1, keepdims=True)
    second_mean = jnp.mean(upstream * normed, axis=-1, keepdims=True)
    return (upstream - first_mean - normed * second_mean) * inverse


def leaky_pair(values):
    cumulative = 0.5 * (1.0 + lax.erf(values * math.sqrt(0.5)))
    density = jnp.exp(-0.5 * values * values) * (1.0 / math.sqrt(2.0 * math.pi))
    unit = SLOPE * values + (1.0 - SLOPE) * (values * cumulative)
    slope = SLOPE + (1.0 - SLOPE) * (cumulative + values * density)
    return unit, slope


def dot(a, b, dims=(((1,), (0,)), ((), ()))):
    return lax.dot_general(a, b, dims, preferred_element_type=F32)


def forward_rows(rows, projection, squeeze):
    normed, _ = normalize(rows.astype(F32))
    projected = dot(normed.astype(BF16), projection).astype(BF16)
    hidden_normed, _ = normalize(projected.astype(F32))
    hidden = hidden_normed.astype(BF16)
    return projected, hidden, dot(hidden, squeeze, NT)


def edges_kernel(first_ref, last_ref, cot_ref, up_ref, down_ref):
    cot = cot_ref[...]
    high = cot.astype(BF16).astype(F32)
    middle = (cot - high).astype(BF16).astype(F32)
    low = cot - high - middle
    stack = jnp.concatenate([high, middle, low, jnp.zeros((EDGE - 3, cot.shape[1]), F32)], axis=0).astype(BF16)
    rest = jnp.zeros((EDGE, first_ref.shape[1] - cot.shape[1]), BF16)
    extra = jnp.concatenate([stack, rest], axis=1)
    up_ref[:EDGE, :] = last_ref[...]
    up_ref[EDGE:, :] = extra
    down_ref[:EDGE, :] = first_ref[...]
    down_ref[EDGE:, :] = extra


def project_kernel(rows_ref, projection_ref, squeeze_ref, projected_ref, hidden_ref, squeezed_ref):
    projected, hidden, squeezed = forward_rows(rows_ref[...], projection_ref[...], squeeze_ref[...])
    projected_ref[...] = projected
    hidden_ref[...] = hidden
    squeezed_ref[...] = squeezed


def shifted(values, taps, sign):
    count = values.shape[0]
    pieces = []
    for k in range(taps):
        amount = (-sign * (k - (taps - 1) // 2)) % count
        moved = values if amount == 0 else pltpu.roll(values, amount, 0)
        pieces.append(moved.astype(BF16))
    return pieces


def pieces_of(n, count, rows):
    found = []
    for s in range(n):
        at = s * count
        while at < (s + 1) * count:
            tap, row = divmod(at, rows)
            length = min(rows - row, (s + 1) * count - at)
            found.append((s, tap, row, at - s * count, length))
            at += length
    return found


def head_kernel(
    n,
    packed,
    place_ref,
    squeezed_ref,
    low_ref,
    high_ref,
    cot_ref,
    hidden_ref,
    projection_ref,
    squeeze_ref,
    first_ref,
    second_ref,
    third_ref,
    final_ref,
    scores_ref,
    delta_ref,
    *outs,
):
    frames = squeezed_ref.shape[0]
    total = frames + 2 * EDGE
    own = slice(EDGE, EDGE + frames)
    seq, core = place_ref[0], place_ref[1]
    row = lax.broadcasted_iota(jnp.int32, (total, LANES), 0)
    inside = ((row >= EDGE) | (seq > 0)) & ((row < EDGE + frames) | (seq < n - 1))

    def mask(values):
        width = values.shape[1]
        if width <= LANES:
            return jnp.where(inside[:, :width], values, 0.0)
        return jnp.concatenate(
            [jnp.where(inside, values[:, i : i + LANES], 0.0) for i in range(0, width, LANES)], axis=1
        )

    edge = jnp.concatenate([low_ref[:EDGE, :], high_ref[:EDGE, :]], axis=0)
    _, _, edge_squeezed = forward_rows(edge, projection_ref[...], squeeze_ref[...])
    squeezed = jnp.concatenate([edge_squeezed[:EDGE], squeezed_ref[...], edge_squeezed[EDGE:]], axis=0)

    def joined(ref):
        parts = ref[EDGE:, :LANES].astype(F32)
        return parts[0:1] + parts[1:2] + parts[2:3]

    rows = [cot_ref[...], joined(low_ref), joined(high_ref), jnp.zeros((5, LANES), F32)]
    columns = jnp.concatenate(rows, axis=0).T
    cot = jnp.concatenate(
        [
            jnp.broadcast_to(columns[frames - EDGE :, 1:2], (EDGE, LANES)),
            jnp.broadcast_to(columns[:, 0:1], (frames, LANES)),
            jnp.broadcast_to(columns[:EDGE, 2:3], (EDGE, LANES)),
        ],
        axis=0,
    )

    weights = (first_ref, second_ref, third_ref)
    act = squeezed
    inputs, slopes = [], []
    for ref in weights:
        unit, slope = leaky_pair(act)
        unit = mask(unit)
        slopes.append(slope)
        inputs.append(unit[own].astype(BF16))
        width = unit.shape[1]
        act = jnp.zeros((total, ref.shape[1]), F32)
        for k, piece in enumerate(shifted(unit, HK, 1)):
            act = act + dot(piece, ref[k * width : (k + 1) * width, :])
    unit, slope = leaky_pair(act)
    final_in = mask(unit).astype(BF16).astype(F32)
    taps = shifted(final_in, PK, 1)
    scores = jnp.zeros((1, frames), F32)
    for k in range(PK):
        scores = scores + dot(final_ref[:, k * C2 : (k + 1) * C2], taps[k][own], NT)
    scores_ref[...] = scores

    upstream = [jnp.zeros((total, LANES), F32)] * (C2 // LANES)
    final_grad = []
    for k in range(PK):
        amount = (k - 1) % total
        moved = cot if amount == 0 else pltpu.roll(cot, amount, 0)
        for h in range(C2 // LANES):
            lanes = slice(k * C2 + h * LANES, k * C2 + (h + 1) * LANES)
            upstream[h] = upstream[h] + moved * final_ref[:, lanes].astype(F32)
            final_grad.append(
                jnp.sum(moved[own] * final_in[own, h * LANES : (h + 1) * LANES], axis=0, keepdims=True)
            )
    upstream = jnp.concatenate(upstream, axis=1)
    slopes.append(slope)
    grads = []
    for layer in (2, 1, 0):
        delta = mask(upstream * slopes[layer + 1])
        pieces = shifted(delta, HK, -1)
        near = jnp.concatenate([p[own] for p in pieces], axis=1)
        grads.append(dot(inputs[layer], near, TN))
        ref = weights[layer]
        width = ref.shape[0] // HK
        upstream = jnp.zeros((total, width), F32)
        for k, piece in enumerate(pieces):
            upstream = upstream + dot(piece, ref[k * width : (k + 1) * width, :], NT)
    third, second, first = grads
    delta = (upstream[own] * slopes[0][own]).astype(BF16)
    delta_ref[...] = delta
    squeeze_grad = dot(delta, hidden_ref[...], TN)

    if not packed:
        squeeze_out, first_out, second_out, third_out, final_out = outs
        squeeze_out[...] = squeeze_grad
        for out, grad in ((first_out, first), (second_out, second), (third_out, third)):
            width, cols = grad.shape[0], out.shape[1]
            for k in range(HK):
                out[k * width : (k + 1) * width, :] = grad[:, k * cols : (k + 1) * cols]
        for i, part in enumerate(final_grad):
            final_out[:, i * LANES : (i + 1) * LANES] = part
        return

    (payload_ref, scratch) = outs
    half = payload_ref.shape[3]
    mine = [(seq ^ s) for s in range(n)]

    def put(s, at, rows):
        slot = mine[s]
        while rows.shape[0]:
            side, start = divmod(at, half)
            length = min(rows.shape[0], half - start)
            payload_ref[side ^ core, slot & 3, slot >> 2, start : start + length, :] = rows[:length]
            rows = rows[length:]
            at += length

    base = 0
    for grad, channels, cols in ((third, C2, C2), (second, C1, C2)):
        count = HK * channels // n
        for s, tap, start, offset, length in pieces_of(n, count, channels):
            for h in range(cols // LANES):
                lanes = slice(tap * cols + h * LANES, tap * cols + (h + 1) * LANES)
                scratch[s, base + h * count + offset : base + h * count + offset + length, :] = grad[
                    start : start + length, lanes
                ]
        base += count * (cols // LANES)
    count = C0 // n
    for s in range(n):
        for h in range(squeeze_grad.shape[1] // LANES):
            scratch[s, base + h * count : base + (h + 1) * count, :] = squeeze_grad[
                s * count : (s + 1) * count, h * LANES : (h + 1) * LANES
            ]
    base += count * (squeeze_grad.shape[1] // LANES)
    count = HK * C0 // n
    for s, tap, start, offset, length in pieces_of(n, count, C0):
        scratch[s, base + offset : base + offset + length, :] = first[
            start : start + length, tap * C1 : (tap + 1) * C1
        ]
    base += count
    final_row = jnp.concatenate(final_grad, axis=1)
    count = final_row.shape[1] // n
    for s in range(n):
        first_half = s * count // LANES * LANES
        piece = final_row[:, first_half : first_half + 2 * LANES]
        if piece.shape[1] < 2 * LANES:
            piece = jnp.concatenate([piece, piece[:, :LANES]], axis=1)
        amount = (first_half - s * count) % (2 * LANES)
        piece = piece if amount == 0 else pltpu.roll(jnp.broadcast_to(piece, (8, 2 * LANES)), amount, 1)
        scratch[s, base : base + 1, :] = piece[0:1, :LANES]
        scratch[s, base + 1 :, :] = jnp.zeros((scratch.shape[1] - base - 1, LANES), F32)
    for s in range(n):
        put(s, 0, scratch[s].astype(BF16))


def feature_kernel(rows_ref, projected_ref, delta_ref, squeeze_ref, projection_ref, out_ref):
    hidden_upstream = dot(delta_ref[...], squeeze_ref[...])
    hidden_normed, hidden_inverse = normalize(projected_ref[...].astype(F32))
    projected_grad = normalize_back(hidden_upstream, hidden_normed, hidden_inverse).astype(BF16)
    normed_grad = dot(projected_grad, projection_ref[...], NT)
    normed, inverse = normalize(rows_ref[...].astype(F32))
    out_ref[...] = normalize_back(normed_grad, normed, inverse)


def unpack_kernel(factor, mine_ref, other_ref, place_ref, squeeze_ref, first_ref, second_ref, third_ref, final_ref, both):
    half = mine_ref.shape[0]
    core = place_ref[1]
    both[pl.ds(pl.multiple_of(core * half, 16), half), :] = mine_ref[...].astype(F32) * factor
    both[pl.ds(pl.multiple_of((1 - core) * half, 16), half), :] = other_ref[...].astype(F32) * factor
    base = 0
    for ref in (third_ref, second_ref, squeeze_ref, first_ref):
        count = ref.shape[0]
        for h in range(ref.shape[1] // LANES):
            ref[:, h * LANES : (h + 1) * LANES] = both[base : base + count, :]
            base += count
    final_ref[...] = both[base : base + 1, :]


def sds(shape, dtype):
    return jax.ShapeDtypeStruct(shape, dtype)


VMEM = pl.BlockSpec(memory_space=pltpu.VMEM)
SMEM = pl.BlockSpec(memory_space=pltpu.SMEM)


def params(mib):
    return pltpu.CompilerParams(vmem_limit_bytes=mib * 1024 * 1024)


def cost(flops, nbytes):
    return pl.CostEstimate(flops=flops, bytes_accessed=nbytes, transcendentals=0)


def shards(
    features,
    score_cotangent,
    projection_weight,
    squeeze_weight,
    first_weight,
    second_weight,
    third_weight,
    final_weight,
):
    n, cores = lax.axis_size("seq"), lax.axis_size("dp")
    frames, feat = features.shape[1:]
    width = projection_weight.shape[1]
    seq, core = lax.axis_index("seq"), lax.axis_index("dp")
    packed = n == 16 and cores == 2
    rows = features.reshape(frames, feat)
    place = jnp.stack([seq, core]).astype(jnp.int32)

    up, down = pl.pallas_call(
        edges_kernel,
        grid=(1,),
        in_specs=[
            pl.BlockSpec((EDGE, feat), lambda i: (0, 0)),
            pl.BlockSpec((EDGE, feat), lambda i: (frames // EDGE - 1, 0)),
            pl.BlockSpec((1, frames), lambda i: (0, 0)),
        ],
        out_specs=[pl.BlockSpec((2 * EDGE, feat), lambda i: (0, 0))] * 2,
        out_shape=[sds((2 * EDGE, feat), BF16)] * 2,
        name="edges",
    )(rows, rows, score_cotangent)
    low = lax.ppermute(up, "seq", [(i, i + 1) for i in range(n - 1)])
    high = lax.ppermute(down, "seq", [(i + 1, i) for i in range(n - 1)])

    projected, hidden, squeezed = pl.pallas_call(
        project_kernel,
        in_specs=[VMEM] * 3,
        out_specs=[VMEM] * 3,
        out_shape=[sds((frames, width), BF16), sds((frames, width), BF16), sds((frames, C0), F32)],
        compiler_params=params(16),
        cost_estimate=cost(2 * frames * width * (feat + C0), 2 * feat * width),
        name="project",
    )(rows, projection_weight, squeeze_weight)

    if packed:
        half = 144
        grad_shapes = [sds((2, 4, 4, half, LANES), BF16)]
        scratch = [pltpu.VMEM((n, 2 * half, LANES), F32)]
    else:
        grad_shapes = [
            sds((C0, width), F32),
            sds(first_weight.shape, F32),
            sds(second_weight.shape, F32),
            sds(third_weight.shape, F32),
            sds((1, PK * C2), F32),
        ]
        scratch = []
    scores, delta, *grads = pl.pallas_call(
        functools.partial(head_kernel, n, packed),
        in_specs=[SMEM] + [VMEM] * 11,
        out_specs=[VMEM] * (2 + len(grad_shapes)),
        out_shape=[sds((1, frames), F32), sds((frames, C0), BF16), *grad_shapes],
        scratch_shapes=scratch,
        compiler_params=params(32),
        cost_estimate=cost(10**9, 4 * 10**6),
        name="head",
    )(
        place,
        squeezed,
        low,
        high,
        score_cotangent,
        hidden,
        projection_weight,
        squeeze_weight,
        first_weight,
        second_weight,
        third_weight,
        final_weight.reshape(1, PK * C2),
    )

    feature_grad = pl.pallas_call(
        feature_kernel,
        in_specs=[VMEM] * 5,
        out_specs=VMEM,
        out_shape=sds((frames, feat), F32),
        compiler_params=params(16),
        cost_estimate=cost(2 * frames * width * (feat + C0), 2 * feat * width),
        name="feature",
    )(rows, projected, delta, squeeze_weight, projection_weight)

    factor = 1.0 / math.sqrt(cores * n * frames)
    if not packed:
        shares = []
        for term in grads[:4] + [grads[4].reshape(PK * C2)]:
            part = lax.psum_scatter(term * factor, "seq", scatter_dimension=0, tiled=True)
            shares.append(lax.psum(part.astype(BF16), "dp").astype(F32))
        return (scores, feature_grad[None], *shares)

    def added(*terms):
        total = terms[0].astype(F32)
        for term in terms[1:]:
            total = total + term.astype(F32)
        return total.astype(BF16)

    swap = [(0, 1), (1, 0)]
    (payload,) = grads
    held = added(payload[0], lax.ppermute(payload[1], "dp", swap))
    for stride in (1, 4):
        moved = [
            lax.ppermute(held[j], "seq", [(i, i ^ (j * stride)) for i in range(n)]) for j in (3, 1, 2)
        ]
        held = added(held[0], *moved)
    other = lax.ppermute(held, "dp", swap)
    shapes = [
        (C0 // n, width),
        (HK * C0 // n, C1),
        (HK * C1 // n, C2),
        (HK * C2 // n, C2),
        (1, LANES),
    ]
    *shares, final = pl.pallas_call(
        functools.partial(unpack_kernel, factor),
        in_specs=[VMEM, VMEM, SMEM],
        out_specs=[VMEM] * 5,
        out_shape=[sds(shape, F32) for shape in shapes],
        scratch_shapes=[pltpu.VMEM((2 * half, LANES), F32)],
        name="unpack",
    )(held, other, place)
    return (scores, feature_grad[None], *shares, final[0, : PK * C2 // n])


def solution(mesh):
    placed = (P("dp", "seq", None), P("dp", "seq"), P(), P(), P(), P(), P(), P())
    return jax.shard_map(
        shards,
        mesh=mesh,
        in_specs=placed,
        out_specs=(
            P("dp", "seq"),
            P("dp", "seq", None),
            P("seq", None),
            P("seq", None),
            P("seq", None),
            P("seq", None),
            P("seq"),
        ),
        check_vma=False,
    )
```

```python
import functools
import math

import jax
import jax.numpy as jnp
from jax import lax
from jax.experimental import pallas as pl
from jax.experimental.pallas import tpu as pltpu
from jax.sharding import PartitionSpec as P

C0 = 64
C1 = 128
C2 = 256
HK = 5
PK = 3
EDGE = 32
REACH = 12
MORE = 16
BACK = 16
LANES = 128

EPSILON = 1e-05
SLOPE = 0.1
BF16 = jnp.bfloat16
F32 = jnp.float32
NT = (((1,), (1,)), ((), ()))
TN = (((0,), (0,)), ((), ()))


def normalize(values):
    average = jnp.mean(values, axis=-1, keepdims=True)
    centred = values - average
    variance = jnp.mean(centred * centred, axis=-1, keepdims=True)
    inverse = lax.rsqrt(variance + EPSILON)
    return (centred * inverse, inverse)


def normalize_back(upstream, normed, inverse):
    first_mean = jnp.mean(upstream, axis=-1, keepdims=True)
    second_mean = jnp.mean(upstream * normed, axis=-1, keepdims=True)
    return (upstream - first_mean - normed * second_mean) * inverse


def leaky_pair(values):
    cumulative = 0.5 * (1.0 + lax.erf(values * math.sqrt(0.5)))
    density = jnp.exp(-0.5 * values * values) * (1.0 / math.sqrt(2.0 * math.pi))
    unit = SLOPE * values + (1.0 - SLOPE) * (values * cumulative)
    slope = SLOPE + (1.0 - SLOPE) * (cumulative + values * density)
    return unit, slope


def dot(a, b, dims=(((1,), (0,)), ((), ()))):
    return lax.dot_general(a, b, dims, preferred_element_type=F32)


def forward_rows(rows, projection, squeeze):
    normed, _ = normalize(rows.astype(F32))
    projected = dot(normed.astype(BF16), projection).astype(BF16)
    hidden_normed, _ = normalize(projected.astype(F32))
    hidden = hidden_normed.astype(BF16)
    return projected, hidden, dot(hidden, squeeze, NT)


def edge_kernel(rows_ref, cot_ref, out_ref, cot_held, sems):
    frames = rows_ref.shape[0]
    copies = [
        pltpu.make_async_copy(cot_ref, cot_held, sems.at[0]),
        pltpu.make_async_copy(rows_ref.at[frames - EDGE :], out_ref.at[:EDGE], sems.at[1]),
    ]
    for copy in copies:
        copy.start()
    copies[0].wait()
    cot = cot_held[...]
    high = cot.astype(BF16).astype(F32)
    middle = (cot - high).astype(BF16).astype(F32)
    low = cot - high - middle
    stack = jnp.concatenate([high, middle, low, jnp.zeros((MORE - 3, frames), F32)], axis=0)
    out_ref[EDGE:, :frames] = stack.astype(BF16)
    out_ref[EDGE:, frames:] = jnp.zeros((MORE, out_ref.shape[1] - frames), BF16)
    copies[1].wait()


def project_kernel(count, *refs):
    sources, held = refs[:count], refs[count : 2 * count]
    projected_ref, hidden_ref, squeezed_ref, sems = refs[2 * count :]
    copies = [pltpu.make_async_copy(a, b, sems.at[i]) for i, (a, b) in enumerate(zip(sources, held))]
    for copy in copies:
        copy.start()
    for copy in copies[:3]:
        copy.wait()
    projected, hidden, squeezed = forward_rows(held[0][...], held[1][...], held[2][...])
    projected_ref[...] = projected
    hidden_ref[...] = hidden
    squeezed_ref[...] = squeezed
    for copy in copies[3:]:
        copy.wait()


def shifted(values, taps, sign):
    count = values.shape[0]
    pieces = []
    for k in range(taps):
        amount = (-sign * (k - (taps - 1) // 2)) % count
        moved = values if amount == 0 else pltpu.roll(values, amount, 0)
        pieces.append(moved.astype(BF16))
    return pieces


def pieces_of(n, count, rows):
    found = []
    for s in range(n):
        at = s * count
        while at < (s + 1) * count:
            tap, row = divmod(at, rows)
            length = min(rows - row, (s + 1) * count - at)
            found.append((s, tap, row, at - s * count, length))
            at += length
    return found


def head_kernel(
    n,
    packed,
    place_ref,
    squeezed_ref,
    edge_ref,
    cot_ref,
    hidden_ref,
    projection_ref,
    squeeze_ref,
    first_ref,
    second_ref,
    third_ref,
    final_ref,
    scores_ref,
    before_ref,
    delta_ref,
    edge_projected_ref,
    *outs,
):
    frames = squeezed_ref.shape[0]
    total = EDGE + frames
    seq, core = place_ref[0], place_ref[1]
    row = lax.broadcasted_iota(jnp.int32, (total, LANES), 0)
    inside = (row >= EDGE - 2 * REACH) & ((row >= EDGE) | (seq > 0))
    window = inside & (row >= EDGE - REACH) & ((row < total - REACH) | (seq == n - 1))

    def mask(values, where):
        width = values.shape[1]
        if width <= LANES:
            return jnp.where(where[:, :width], values, 0.0)
        return jnp.concatenate(
            [jnp.where(where, values[:, i : i + LANES], 0.0) for i in range(0, width, LANES)], axis=1
        )

    edge_projected, edge_hidden, edge_squeezed = forward_rows(
        edge_ref[:EDGE, :], projection_ref[...], squeeze_ref[...]
    )
    edge_projected_ref[...] = edge_projected[EDGE - BACK :]
    squeezed = jnp.concatenate([edge_squeezed, squeezed_ref[...]], axis=0)

    parts = edge_ref[EDGE:, :LANES].astype(F32)
    parts = parts[0:1] + parts[1:2] + parts[2:3]
    columns = jnp.concatenate([cot_ref[...], parts, jnp.zeros((6, LANES), F32)], axis=0).T
    cot = jnp.concatenate(
        [
            jnp.broadcast_to(columns[frames - EDGE :, 1:2], (EDGE, LANES)),
            jnp.broadcast_to(columns[:, 0:1], (frames, LANES)),
        ],
        axis=0,
    )
    cot = mask(cot, inside)

    weights = (first_ref, second_ref, third_ref)
    act = squeezed
    inputs, slopes = [], []
    for ref in weights:
        unit, slope = leaky_pair(act)
        unit = mask(unit, inside)
        slopes.append(slope)
        inputs.append(mask(unit, window).astype(BF16))
        width = unit.shape[1]
        act = jnp.zeros((total, ref.shape[1]), F32)
        for k, piece in enumerate(shifted(unit, HK, 1)):
            act = act + dot(piece, ref[k * width : (k + 1) * width, :])
    unit, slope = leaky_pair(act)
    final_in = mask(unit, inside).astype(BF16).astype(F32)
    taps = shifted(final_in, PK, 1)
    for ref, rows in ((scores_ref, slice(EDGE, total)), (before_ref, slice(0, LANES))):
        scores = jnp.zeros((1, rows.stop - rows.start), F32)
        for k in range(PK):
            scores = scores + dot(final_ref[:, k * C2 : (k + 1) * C2], taps[k][rows], NT)
        ref[...] = scores

    upstream = [jnp.zeros((total, LANES), F32)] * (C2 // LANES)
    final_grad = []
    final_in = mask(final_in, window)
    for k in range(PK):
        amount = (k - 1) % total
        moved = cot if amount == 0 else pltpu.roll(cot, amount, 0)
        for h in range(C2 // LANES):
            lanes = slice(k * C2 + h * LANES, k * C2 + (h + 1) * LANES)
            upstream[h] = upstream[h] + moved * final_ref[:, lanes].astype(F32)
            final_grad.append(
                jnp.sum(moved * final_in[:, h * LANES : (h + 1) * LANES], axis=0, keepdims=True)
            )
    upstream = jnp.concatenate(upstream, axis=1)
    slopes.append(slope)
    grads = []
    for layer in (2, 1, 0):
        delta = mask(upstream * slopes[layer + 1], inside)
        pieces = shifted(delta, HK, -1)
        grads.append(dot(inputs[layer], jnp.concatenate(pieces, axis=1), TN))
        ref = weights[layer]
        width = ref.shape[0] // HK
        upstream = jnp.zeros((total, width), F32)
        for k, piece in enumerate(pieces):
            upstream = upstream + dot(piece, ref[k * width : (k + 1) * width, :], NT)
    third, second, first = grads
    delta = mask(upstream * slopes[0], inside)
    delta_ref[...] = delta[EDGE - BACK :].astype(BF16)
    hidden = jnp.concatenate([edge_hidden, hidden_ref[...]], axis=0)
    squeeze_grad = dot(mask(delta, window).astype(BF16), hidden, TN)

    if not packed:
        squeeze_out, first_out, second_out, third_out, final_out = outs
        squeeze_out[...] = squeeze_grad
        for out, grad in ((first_out, first), (second_out, second), (third_out, third)):
            width, cols = grad.shape[0], out.shape[1]
            for k in range(HK):
                out[k * width : (k + 1) * width, :] = grad[:, k * cols : (k + 1) * cols]
        for i, part in enumerate(final_grad):
            final_out[:, i * LANES : (i + 1) * LANES] = part
        return

    (payload_ref, scratch) = outs
    half = payload_ref.shape[3]
    mine = [(seq ^ s) for s in range(n)]

    def put(s, at, rows):
        slot = mine[s]
        while rows.shape[0]:
            side, start = divmod(at, half)
            length = min(rows.shape[0], half - start)
            payload_ref[side ^ core, slot & 3, slot >> 2, start : start + length, :] = rows[:length]
            rows = rows[length:]
            at += length

    base = 0
    for grad, channels, cols in ((third, C2, C2), (second, C1, C2)):
        count = HK * channels // n
        for s, tap, start, offset, length in pieces_of(n, count, channels):
            for h in range(cols // LANES):
                lanes = slice(tap * cols + h * LANES, tap * cols + (h + 1) * LANES)
                scratch[s, base + h * count + offset : base + h * count + offset + length, :] = grad[
                    start : start + length, lanes
                ]
        base += count * (cols // LANES)
    count = C0 // n
    for s in range(n):
        for h in range(squeeze_grad.shape[1] // LANES):
            scratch[s, base + h * count : base + (h + 1) * count, :] = squeeze_grad[
                s * count : (s + 1) * count, h * LANES : (h + 1) * LANES
            ]
    base += count * (squeeze_grad.shape[1] // LANES)
    count = HK * C0 // n
    for s, tap, start, offset, length in pieces_of(n, count, C0):
        scratch[s, base + offset : base + offset + length, :] = first[
            start : start + length, tap * C1 : (tap + 1) * C1
        ]
    base += count
    final_row = jnp.concatenate(final_grad, axis=1)
    count = final_row.shape[1] // n
    for s in range(n):
        first_half = s * count // LANES * LANES
        piece = final_row[:, first_half : first_half + 2 * LANES]
        if piece.shape[1] < 2 * LANES:
            piece = jnp.concatenate([piece, piece[:, :LANES]], axis=1)
        amount = (first_half - s * count) % (2 * LANES)
        piece = piece if amount == 0 else pltpu.roll(jnp.broadcast_to(piece, (8, 2 * LANES)), amount, 1)
        scratch[s, base : base + 1, :] = piece[0:1, :LANES]
        scratch[s, base + 1 :, :] = jnp.zeros((scratch.shape[1] - base - 1, LANES), F32)
    for s in range(n):
        put(s, 0, scratch[s].astype(BF16))


def feature_kernel(
    rows_ref, edge_ref, projected_ref, edge_projected_ref, delta_ref, before_ref, squeeze_ref, projection_ref, out_ref, back_ref
):
    hidden_upstream = dot(delta_ref[...], squeeze_ref[...])
    projected = jnp.concatenate([edge_projected_ref[...], projected_ref[...]], axis=0)
    hidden_normed, hidden_inverse = normalize(projected.astype(F32))
    projected_grad = normalize_back(hidden_upstream, hidden_normed, hidden_inverse).astype(BF16)
    normed_grad = dot(projected_grad, projection_ref[...], NT)
    rows = jnp.concatenate([edge_ref[EDGE - BACK : EDGE, :], rows_ref[...]], axis=0)
    normed, inverse = normalize(rows.astype(F32))
    grad = normalize_back(normed_grad, normed, inverse)
    out_ref[...] = grad[BACK:]
    back_ref[:BACK, :] = grad[:BACK]
    back_ref[BACK:, :LANES] = jnp.broadcast_to(before_ref[...], (8, LANES))
    back_ref[BACK:, LANES:] = jnp.zeros((8, back_ref.shape[1] - LANES), F32)


def assemble_kernel(n, place_ref, own_ref, scores_ref, back_ref, grad_ref, final_scores_ref):
    frames = own_ref.shape[0]
    last = place_ref[0] == n - 1
    grad_ref[: frames - BACK, :] = own_ref[: frames - BACK, :]
    row = lax.broadcasted_iota(jnp.int32, (BACK, own_ref.shape[1]), 0)
    keep = last | (row < BACK - REACH)
    grad_ref[frames - BACK :, :] = jnp.where(keep, own_ref[frames - BACK :, :], back_ref[:BACK, :])
    moved = pltpu.roll(back_ref[BACK:, :LANES], frames - EDGE, 1)
    lane = lax.broadcasted_iota(jnp.int32, (1, frames), 1)
    final_scores_ref[...] = jnp.where(last | (lane < frames - REACH), scores_ref[...], moved[0:1])


def unpack_kernel(factor, mine_ref, other_ref, place_ref, squeeze_ref, first_ref, second_ref, third_ref, final_ref, both):
    half = mine_ref.shape[0]
    core = place_ref[1]
    both[pl.ds(pl.multiple_of(core * half, 16), half), :] = mine_ref[...].astype(F32) * factor
    both[pl.ds(pl.multiple_of((1 - core) * half, 16), half), :] = other_ref[...].astype(F32) * factor
    base = 0
    for ref in (third_ref, second_ref, squeeze_ref, first_ref):
        count = ref.shape[0]
        for h in range(ref.shape[1] // LANES):
            ref[:, h * LANES : (h + 1) * LANES] = both[base : base + count, :]
            base += count
    final_ref[...] = both[base : base + 1, : final_ref.shape[1]]


def sds(shape, dtype):
    return jax.ShapeDtypeStruct(shape, dtype)


def hbm(array):
    return pltpu.with_memory_space_constraint(array, pltpu.HBM)


def vmem(shape, dtype):
    return pltpu.VMEM(shape, dtype)


VMEM = pl.BlockSpec(memory_space=pltpu.VMEM)
HBM = pl.BlockSpec(memory_space=pltpu.HBM)
SMEM = pl.BlockSpec(memory_space=pltpu.SMEM)


def params(mib):
    return pltpu.CompilerParams(vmem_limit_bytes=mib * 1024 * 1024)


def cost(flops, nbytes):
    return pl.CostEstimate(flops=flops, bytes_accessed=nbytes, transcendentals=0)


def shards(
    features,
    score_cotangent,
    projection_weight,
    squeeze_weight,
    first_weight,
    second_weight,
    third_weight,
    final_weight,
):
    n, cores = lax.axis_size("seq"), lax.axis_size("dp")
    frames, feat = features.shape[1:]
    width = projection_weight.shape[1]
    seq, core = lax.axis_index("seq"), lax.axis_index("dp")
    packed = n == 16 and cores == 2
    rows = features.reshape(frames, feat)
    place = jnp.stack([seq, core]).astype(jnp.int32)

    edge = pl.pallas_call(
        edge_kernel,
        in_specs=[HBM, HBM],
        out_specs=VMEM,
        out_shape=vmem((EDGE + MORE, feat), BF16),
        scratch_shapes=[pltpu.VMEM((1, frames), F32), pltpu.SemaphoreType.DMA((2,))],
        name="edge",
    )(hbm(rows), hbm(score_cotangent))
    edge = lax.ppermute(edge, "seq", [(i, i + 1) for i in range(n - 1)])

    sources = (
        rows,
        projection_weight,
        squeeze_weight,
        score_cotangent,
        first_weight,
        second_weight,
        third_weight,
    )
    rows, projection, squeeze, cot, first, second, third, projected, hidden, squeezed = pl.pallas_call(
        functools.partial(project_kernel, len(sources)),
        in_specs=[HBM] * len(sources),
        out_specs=[VMEM] * (len(sources) + 3),
        out_shape=[
            *[vmem(a.shape, a.dtype) for a in sources],
            vmem((frames, width), BF16),
            vmem((frames, width), BF16),
            vmem((frames, C0), F32),
        ],
        scratch_shapes=[pltpu.SemaphoreType.DMA((len(sources),))],
        compiler_params=params(8),
        cost_estimate=cost(2 * frames * width * (feat + C0), 2 * feat * width),
        name="project",
    )(*[hbm(a) for a in sources])

    if packed:
        half = 144
        grad_shapes = [sds((2, 4, 4, half, LANES), BF16)]
        scratch = [pltpu.VMEM((n, 2 * half, LANES), F32)]
    else:
        grad_shapes = [
            sds((C0, width), F32),
            sds(first_weight.shape, F32),
            sds(second_weight.shape, F32),
            sds(third_weight.shape, F32),
            sds((1, PK * C2), F32),
        ]
        scratch = []
    own_scores, before, delta, edge_projected, *grads = pl.pallas_call(
        functools.partial(head_kernel, n, packed),
        in_specs=[SMEM] + [VMEM] * 10,
        out_specs=[VMEM] * (4 + len(grad_shapes)),
        out_shape=[
            sds((1, frames), F32),
            sds((1, LANES), F32),
            sds((BACK + frames, C0), BF16),
            sds((BACK, width), BF16),
            *grad_shapes,
        ],
        scratch_shapes=scratch,
        compiler_params=params(20),
        cost_estimate=cost(10**9, 4 * 10**6),
        name="head",
    )(
        place,
        squeezed,
        edge,
        cot,
        hidden,
        projection,
        squeeze,
        first,
        second,
        third,
        final_weight.reshape(1, PK * C2),
    )

    def features_back():
        own_grad, back = pl.pallas_call(
            feature_kernel,
            in_specs=[VMEM] * 8,
            out_specs=[VMEM] * 2,
            out_shape=[sds((frames, feat), F32), sds((BACK + 8, feat), F32)],
            compiler_params=params(8),
            cost_estimate=cost(2 * frames * width * (feat + C0), 2 * feat * width),
            name="feature",
        )(rows, edge, projected, edge_projected, delta, before, squeeze, projection)
        back = lax.ppermute(back, "seq", [(i + 1, i) for i in range(n - 1)])
        feature_grad, scores = pl.pallas_call(
            functools.partial(assemble_kernel, n),
            in_specs=[SMEM] + [VMEM] * 3,
            out_specs=[VMEM] * 2,
            out_shape=[sds((frames, feat), F32), sds((1, frames), F32)],
            compiler_params=params(4),
            cost_estimate=cost(frames * feat, 8 * frames * feat),
            name="assemble",
        )(place, own_grad, own_scores, back)
        return feature_grad[None], scores

    factor = 1.0 / math.sqrt(cores * n * frames)
    if not packed:
        shares = []
        for term in grads[:4] + [grads[4].reshape(PK * C2)]:
            part = lax.psum_scatter(term * factor, "seq", scatter_dimension=0, tiled=True)
            shares.append(lax.psum(part.astype(BF16), "dp").astype(F32))
        feature_grad, scores = features_back()
        return (scores, feature_grad, *shares)

    def added(*terms):
        total = terms[0].astype(F32)
        for term in terms[1:]:
            total = total + term.astype(F32)
        return total.astype(BF16)

    swap = [(0, 1), (1, 0)]
    (payload,) = grads
    held = added(payload[0], lax.ppermute(payload[1], "dp", swap))
    for stride in (1, 4):
        moved = [
            lax.ppermute(held[j], "seq", [(i, i ^ (j * stride)) for i in range(n)]) for j in (3, 1, 2)
        ]
        held = added(held[0], *moved)
        if stride == 1:
            feature_grad, scores = features_back()
            held, feature_grad, scores = lax.optimization_barrier((held, feature_grad, scores))
    other = lax.ppermute(held, "dp", swap)
    shapes = [
        (C0 // n, width),
        (HK * C0 // n, C1),
        (HK * C1 // n, C2),
        (HK * C2 // n, C2),
        (1, PK * C2 // n),
    ]
    *shares, final = pl.pallas_call(
        functools.partial(unpack_kernel, factor),
        in_specs=[VMEM, VMEM, SMEM],
        out_specs=[VMEM] * 5,
        out_shape=[sds(shape, F32) for shape in shapes],
        scratch_shapes=[pltpu.VMEM((2 * half, LANES), F32)],
        compiler_params=params(4),
        name="unpack",
    )(held, other, place)
    return (scores, feature_grad, *shares, final.reshape(PK * C2 // n))


def solution(mesh):
    placed = (P("dp", "seq", None), P("dp", "seq"), P(), P(), P(), P(), P(), P())
    return jax.shard_map(
        shards,
        mesh=mesh,
        in_specs=placed,
        out_specs=(
            P("dp", "seq"),
            P("dp", "seq", None),
            P("seq", None),
            P("seq", None),
            P("seq", None),
            P("seq", None),
            P("seq"),
        ),
        check_vma=False,
    )
```

```python
import functools
import math

import jax
import jax.numpy as jnp
from jax import lax
from jax.experimental import pallas as pl
from jax.experimental.pallas import tpu as pltpu
from jax.sharding import PartitionSpec as P

C0 = 64
C1 = 128
C2 = 256
HK = 5
PK = 3
EDGE = 32
REACH = 12
MORE = 8
BACK = 16
LANES = 128

EPSILON = 1e-05
SLOPE = 0.1
BF16 = jnp.bfloat16
F32 = jnp.float32
NT = (((1,), (1,)), ((), ()))
TN = (((0,), (0,)), ((), ()))


def normalize(values):
    average = jnp.mean(values, axis=-1, keepdims=True)
    centred = values - average
    variance = jnp.mean(centred * centred, axis=-1, keepdims=True)
    inverse = lax.rsqrt(variance + EPSILON)
    return (centred * inverse, inverse)


def normalize_back(upstream, normed, inverse):
    first_mean = jnp.mean(upstream, axis=-1, keepdims=True)
    second_mean = jnp.mean(upstream * normed, axis=-1, keepdims=True)
    return (upstream - first_mean - normed * second_mean) * inverse


def leaky_pair(values):
    cumulative = 0.5 * (1.0 + lax.erf(values * math.sqrt(0.5)))
    density = jnp.exp(-0.5 * values * values) * (1.0 / math.sqrt(2.0 * math.pi))
    unit = SLOPE * values + (1.0 - SLOPE) * (values * cumulative)
    slope = SLOPE + (1.0 - SLOPE) * (cumulative + values * density)
    return unit, slope


def dot(a, b, dims=(((1,), (0,)), ((), ()))):
    return lax.dot_general(a, b, dims, preferred_element_type=F32)


def forward_rows(rows, projection, squeeze):
    normed, _ = normalize(rows.astype(F32))
    projected = dot(normed.astype(BF16), projection).astype(BF16)
    hidden_normed, _ = normalize(projected.astype(F32))
    hidden = hidden_normed.astype(BF16)
    return projected, hidden, dot(hidden, squeeze, NT)


def here():
    return lax.axis_index("seq"), lax.rem(lax.axis_index("dp"), 2)


def edge_kernel(rows_ref, cot_ref, out_ref, held, cot_held, sems):
    frames, feat = rows_ref.shape
    _, odd = here()
    start = pl.multiple_of(odd * (frames - EDGE), 16)
    copies = [
        pltpu.make_async_copy(cot_ref, cot_held, sems.at[0]),
        pltpu.make_async_copy(rows_ref.at[pl.ds(start, EDGE)], held, sems.at[1]),
    ]
    for copy in copies:
        copy.start()
    copies[0].wait()
    cot = cot_held[...]
    high = cot.astype(BF16).astype(F32)
    middle = (cot - high).astype(BF16).astype(F32)
    low = cot - high - middle
    stack = jnp.concatenate([high, middle, low, jnp.zeros((MORE - 3, frames), F32)], axis=0)
    stack = jnp.concatenate([stack] * (EDGE // MORE), axis=0)
    row = lax.broadcasted_iota(jnp.int32, (EDGE, frames), 0)
    carries = (row < MORE) & (odd == 1) | (row >= EDGE - MORE) & (odd == 0)
    copies[1].wait()
    out_ref[:, frames:] = held[:, frames:]
    out_ref[:, :frames] = jnp.where(carries, stack, held[:, :frames].astype(F32)).astype(BF16)


def project_kernel(count, *refs):
    sources, held = refs[:count], refs[count : 2 * count]
    projected_ref, hidden_ref, squeezed_ref, sems = refs[2 * count :]
    copies = [pltpu.make_async_copy(a, b, sems.at[i]) for i, (a, b) in enumerate(zip(sources, held))]
    for copy in copies:
        copy.start()
    for copy in copies[:3]:
        copy.wait()
    projected, hidden, squeezed = forward_rows(held[0][...], held[1][...], held[2][...])
    projected_ref[...] = projected
    hidden_ref[...] = hidden
    squeezed_ref[...] = squeezed
    for copy in copies[3:]:
        copy.wait()


def shifted(values, taps, sign):
    count = values.shape[0]
    pieces = []
    for k in range(taps):
        amount = (-sign * (k - (taps - 1) // 2)) % count
        moved = values if amount == 0 else pltpu.roll(values, amount, 0)
        pieces.append(moved.astype(BF16))
    return pieces


def pieces_of(n, count, rows):
    found = []
    for s in range(n):
        at = s * count
        while at < (s + 1) * count:
            tap, row = divmod(at, rows)
            length = min(rows - row, (s + 1) * count - at)
            found.append((s, tap, row, at - s * count, length))
            at += length
    return found


def head_kernel(
    n,
    packed,
    squeezed_ref,
    edge_ref,
    cot_ref,
    hidden_ref,
    projection_ref,
    squeeze_ref,
    first_ref,
    second_ref,
    third_ref,
    final_ref,
    scores_ref,
    edge_scores_ref,
    delta_ref,
    edge_projected_ref,
    *outs,
):
    frames = squeezed_ref.shape[0]
    total = EDGE + frames
    seq, odd = here()
    row = lax.broadcasted_iota(jnp.int32, (total, LANES), 0)
    frame = row - jnp.where(row >= frames, odd * total, 0)
    before = jnp.where((odd == 1) & (seq > 0), REACH, 0)
    after = jnp.where((odd == 0) & (seq < n - 1), REACH, 0)
    inside = (frame >= -2 * before) & (frame < frames + 2 * after)
    first = jnp.where((odd == 0) & (seq > 0), REACH, -before)
    last = jnp.where((odd == 1) & (seq < n - 1), -REACH, after)
    window = (frame >= first) & (frame < frames + last)

    def mask(values, where):
        width = values.shape[1]
        if width <= LANES:
            return jnp.where(where[:, :width], values, 0.0)
        return jnp.concatenate(
            [jnp.where(where, values[:, i : i + LANES], 0.0) for i in range(0, width, LANES)], axis=1
        )

    edge_projected, edge_hidden, edge_squeezed = forward_rows(
        edge_ref[...], projection_ref[...], squeeze_ref[...]
    )
    edge_projected_ref[...] = edge_projected
    squeezed = jnp.concatenate([squeezed_ref[...], edge_squeezed], axis=0)

    parts = edge_ref[:, :LANES].astype(F32)
    parts = jnp.where(odd == 0, parts[EDGE - MORE :], parts[:MORE])
    parts = parts[0:1] + parts[1:2] + parts[2:3]
    columns = jnp.concatenate([cot_ref[...], parts, jnp.zeros((6, LANES), F32)], axis=0).T
    cot = jnp.concatenate(
        [
            jnp.broadcast_to(columns[:, 0:1], (frames, LANES)),
            jnp.broadcast_to(
                jnp.where(odd == 0, columns[:EDGE, 1:2], columns[frames - EDGE :, 1:2]), (EDGE, LANES)
            ),
        ],
        axis=0,
    )
    cot = mask(cot, inside)

    weights = (first_ref, second_ref, third_ref)
    act = squeezed
    inputs, slopes = [], []
    for ref in weights:
        unit, slope = leaky_pair(act)
        unit = mask(unit, inside)
        slopes.append(slope)
        inputs.append(mask(unit, window).astype(BF16))
        width = unit.shape[1]
        act = jnp.zeros((total, ref.shape[1]), F32)
        for k, piece in enumerate(shifted(unit, HK, 1)):
            act = act + dot(piece, ref[k * width : (k + 1) * width, :])
    unit, slope = leaky_pair(act)
    final_in = mask(unit, inside).astype(BF16).astype(F32)
    taps = shifted(final_in, PK, 1)
    for ref, rows in ((scores_ref, slice(0, frames)), (edge_scores_ref, slice(total - LANES, total))):
        scores = jnp.zeros((1, rows.stop - rows.start), F32)
        for k in range(PK):
            scores = scores + dot(final_ref[:, k * C2 : (k + 1) * C2], taps[k][rows], NT)
        ref[...] = scores

    upstream = [jnp.zeros((total, LANES), F32)] * (C2 // LANES)
    final_grad = []
    final_in = mask(final_in, window)
    for k in range(PK):
        amount = (k - 1) % total
        moved = cot if amount == 0 else pltpu.roll(cot, amount, 0)
        for h in range(C2 // LANES):
            lanes = slice(k * C2 + h * LANES, k * C2 + (h + 1) * LANES)
            upstream[h] = upstream[h] + moved * final_ref[:, lanes].astype(F32)
            final_grad.append(
                jnp.sum(moved * final_in[:, h * LANES : (h + 1) * LANES], axis=0, keepdims=True)
            )
    upstream = jnp.concatenate(upstream, axis=1)
    slopes.append(slope)
    grads = []
    for layer in (2, 1, 0):
        delta = mask(upstream * slopes[layer + 1], inside)
        pieces = shifted(delta, HK, -1)
        grads.append(dot(inputs[layer], jnp.concatenate(pieces, axis=1), TN))
        ref = weights[layer]
        width = ref.shape[0] // HK
        upstream = jnp.zeros((total, width), F32)
        for k, piece in enumerate(pieces):
            upstream = upstream + dot(piece, ref[k * width : (k + 1) * width, :], NT)
    third, second, first = grads
    delta = mask(upstream * slopes[0], inside)
    delta_ref[...] = delta.astype(BF16)
    hidden = jnp.concatenate([hidden_ref[...], edge_hidden], axis=0)
    squeeze_grad = dot(mask(delta, window).astype(BF16), hidden, TN)

    if not packed:
        squeeze_out, first_out, second_out, third_out, final_out = outs
        squeeze_out[...] = squeeze_grad
        for out, grad in ((first_out, first), (second_out, second), (third_out, third)):
            width, cols = grad.shape[0], out.shape[1]
            for k in range(HK):
                out[k * width : (k + 1) * width, :] = grad[:, k * cols : (k + 1) * cols]
        for i, part in enumerate(final_grad):
            final_out[:, i * LANES : (i + 1) * LANES] = part
        return

    (payload_ref, scratch) = outs
    half = payload_ref.shape[3]
    mine = [(seq ^ s) for s in range(n)]

    def put(s, at, rows):
        slot = mine[s]
        while rows.shape[0]:
            side, start = divmod(at, half)
            length = min(rows.shape[0], half - start)
            payload_ref[side ^ odd, slot & 3, slot >> 2, start : start + length, :] = rows[:length]
            rows = rows[length:]
            at += length

    base = 0
    for grad, channels, cols in ((third, C2, C2), (second, C1, C2)):
        count = HK * channels // n
        for s, tap, start, offset, length in pieces_of(n, count, channels):
            for h in range(cols // LANES):
                lanes = slice(tap * cols + h * LANES, tap * cols + (h + 1) * LANES)
                scratch[s, base + h * count + offset : base + h * count + offset + length, :] = grad[
                    start : start + length, lanes
                ]
        base += count * (cols // LANES)
    count = C0 // n
    for s in range(n):
        for h in range(squeeze_grad.shape[1] // LANES):
            scratch[s, base + h * count : base + (h + 1) * count, :] = squeeze_grad[
                s * count : (s + 1) * count, h * LANES : (h + 1) * LANES
            ]
    base += count * (squeeze_grad.shape[1] // LANES)
    count = HK * C0 // n
    for s, tap, start, offset, length in pieces_of(n, count, C0):
        scratch[s, base + offset : base + offset + length, :] = first[
            start : start + length, tap * C1 : (tap + 1) * C1
        ]
    base += count
    final_row = jnp.concatenate(final_grad, axis=1)
    count = final_row.shape[1] // n
    for s in range(n):
        first_half = s * count // LANES * LANES
        piece = final_row[:, first_half : first_half + 2 * LANES]
        if piece.shape[1] < 2 * LANES:
            piece = jnp.concatenate([piece, piece[:, :LANES]], axis=1)
        amount = (first_half - s * count) % (2 * LANES)
        piece = piece if amount == 0 else pltpu.roll(jnp.broadcast_to(piece, (8, 2 * LANES)), amount, 1)
        scratch[s, base : base + 1, :] = piece[0:1, :LANES]
        scratch[s, base + 1 :, :] = jnp.zeros((scratch.shape[1] - base - 1, LANES), F32)
    for s in range(n):
        put(s, 0, scratch[s].astype(BF16))


def feature_kernel(
    rows_ref, edge_ref, projected_ref, edge_projected_ref, delta_ref, after_ref, squeeze_ref, projection_ref, out_ref, back_ref
):
    hidden_upstream = dot(delta_ref[...], squeeze_ref[...])
    projected = jnp.concatenate([projected_ref[...], edge_projected_ref[...]], axis=0)
    hidden_normed, hidden_inverse = normalize(projected.astype(F32))
    projected_grad = normalize_back(hidden_upstream, hidden_normed, hidden_inverse).astype(BF16)
    normed_grad = dot(projected_grad, projection_ref[...], NT)
    rows = jnp.concatenate([rows_ref[...], edge_ref[...]], axis=0)
    normed, inverse = normalize(rows.astype(F32))
    grad = normalize_back(normed_grad, normed, inverse)
    out_ref[...] = grad[:-EDGE]
    back_ref[:BACK, :] = jnp.where(here()[1] == 0, grad[-EDGE : BACK - EDGE], grad[-BACK:])
    back_ref[BACK:, :LANES] = jnp.broadcast_to(after_ref[...], (8, LANES))
    back_ref[BACK:, LANES:] = jnp.zeros((8, back_ref.shape[1] - LANES), F32)


def assemble_kernel(n, own_ref, scores_ref, back_ref, grad_ref, final_scores_ref):
    frames = own_ref.shape[0]
    seq, odd = here()
    low, high = (odd == 0) & (seq > 0), (odd == 1) & (seq < n - 1)
    grad_ref[BACK : frames - BACK, :] = own_ref[BACK : frames - BACK, :]
    row = lax.broadcasted_iota(jnp.int32, (BACK, own_ref.shape[1]), 0)
    came = back_ref[:BACK, :]
    grad_ref[:BACK, :] = jnp.where(low & (row < REACH), came, own_ref[:BACK, :])
    grad_ref[frames - BACK :, :] = jnp.where(high & (row >= BACK - REACH), came, own_ref[frames - BACK :, :])
    scores = back_ref[BACK:, :LANES]
    moved = pltpu.roll(scores, EDGE, 1)
    lane = lax.broadcasted_iota(jnp.int32, (1, frames), 1)
    kept = jnp.where(high & (lane >= frames - REACH), scores[0:1], scores_ref[...])
    final_scores_ref[...] = jnp.where(low & (lane < REACH), moved[0:1], kept)


def unpack_kernel(factor, mine_ref, other_ref, squeeze_ref, first_ref, second_ref, third_ref, final_ref, both):
    half = mine_ref.shape[0]
    _, core = here()
    both[pl.ds(pl.multiple_of(core * half, 16), half), :] = mine_ref[...].astype(F32) * factor
    both[pl.ds(pl.multiple_of((1 - core) * half, 16), half), :] = other_ref[...].astype(F32) * factor
    base = 0
    for ref in (third_ref, second_ref, squeeze_ref, first_ref):
        count = ref.shape[0]
        for h in range(ref.shape[1] // LANES):
            ref[:, h * LANES : (h + 1) * LANES] = both[base : base + count, :]
            base += count
    final_ref[...] = both[base : base + 1, : final_ref.shape[1]]


def sds(shape, dtype):
    return jax.ShapeDtypeStruct(shape, dtype)


def hbm(array):
    return pltpu.with_memory_space_constraint(array, pltpu.HBM)


def vmem(shape, dtype):
    return pltpu.VMEM(shape, dtype)


VMEM = pl.BlockSpec(memory_space=pltpu.VMEM)
HBM = pl.BlockSpec(memory_space=pltpu.HBM)


def params(mib):
    return pltpu.CompilerParams(vmem_limit_bytes=mib * 1024 * 1024)


def cost(flops, nbytes):
    return pl.CostEstimate(flops=flops, bytes_accessed=nbytes, transcendentals=0)


def shards(
    features,
    score_cotangent,
    projection_weight,
    squeeze_weight,
    first_weight,
    second_weight,
    third_weight,
    final_weight,
):
    n, cores = lax.axis_size("seq"), lax.axis_size("dp")
    frames, feat = features.shape[1:]
    width = projection_weight.shape[1]
    packed = n == 16 and cores == 2
    rows = features.reshape(frames, feat)
    along = []
    for i in range(0, cores * n, n):
        down = [(i + j + 1, i + j) for j in range(n - 1)]
        along += down if i // n % 2 == 0 else [(target, source) for source, target in down]
    for i in range(0, (cores // 2) * 2 * n, 2 * n):
        along += [(i, i + n), (i + 2 * n - 1, i + n - 1)]
    along = sorted(along)
    returning = sorted((target, source) for source, target in along)

    edge = pl.pallas_call(
        edge_kernel,
        in_specs=[HBM, HBM],
        out_specs=VMEM,
        out_shape=vmem((EDGE, feat), BF16),
        scratch_shapes=[pltpu.VMEM((EDGE, feat), BF16), pltpu.VMEM((1, frames), F32), pltpu.SemaphoreType.DMA((2,))],
        name="edge",
    )(hbm(rows), hbm(score_cotangent))
    edge = lax.ppermute(edge, ("dp", "seq"), along)

    sources = (
        rows,
        projection_weight,
        squeeze_weight,
        score_cotangent,
        first_weight,
        second_weight,
        third_weight,
    )
    rows, projection, squeeze, cot, first, second, third, projected, hidden, squeezed = pl.pallas_call(
        functools.partial(project_kernel, len(sources)),
        in_specs=[HBM] * len(sources),
        out_specs=[VMEM] * (len(sources) + 3),
        out_shape=[
            *[vmem(a.shape, a.dtype) for a in sources],
            vmem((frames, width), BF16),
            vmem((frames, width), BF16),
            vmem((frames, C0), F32),
        ],
        scratch_shapes=[pltpu.SemaphoreType.DMA((len(sources),))],
        compiler_params=params(8),
        cost_estimate=cost(2 * frames * width * (feat + C0), 2 * feat * width),
        name="project",
    )(*[hbm(a) for a in sources])

    if packed:
        half = 144
        grad_shapes = [sds((2, 4, 4, half, LANES), BF16)]
        scratch = [pltpu.VMEM((n, 2 * half, LANES), F32)]
    else:
        grad_shapes = [
            sds((C0, width), F32),
            sds(first_weight.shape, F32),
            sds(second_weight.shape, F32),
            sds(third_weight.shape, F32),
            sds((1, PK * C2), F32),
        ]
        scratch = []
    own_scores, after, delta, edge_projected, *grads = pl.pallas_call(
        functools.partial(head_kernel, n, packed),
        in_specs=[VMEM] * 10,
        out_specs=[VMEM] * (4 + len(grad_shapes)),
        out_shape=[
            sds((1, frames), F32),
            sds((1, LANES), F32),
            sds((frames + EDGE, C0), BF16),
            sds((EDGE, width), BF16),
            *grad_shapes,
        ],
        scratch_shapes=scratch,
        compiler_params=params(20),
        cost_estimate=cost(10**9, 4 * 10**6),
        name="head",
    )(
        squeezed,
        edge,
        cot,
        hidden,
        projection,
        squeeze,
        first,
        second,
        third,
        final_weight.reshape(1, PK * C2),
    )

    def features_back():
        own_grad, back = pl.pallas_call(
            feature_kernel,
            in_specs=[VMEM] * 8,
            out_specs=[VMEM] * 2,
            out_shape=[sds((frames, feat), F32), sds((BACK + 8, feat), F32)],
            compiler_params=params(8),
            cost_estimate=cost(2 * frames * width * (feat + C0), 2 * feat * width),
            name="feature",
        )(rows, edge, projected, edge_projected, delta, after, squeeze, projection)
        back = lax.ppermute(back, ("dp", "seq"), returning)
        return own_grad, back

    def assembled(own_grad, back):
        feature_grad, scores = pl.pallas_call(
            functools.partial(assemble_kernel, n),
            in_specs=[VMEM] * 3,
            out_specs=[VMEM] * 2,
            out_shape=[sds((frames, feat), F32), sds((1, frames), F32)],
            compiler_params=params(4),
            cost_estimate=cost(frames * feat, 8 * frames * feat),
            name="assemble",
        )(own_grad, own_scores, back)
        return feature_grad[None], scores

    factor = 1.0 / math.sqrt(cores * n * frames)
    if not packed:
        shares = []
        for term in grads[:4] + [grads[4].reshape(PK * C2)]:
            part = lax.psum_scatter(term * factor, "seq", scatter_dimension=0, tiled=True)
            shares.append(lax.psum(part.astype(BF16), "dp").astype(F32))
        feature_grad, scores = assembled(*features_back())
        return (scores, feature_grad, *shares)

    def added(*terms):
        total = terms[0].astype(F32)
        for term in terms[1:]:
            total = total + term.astype(F32)
        return total.astype(BF16)

    swap = [(0, 1), (1, 0)]
    (payload,) = grads
    held = added(payload[0], lax.ppermute(payload[1], "dp", swap))
    for stride in (1, 4):
        moved = [
            lax.ppermute(held[j], "seq", [(i, i ^ (j * stride)) for i in range(n)]) for j in (3, 1, 2)
        ]
        held = added(held[0], *moved)
        if stride == 1:
            own_grad, back = features_back()
            held, own_grad = lax.optimization_barrier((held, own_grad))
        else:
            feature_grad, scores = assembled(own_grad, back)
            held, feature_grad, scores = lax.optimization_barrier((held, feature_grad, scores))
    other = lax.ppermute(held, "dp", swap)
    shapes = [
        (C0 // n, width),
        (HK * C0 // n, C1),
        (HK * C1 // n, C2),
        (HK * C2 // n, C2),
        (1, PK * C2 // n),
    ]
    *shares, final = pl.pallas_call(
        functools.partial(unpack_kernel, factor),
        in_specs=[VMEM, VMEM],
        out_specs=[VMEM] * 5,
        out_shape=[sds(shape, F32) for shape in shapes],
        scratch_shapes=[pltpu.VMEM((2 * half, LANES), F32)],
        compiler_params=params(4),
        name="unpack",
    )(held, other)
    return (scores, feature_grad, *shares, final.reshape(PK * C2 // n))


def solution(mesh):
    placed = (P("dp", "seq", None), P("dp", "seq"), P(), P(), P(), P(), P(), P())
    return jax.shard_map(
        shards,
        mesh=mesh,
        in_specs=placed,
        out_specs=(
            P("dp", "seq"),
            P("dp", "seq", None),
            P("seq", None),
            P("seq", None),
            P("seq", None),
            P("seq", None),
            P("seq"),
        ),
        check_vma=False,
    )
```

```python
import functools
import math

import jax
import jax.numpy as jnp
from jax import lax
from jax.experimental import pallas as pl
from jax.experimental.pallas import tpu as pltpu
from jax.sharding import PartitionSpec as P

C0 = 64
C1 = 128
C2 = 256
HK = 5
PK = 3
EDGE = 32
REACH = 12
MORE = 8
BACK = 16
LANES = 128

EPSILON = 1e-05
SLOPE = 0.1
BF16 = jnp.bfloat16
F32 = jnp.float32
NT = (((1,), (1,)), ((), ()))
TN = (((0,), (0,)), ((), ()))


def normalize(values):
    average = jnp.mean(values, axis=-1, keepdims=True)
    centred = values - average
    variance = jnp.mean(centred * centred, axis=-1, keepdims=True)
    inverse = lax.rsqrt(variance + EPSILON)
    return (centred * inverse, inverse)


def normalize_back(upstream, normed, inverse):
    first_mean = jnp.mean(upstream, axis=-1, keepdims=True)
    second_mean = jnp.mean(upstream * normed, axis=-1, keepdims=True)
    return (upstream - first_mean - normed * second_mean) * inverse


def leaky_pair(values):
    cumulative = 0.5 * (1.0 + lax.erf(values * math.sqrt(0.5)))
    density = jnp.exp(-0.5 * values * values) * (1.0 / math.sqrt(2.0 * math.pi))
    unit = SLOPE * values + (1.0 - SLOPE) * (values * cumulative)
    slope = SLOPE + (1.0 - SLOPE) * (cumulative + values * density)
    return unit, slope


def dot(a, b, dims=(((1,), (0,)), ((), ()))):
    return lax.dot_general(a, b, dims, preferred_element_type=F32)


def forward_rows(rows, projection, squeeze):
    normed, _ = normalize(rows.astype(F32))
    projected = dot(normed.astype(BF16), projection).astype(BF16)
    hidden_normed, _ = normalize(projected.astype(F32))
    hidden = hidden_normed.astype(BF16)
    return projected, hidden, dot(hidden, squeeze, NT)


def here():
    return lax.axis_index("seq"), lax.rem(lax.axis_index("dp"), 2)


def edge_kernel(rows_ref, cot_ref, out_ref, held, cot_held, sems):
    frames, feat = rows_ref.shape
    _, odd = here()
    start = pl.multiple_of(odd * (frames - EDGE), 16)
    copies = [
        pltpu.make_async_copy(cot_ref, cot_held, sems.at[0]),
        pltpu.make_async_copy(rows_ref.at[pl.ds(start, EDGE)], held, sems.at[1]),
    ]
    for copy in copies:
        copy.start()
    copies[0].wait()
    cot = cot_held[...]
    high = cot.astype(BF16).astype(F32)
    middle = (cot - high).astype(BF16).astype(F32)
    low = cot - high - middle
    stack = jnp.concatenate([high, middle, low, jnp.zeros((MORE - 3, frames), F32)], axis=0)
    stack = jnp.concatenate([stack] * (EDGE // MORE), axis=0)
    row = lax.broadcasted_iota(jnp.int32, (EDGE, frames), 0)
    carries = (row < MORE) & (odd == 1) | (row >= EDGE - MORE) & (odd == 0)
    copies[1].wait()
    out_ref[:, frames:] = held[:, frames:]
    out_ref[:, :frames] = jnp.where(carries, stack, held[:, :frames].astype(F32)).astype(BF16)


def project_kernel(count, final_ref, *refs):
    sources, held = refs[:count], refs[count : 2 * count]
    final_out, final_held = refs[-3], refs[-2]
    final_copy = pltpu.make_async_copy(final_ref, final_held, refs[-1].at[count])
    projected_ref, hidden_ref, squeezed_ref, _, _, sems = refs[2 * count :]
    copies = [pltpu.make_async_copy(a, b, sems.at[i]) for i, (a, b) in enumerate(zip(sources, held))]
    for copy in copies:
        copy.start()
    final_copy.start()
    for copy in copies[:3]:
        copy.wait()
    projected, hidden, squeezed = forward_rows(held[0][...], held[1][...], held[2][...])
    projected_ref[...] = projected
    hidden_ref[...] = hidden
    squeezed_ref[...] = squeezed
    for copy in copies[3:]:
        copy.wait()
    final_copy.wait()
    final_out[...] = final_held[...].reshape(final_out.shape)


def shifted(values, taps, sign):
    count = values.shape[0]
    pieces = []
    for k in range(taps):
        amount = (-sign * (k - (taps - 1) // 2)) % count
        moved = values if amount == 0 else pltpu.roll(values, amount, 0)
        pieces.append(moved.astype(BF16))
    return pieces


PACK = (264, 160, 0, 240, 284)
PACKED = 288


def final_rows(s, n):
    return min(s * (PK * C2 // n) // LANES, PK * C2 // LANES - 2)


def pieces_of(n, count, rows):
    found = []
    for s in range(n):
        at = s * count
        while at < (s + 1) * count:
            tap, row = divmod(at, rows)
            length = min(rows - row, (s + 1) * count - at)
            found.append((s, tap, row, at - s * count, length))
            at += length
    return found


def head_kernel(
    n,
    packed,
    squeezed_ref,
    edge_ref,
    cot_ref,
    hidden_ref,
    projection_ref,
    squeeze_ref,
    first_ref,
    second_ref,
    third_ref,
    final_ref,
    scores_ref,
    edge_scores_ref,
    delta_ref,
    edge_projected_ref,
    *outs,
):
    frames = squeezed_ref.shape[0]
    total = EDGE + frames
    seq, odd = here()
    row = lax.broadcasted_iota(jnp.int32, (total, LANES), 0)
    frame = row - jnp.where(row >= frames, odd * total, 0)
    before = jnp.where((odd == 1) & (seq > 0), REACH, 0)
    after = jnp.where((odd == 0) & (seq < n - 1), REACH, 0)
    inside = (frame >= -2 * before) & (frame < frames + 2 * after)
    first = jnp.where((odd == 0) & (seq > 0), REACH, -before)
    last = jnp.where((odd == 1) & (seq < n - 1), -REACH, after)
    window = (frame >= first) & (frame < frames + last)

    def mask(values, where):
        width = values.shape[1]
        if width <= LANES:
            return jnp.where(where[:, :width], values, 0.0)
        return jnp.concatenate(
            [jnp.where(where, values[:, i : i + LANES], 0.0) for i in range(0, width, LANES)], axis=1
        )

    edge_projected, edge_hidden, edge_squeezed = forward_rows(
        edge_ref[...], projection_ref[...], squeeze_ref[...]
    )
    edge_projected_ref[...] = edge_projected
    squeezed = jnp.concatenate([squeezed_ref[...], edge_squeezed], axis=0)

    parts = edge_ref[:, :LANES].astype(F32)
    parts = jnp.where(odd == 0, parts[EDGE - MORE :], parts[:MORE])
    parts = parts[0:1] + parts[1:2] + parts[2:3]
    columns = jnp.concatenate([cot_ref[...], parts, jnp.zeros((6, LANES), F32)], axis=0).T
    cot = jnp.concatenate(
        [
            jnp.broadcast_to(columns[:, 0:1], (frames, LANES)),
            jnp.broadcast_to(
                jnp.where(odd == 0, columns[:EDGE, 1:2], columns[frames - EDGE :, 1:2]), (EDGE, LANES)
            ),
        ],
        axis=0,
    )
    cot = mask(cot, inside)

    weights = (first_ref, second_ref, third_ref)
    act = squeezed
    inputs, slopes = [], []
    for ref in weights:
        unit, slope = leaky_pair(act)
        unit = mask(unit, inside)
        slopes.append(slope)
        inputs.append(mask(unit, window).astype(BF16))
        width = unit.shape[1]
        act = jnp.zeros((total, ref.shape[1]), F32)
        for k, piece in enumerate(shifted(unit, HK, 1)):
            act = act + dot(piece, ref[k * width : (k + 1) * width, :])
    unit, slope = leaky_pair(act)
    final_in = mask(unit, inside).astype(BF16).astype(F32)
    taps = shifted(final_in, PK, 1)
    for ref, rows in ((scores_ref, slice(0, frames)), (edge_scores_ref, slice(total - LANES, total))):
        scores = jnp.zeros((1, rows.stop - rows.start), F32)
        for k in range(PK):
            scores = scores + dot(final_ref[:, k * C2 : (k + 1) * C2], taps[k][rows], NT)
        ref[...] = scores

    upstream = [jnp.zeros((total, LANES), F32)] * (C2 // LANES)
    final_grad = []
    final_in = mask(final_in, window)
    for k in range(PK):
        amount = (k - 1) % total
        moved = cot if amount == 0 else pltpu.roll(cot, amount, 0)
        for h in range(C2 // LANES):
            lanes = slice(k * C2 + h * LANES, k * C2 + (h + 1) * LANES)
            upstream[h] = upstream[h] + moved * final_ref[:, lanes].astype(F32)
            final_grad.append(
                jnp.sum(moved * final_in[:, h * LANES : (h + 1) * LANES], axis=0, keepdims=True)
            )
    upstream = jnp.concatenate(upstream, axis=1)
    slopes.append(slope)
    if packed:
        payload_ref, scratch = outs
        mine = [seq ^ s for s in range(n)]

        def block(s):
            q, z = mine[s] & 3, mine[s] >> 2
            holder = (z ^ (z >> 1)) & 1
            return holder ^ odd, jnp.where(holder == 0, q, (q >> 1) | ((q & 1) << 1)), z >> 1

    def keep(layer, tap, grad):
        channels, cols = grad.shape
        if not packed:
            outs[layer + 1][tap * channels : (tap + 1) * channels, :] = grad
            return
        count = HK * channels // n
        for s, at, start, offset, length in pieces_of(n, count, channels):
            if at != tap:
                continue
            for h in range(cols // LANES):
                piece = grad[start : start + length, h * LANES : (h + 1) * LANES]
                first_row = PACK[layer] + h * count + offset
                if layer == 2:
                    payload_ref[(*block(s), slice(first_row, first_row + length))] = piece.astype(BF16)
                else:
                    scratch[s, first_row - PACK[1] : first_row - PACK[1] + length, :] = piece

    for layer in (2, 1, 0):
        delta = mask(upstream * slopes[layer + 1], inside)
        pieces = shifted(delta, HK, -1)
        rows = inputs[layer].T
        ref = weights[layer]
        width = ref.shape[0] // HK
        upstream = jnp.zeros((total, width), F32)
        for k, piece in enumerate(pieces):
            upstream = upstream + dot(piece, ref[k * width : (k + 1) * width, :], NT)
        for k, piece in enumerate(pieces):
            keep(layer, k, dot(rows, piece))
    delta = mask(upstream * slopes[0], inside)
    delta_ref[...] = delta.astype(BF16)
    hidden = jnp.concatenate([hidden_ref[...], edge_hidden], axis=0)
    squeeze_grad = dot(mask(delta, window).astype(BF16), hidden, TN)

    if not packed:
        outs[0][...] = squeeze_grad
        for i, part in enumerate(final_grad):
            outs[4][:, i * LANES : (i + 1) * LANES] = part
        return

    count = C0 // n
    for s in range(n):
        for h in range(squeeze_grad.shape[1] // LANES):
            first_row = PACK[3] - PACK[1] + h * count
            scratch[s, first_row : first_row + count, :] = squeeze_grad[
                s * count : (s + 1) * count, h * LANES : (h + 1) * LANES
            ]
        row = final_rows(s, n)
        first_row = PACK[4] - PACK[1]
        scratch[s, first_row : first_row + 1, :] = final_grad[row]
        scratch[s, first_row + 1 : first_row + 2, :] = final_grad[row + 1]
        scratch[s, first_row + 2 :, :] = jnp.zeros((PACKED - PACK[4] - 2, LANES), F32)
        payload_ref[(*block(s), slice(PACK[1], PACKED))] = scratch[s].astype(BF16)


def feature_kernel(
    rows_ref, edge_ref, projected_ref, edge_projected_ref, delta_ref, after_ref, squeeze_ref, projection_ref, out_ref, back_ref
):
    hidden_upstream = dot(delta_ref[...], squeeze_ref[...])
    projected = jnp.concatenate([projected_ref[...], edge_projected_ref[...]], axis=0)
    hidden_normed, hidden_inverse = normalize(projected.astype(F32))
    projected_grad = normalize_back(hidden_upstream, hidden_normed, hidden_inverse).astype(BF16)
    normed_grad = dot(projected_grad, projection_ref[...], NT)
    rows = jnp.concatenate([rows_ref[...], edge_ref[...]], axis=0)
    normed, inverse = normalize(rows.astype(F32))
    grad = normalize_back(normed_grad, normed, inverse)
    out_ref[...] = grad[:-EDGE]
    back_ref[:BACK, :] = jnp.where(here()[1] == 0, grad[-EDGE : BACK - EDGE], grad[-BACK:])
    back_ref[BACK:, :LANES] = jnp.broadcast_to(after_ref[...], (8, LANES))
    back_ref[BACK:, LANES:] = jnp.zeros((8, back_ref.shape[1] - LANES), F32)


def assemble_kernel(n, own_ref, scores_ref, back_ref, grad_ref, final_scores_ref):
    frames = own_ref.shape[0]
    seq, odd = here()
    low, high = (odd == 0) & (seq > 0), (odd == 1) & (seq < n - 1)
    grad_ref[BACK : frames - BACK, :] = own_ref[BACK : frames - BACK, :]
    row = lax.broadcasted_iota(jnp.int32, (BACK, own_ref.shape[1]), 0)
    came = back_ref[:BACK, :]
    grad_ref[:BACK, :] = jnp.where(low & (row < REACH), came, own_ref[:BACK, :])
    grad_ref[frames - BACK :, :] = jnp.where(high & (row >= BACK - REACH), came, own_ref[frames - BACK :, :])
    scores = back_ref[BACK:, :LANES]
    moved = pltpu.roll(scores, EDGE, 1)
    lane = lax.broadcasted_iota(jnp.int32, (1, frames), 1)
    kept = jnp.where(high & (lane >= frames - REACH), scores[0:1], scores_ref[...])
    final_scores_ref[...] = jnp.where(low & (lane < REACH), moved[0:1], kept)


def unpack_kernel(n, factor, mine_ref, other_ref, squeeze_ref, first_ref, second_ref, third_ref, final_ref, both):
    both[...] = (mine_ref[...].astype(F32) + other_ref[...].astype(F32)) * factor
    for base, ref in zip(PACK, (first_ref, second_ref, third_ref, squeeze_ref)):
        count = ref.shape[0]
        for h in range(ref.shape[1] // LANES):
            ref[:, h * LANES : (h + 1) * LANES] = both[base + h * count : base + (h + 1) * count, :]
    count = final_ref.shape[1]
    at = here()[0] * count
    at = at - jnp.minimum(lax.div(at, LANES), PK * C2 // LANES - 2) * LANES
    pair = jnp.concatenate([both[PACK[4] : PACK[4] + 1, :], both[PACK[4] + 1 : PACK[4] + 2, :]], axis=1)
    pair = pltpu.roll(jnp.broadcast_to(pair, (8, 2 * LANES)), 2 * LANES - at, 1)
    final_ref[...] = pair[0:1, :count]


def sds(shape, dtype):
    return jax.ShapeDtypeStruct(shape, dtype)


def hbm(array):
    return pltpu.with_memory_space_constraint(array, pltpu.HBM)


def vmem(shape, dtype):
    return pltpu.VMEM(shape, dtype)


VMEM = pl.BlockSpec(memory_space=pltpu.VMEM)
HBM = pl.BlockSpec(memory_space=pltpu.HBM)


def params(mib):
    return pltpu.CompilerParams(vmem_limit_bytes=mib * 1024 * 1024)


def cost(flops, nbytes):
    return pl.CostEstimate(flops=flops, bytes_accessed=nbytes, transcendentals=0)


def shards(
    features,
    score_cotangent,
    projection_weight,
    squeeze_weight,
    first_weight,
    second_weight,
    third_weight,
    final_weight,
):
    n, cores = lax.axis_size("seq"), lax.axis_size("dp")
    frames, feat = features.shape[1:]
    width = projection_weight.shape[1]
    packed = n == 16 and cores == 2
    rows = features.reshape(frames, feat)
    along = []
    for i in range(0, cores * n, n):
        down = [(i + j + 1, i + j) for j in range(n - 1)]
        along += down if i // n % 2 == 0 else [(target, source) for source, target in down]
    for i in range(0, (cores // 2) * 2 * n, 2 * n):
        along += [(i, i + n), (i + 2 * n - 1, i + n - 1)]
    along = sorted(along)
    returning = sorted((target, source) for source, target in along)

    edge = pl.pallas_call(
        edge_kernel,
        in_specs=[HBM, HBM],
        out_specs=VMEM,
        out_shape=vmem((EDGE, feat), BF16),
        scratch_shapes=[pltpu.VMEM((EDGE, feat), BF16), pltpu.VMEM((1, frames), F32), pltpu.SemaphoreType.DMA((2,))],
        name="edge",
    )(hbm(rows), hbm(score_cotangent))
    edge = lax.ppermute(edge, ("dp", "seq"), along)

    sources = (
        rows,
        projection_weight,
        squeeze_weight,
        score_cotangent,
        first_weight,
        second_weight,
        third_weight,
    )
    rows, projection, squeeze, cot, first, second, third, projected, hidden, squeezed, final = pl.pallas_call(
        functools.partial(project_kernel, len(sources)),
        in_specs=[HBM] * (1 + len(sources)),
        out_specs=[VMEM] * (len(sources) + 4),
        out_shape=[
            *[vmem(a.shape, a.dtype) for a in sources],
            vmem((frames, width), BF16),
            vmem((frames, width), BF16),
            vmem((frames, C0), F32),
            vmem((1, PK * C2), BF16),
        ],
        scratch_shapes=[pltpu.VMEM((PK * C2,), BF16), pltpu.SemaphoreType.DMA((len(sources) + 1,))],
        compiler_params=params(8),
        cost_estimate=cost(2 * frames * width * (feat + C0), 2 * feat * width),
        name="project",
    )(hbm(final_weight), *[hbm(a) for a in sources])

    if packed:
        grad_shapes = [sds((2, 4, 2, PACKED, LANES), BF16)]
        scratch = [pltpu.VMEM((n, PACKED - PACK[1], LANES), F32)]
    else:
        grad_shapes = [
            sds((C0, width), F32),
            sds(first_weight.shape, F32),
            sds(second_weight.shape, F32),
            sds(third_weight.shape, F32),
            sds((1, PK * C2), F32),
        ]
        scratch = []
    own_scores, after, delta, edge_projected, *grads = pl.pallas_call(
        functools.partial(head_kernel, n, packed),
        in_specs=[VMEM] * 10,
        out_specs=[VMEM] * (4 + len(grad_shapes)),
        out_shape=[
            sds((1, frames), F32),
            sds((1, LANES), F32),
            sds((frames + EDGE, C0), BF16),
            sds((EDGE, width), BF16),
            *grad_shapes,
        ],
        scratch_shapes=scratch,
        compiler_params=params(20),
        cost_estimate=cost(10**9, 4 * 10**6),
        name="head",
    )(
        squeezed,
        edge,
        cot,
        hidden,
        projection,
        squeeze,
        first,
        second,
        third,
        final,
    )

    def features_back():
        own_grad, back = pl.pallas_call(
            feature_kernel,
            in_specs=[VMEM] * 8,
            out_specs=[VMEM] * 2,
            out_shape=[sds((frames, feat), F32), sds((BACK + 8, feat), F32)],
            compiler_params=params(8),
            cost_estimate=cost(2 * frames * width * (feat + C0), 2 * feat * width),
            name="feature",
        )(rows, edge, projected, edge_projected, delta, after, squeeze, projection)
        back = lax.ppermute(back, ("dp", "seq"), returning)
        return own_grad, back

    def assembled(own_grad, back):
        feature_grad, scores = pl.pallas_call(
            functools.partial(assemble_kernel, n),
            in_specs=[VMEM] * 3,
            out_specs=[VMEM] * 2,
            out_shape=[sds((frames, feat), F32), sds((1, frames), F32)],
            compiler_params=params(4),
            cost_estimate=cost(frames * feat, 8 * frames * feat),
            name="assemble",
        )(own_grad, own_scores, back)
        return feature_grad[None], scores

    factor = 1.0 / math.sqrt(cores * n * frames)
    if not packed:
        shares = []
        for term in grads[:4] + [grads[4].reshape(PK * C2)]:
            part = lax.psum_scatter(term * factor, "seq", scatter_dimension=0, tiled=True)
            shares.append(lax.psum(part.astype(BF16), "dp").astype(F32))
        feature_grad, scores = assembled(*features_back())
        return (scores, feature_grad, *shares)

    def added(*terms):
        total = terms[0].astype(F32)
        for term in terms[1:]:
            total = total + term.astype(F32)
        return total.astype(BF16)

    def mixed(zero, one):
        return [(i, i ^ zero) for i in range(n)] + [(n + i, n + (i ^ one)) for i in range(n)]

    swap = [(0, 1), (1, 0)]
    (payload,) = grads
    came = lax.ppermute(payload[1], "dp", swap)
    own_grad, back = features_back()
    came, own_grad = lax.optimization_barrier((came, own_grad))
    held = added(payload[0], came)
    moved = [lax.ppermute(held[j], ("dp", "seq"), mixed(j, (j >> 1) | ((j & 1) << 1))) for j in (1, 3, 2)]
    held, back = lax.optimization_barrier((added(held[0], *moved), back))
    held = added(
        lax.ppermute(held[1], ("dp", "seq"), mixed(12, 8)), lax.ppermute(held[0], ("dp", "seq"), mixed(0, 4))
    )
    feature_grad, scores = assembled(own_grad, back)
    held, feature_grad, scores = lax.optimization_barrier((held, feature_grad, scores))
    other = lax.ppermute(held, "dp", swap)
    shapes = [
        (C0 // n, width),
        (HK * C0 // n, C1),
        (HK * C1 // n, C2),
        (HK * C2 // n, C2),
        (1, PK * C2 // n),
    ]
    *shares, final = pl.pallas_call(
        functools.partial(unpack_kernel, n, factor),
        in_specs=[VMEM, VMEM],
        out_specs=[VMEM] * 5,
        out_shape=[sds(shape, F32) for shape in shapes],
        scratch_shapes=[pltpu.VMEM((PACKED, LANES), F32)],
        compiler_params=params(4),
        name="unpack",
    )(held, other)
    return (scores, feature_grad, *shares, final.reshape(PK * C2 // n))


def solution(mesh):
    placed = (P("dp", "seq", None), P("dp", "seq"), P(), P(), P(), P(), P(), P())
    return jax.shard_map(
        shards,
        mesh=mesh,
        in_specs=placed,
        out_specs=(
            P("dp", "seq"),
            P("dp", "seq", None),
            P("seq", None),
            P("seq", None),
            P("seq", None),
            P("seq", None),
            P("seq"),
        ),
        check_vma=False,
    )
```

```python
import functools
import math

import jax
import jax.numpy as jnp
from jax import lax
from jax.experimental import pallas as pl
from jax.experimental.pallas import tpu as pltpu
from jax.sharding import PartitionSpec as P

C0 = 64
C1 = 128
C2 = 256
HK = 5
PK = 3
EDGE = 32
REACH = 12
MORE = 8
BACK = 16
LANES = 128

EPSILON = 1e-05
SLOPE = 0.1
BF16 = jnp.bfloat16
F32 = jnp.float32
NT = (((1,), (1,)), ((), ()))
TN = (((0,), (0,)), ((), ()))


def normalize(values):
    average = jnp.mean(values, axis=-1, keepdims=True)
    centred = values - average
    variance = jnp.mean(centred * centred, axis=-1, keepdims=True)
    inverse = lax.rsqrt(variance + EPSILON)
    return (centred * inverse, inverse)


def normalize_back(upstream, normed, inverse):
    first_mean = jnp.mean(upstream, axis=-1, keepdims=True)
    second_mean = jnp.mean(upstream * normed, axis=-1, keepdims=True)
    return (upstream - first_mean - normed * second_mean) * inverse


def leaky_pair(values):
    cumulative = 0.5 * (1.0 + lax.erf(values * math.sqrt(0.5)))
    density = jnp.exp(-0.5 * values * values) * (1.0 / math.sqrt(2.0 * math.pi))
    unit = SLOPE * values + (1.0 - SLOPE) * (values * cumulative)
    slope = SLOPE + (1.0 - SLOPE) * (cumulative + values * density)
    return unit, slope


def dot(a, b, dims=(((1,), (0,)), ((), ()))):
    return lax.dot_general(a, b, dims, preferred_element_type=F32)


def forward_rows(rows, projection, squeeze):
    normed, _ = normalize(rows.astype(F32))
    projected = dot(normed.astype(BF16), projection).astype(BF16)
    hidden_normed, _ = normalize(projected.astype(F32))
    hidden = hidden_normed.astype(BF16)
    return projected, hidden, dot(hidden, squeeze, NT)


def here():
    return lax.axis_index("seq"), lax.rem(lax.axis_index("dp"), 2)


def edge_kernel(rows_ref, cot_ref, out_ref, held, cot_held, sems):
    frames, feat = rows_ref.shape
    _, odd = here()
    start = pl.multiple_of(odd * (frames - EDGE), 16)
    copies = [
        pltpu.make_async_copy(cot_ref, cot_held, sems.at[0]),
        pltpu.make_async_copy(rows_ref.at[pl.ds(start, EDGE)], held, sems.at[1]),
    ]
    for copy in copies:
        copy.start()
    copies[0].wait()
    cot = cot_held[...]
    high = cot.astype(BF16).astype(F32)
    middle = (cot - high).astype(BF16).astype(F32)
    low = cot - high - middle
    stack = jnp.concatenate([high, middle, low, jnp.zeros((MORE - 3, frames), F32)], axis=0)
    stack = jnp.concatenate([stack] * (EDGE // MORE), axis=0)
    row = lax.broadcasted_iota(jnp.int32, (EDGE, frames), 0)
    carries = (row < MORE) & (odd == 1) | (row >= EDGE - MORE) & (odd == 0)
    copies[1].wait()
    out_ref[:, frames:] = held[:, frames:]
    out_ref[:, :frames] = jnp.where(carries, stack, held[:, :frames].astype(F32)).astype(BF16)


def project_kernel(count, final_ref, *refs):
    sources, held = refs[:count], refs[count : 2 * count]
    final_out, final_held = refs[-3], refs[-2]
    final_copy = pltpu.make_async_copy(final_ref, final_held, refs[-1].at[count])
    projected_ref, hidden_ref, squeezed_ref, _, _, sems = refs[2 * count :]
    copies = [pltpu.make_async_copy(a, b, sems.at[i]) for i, (a, b) in enumerate(zip(sources, held))]
    for copy in copies:
        copy.start()
    final_copy.start()
    for copy in copies[:3]:
        copy.wait()
    projected, hidden, squeezed = forward_rows(held[0][...], held[1][...], held[2][...])
    projected_ref[...] = projected
    hidden_ref[...] = hidden
    squeezed_ref[...] = squeezed
    for copy in copies[3:]:
        copy.wait()
    final_copy.wait()
    final_out[...] = final_held[...].reshape(final_out.shape)


def shifted(values, taps, sign):
    count = values.shape[0]
    pieces = []
    for k in range(taps):
        amount = (-sign * (k - (taps - 1) // 2)) % count
        moved = values if amount == 0 else pltpu.roll(values, amount, 0)
        pieces.append(moved.astype(BF16))
    return pieces


PACK = (264, 160, 0, 240, 284)
PACKED = 288


def final_rows(s, n):
    return min(s * (PK * C2 // n) // LANES, PK * C2 // LANES - 2)


def pieces_of(n, count, rows):
    found = []
    for s in range(n):
        at = s * count
        while at < (s + 1) * count:
            tap, row = divmod(at, rows)
            length = min(rows - row, (s + 1) * count - at)
            found.append((s, tap, row, at - s * count, length))
            at += length
    return found


def head_kernel(
    n,
    packed,
    squeezed_ref,
    edge_ref,
    cot_ref,
    hidden_ref,
    projection_ref,
    squeeze_ref,
    first_ref,
    second_ref,
    third_ref,
    final_ref,
    scores_ref,
    edge_scores_ref,
    delta_ref,
    edge_projected_ref,
    *outs,
):
    frames = squeezed_ref.shape[0]
    total = EDGE + frames
    seq, odd = here()
    row = lax.broadcasted_iota(jnp.int32, (total, LANES), 0)
    frame = row - jnp.where(row >= frames, odd * total, 0)
    before = jnp.where((odd == 1) & (seq > 0), REACH, 0)
    after = jnp.where((odd == 0) & (seq < n - 1), REACH, 0)
    inside = (frame >= -2 * before) & (frame < frames + 2 * after)
    first = jnp.where((odd == 0) & (seq > 0), REACH, -before)
    last = jnp.where((odd == 1) & (seq < n - 1), -REACH, after)
    window = (frame >= first) & (frame < frames + last)

    def mask(values, where):
        width = values.shape[1]
        if width <= LANES:
            return jnp.where(where[:, :width], values, 0.0)
        return jnp.concatenate(
            [jnp.where(where, values[:, i : i + LANES], 0.0) for i in range(0, width, LANES)], axis=1
        )

    edge_projected, edge_hidden, edge_squeezed = forward_rows(
        edge_ref[...], projection_ref[...], squeeze_ref[...]
    )
    edge_projected_ref[...] = edge_projected
    squeezed = jnp.concatenate([squeezed_ref[...], edge_squeezed], axis=0)

    parts = edge_ref[:, :LANES].astype(F32)
    parts = jnp.where(odd == 0, parts[EDGE - MORE :], parts[:MORE])
    parts = parts[0:1] + parts[1:2] + parts[2:3]
    columns = jnp.concatenate([cot_ref[...], parts, jnp.zeros((6, LANES), F32)], axis=0).T
    cot = jnp.concatenate(
        [
            jnp.broadcast_to(columns[:, 0:1], (frames, LANES)),
            jnp.broadcast_to(
                jnp.where(odd == 0, columns[:EDGE, 1:2], columns[frames - EDGE :, 1:2]), (EDGE, LANES)
            ),
        ],
        axis=0,
    )
    cot = mask(cot, inside)

    weights = (first_ref, second_ref, third_ref)
    act = squeezed
    inputs, slopes = [], []
    for ref in weights:
        unit, slope = leaky_pair(act)
        unit = mask(unit, inside)
        slopes.append(slope)
        inputs.append(mask(unit, window).astype(BF16))
        width = unit.shape[1]
        pieces = shifted(unit, HK, 1)
        if width % LANES == 0:
            act = dot(jnp.concatenate(pieces, axis=1), ref[...])
        else:
            act = jnp.zeros((total, ref.shape[1]), F32)
            for k, piece in enumerate(pieces):
                act = act + dot(piece, ref[k * width : (k + 1) * width, :])
    unit, slope = leaky_pair(act)
    final_in = mask(unit, inside).astype(BF16).astype(F32)
    taps = shifted(final_in, PK, 1)
    for ref, rows in ((scores_ref, slice(0, frames)), (edge_scores_ref, slice(total - LANES, total))):
        scores = jnp.zeros((1, rows.stop - rows.start), F32)
        for k in range(PK):
            scores = scores + dot(final_ref[:, k * C2 : (k + 1) * C2], taps[k][rows], NT)
        ref[...] = scores

    upstream = [jnp.zeros((total, LANES), F32)] * (C2 // LANES)
    final_grad = []
    final_in = mask(final_in, window)
    for k in range(PK):
        amount = (k - 1) % total
        moved = cot if amount == 0 else pltpu.roll(cot, amount, 0)
        for h in range(C2 // LANES):
            lanes = slice(k * C2 + h * LANES, k * C2 + (h + 1) * LANES)
            upstream[h] = upstream[h] + moved * final_ref[:, lanes].astype(F32)
            final_grad.append(
                jnp.sum(moved * final_in[:, h * LANES : (h + 1) * LANES], axis=0, keepdims=True)
            )
    upstream = jnp.concatenate(upstream, axis=1)
    slopes.append(slope)
    if packed:
        payload_ref, scratch = outs
        mine = [seq ^ s for s in range(n)]

        def block(s):
            q, z = mine[s] & 3, mine[s] >> 2
            holder = (z ^ (z >> 1)) & 1
            return holder ^ odd, jnp.where(holder == 0, q, (q >> 1) | ((q & 1) << 1)), z >> 1

    def keep(layer, tap, grad):
        channels, cols = grad.shape
        if not packed:
            outs[layer + 1][tap * channels : (tap + 1) * channels, :] = grad
            return
        count = HK * channels // n
        for s, at, start, offset, length in pieces_of(n, count, channels):
            if at != tap:
                continue
            for h in range(cols // LANES):
                piece = grad[start : start + length, h * LANES : (h + 1) * LANES]
                first_row = PACK[layer] + h * count + offset
                if layer == 2:
                    payload_ref[(*block(s), slice(first_row, first_row + length))] = piece.astype(BF16)
                else:
                    scratch[s, first_row - PACK[1] : first_row - PACK[1] + length, :] = piece

    for layer in (2, 1, 0):
        delta = mask(upstream * slopes[layer + 1], inside)
        pieces = shifted(delta, HK, -1)
        rows = inputs[layer].T
        ref = weights[layer]
        width = ref.shape[0] // HK
        upstream = jnp.zeros((total, width), F32)
        for k, piece in enumerate(pieces):
            upstream = upstream + dot(piece, ref[k * width : (k + 1) * width, :], NT)
        for k, piece in enumerate(pieces):
            keep(layer, k, dot(rows, piece))
    delta = mask(upstream * slopes[0], inside)
    delta_ref[...] = delta.astype(BF16)
    hidden = jnp.concatenate([hidden_ref[...], edge_hidden], axis=0)
    squeeze_grad = dot(mask(delta, window).astype(BF16), hidden, TN)

    if not packed:
        outs[0][...] = squeeze_grad
        for i, part in enumerate(final_grad):
            outs[4][:, i * LANES : (i + 1) * LANES] = part
        return

    count = C0 // n
    for s in range(n):
        for h in range(squeeze_grad.shape[1] // LANES):
            first_row = PACK[3] - PACK[1] + h * count
            scratch[s, first_row : first_row + count, :] = squeeze_grad[
                s * count : (s + 1) * count, h * LANES : (h + 1) * LANES
            ]
        row = final_rows(s, n)
        first_row = PACK[4] - PACK[1]
        scratch[s, first_row : first_row + 1, :] = final_grad[row]
        scratch[s, first_row + 1 : first_row + 2, :] = final_grad[row + 1]
        scratch[s, first_row + 2 :, :] = jnp.zeros((PACKED - PACK[4] - 2, LANES), F32)
        payload_ref[(*block(s), slice(PACK[1], PACKED))] = scratch[s].astype(BF16)


def feature_kernel(
    rows_ref, edge_ref, projected_ref, edge_projected_ref, delta_ref, edge_scores_ref, squeeze_ref, projection_ref, out_ref, back_ref
):
    hidden_upstream = dot(delta_ref[...], squeeze_ref[...])
    projected = jnp.concatenate([projected_ref[...], edge_projected_ref[...]], axis=0)
    hidden_normed, hidden_inverse = normalize(projected.astype(F32))
    projected_grad = normalize_back(hidden_upstream, hidden_normed, hidden_inverse).astype(BF16)
    normed_grad = dot(projected_grad, projection_ref[...], NT)
    rows = jnp.concatenate([rows_ref[...], edge_ref[...]], axis=0)
    normed, inverse = normalize(rows.astype(F32))
    grad = normalize_back(normed_grad, normed, inverse)
    out_ref[...] = grad[:-EDGE]
    back_ref[:BACK, :] = jnp.where(here()[1] == 0, grad[-EDGE : BACK - EDGE], grad[-BACK:])
    row = lax.broadcasted_iota(jnp.int32, (BACK, LANES), 0)
    spare = jnp.where(here()[1] == 0, row, BACK - 1 - row) >= REACH
    back_ref[:, :LANES] = jnp.where(spare, edge_scores_ref[...], back_ref[:, :LANES])


def assemble_kernel(n, own_ref, scores_ref, back_ref, grad_ref, final_scores_ref):
    frames = own_ref.shape[0]
    seq, odd = here()
    low, high = (odd == 0) & (seq > 0), (odd == 1) & (seq < n - 1)
    grad_ref[BACK : frames - BACK, :] = own_ref[BACK : frames - BACK, :]
    row = lax.broadcasted_iota(jnp.int32, (BACK, own_ref.shape[1]), 0)
    came = back_ref[:BACK, :]
    grad_ref[:BACK, :] = jnp.where(low & (row < REACH), came, own_ref[:BACK, :])
    grad_ref[frames - BACK :, :] = jnp.where(high & (row >= BACK - REACH), came, own_ref[frames - BACK :, :])
    scores = back_ref[:8, :LANES]
    scores = jnp.where(odd == 0, back_ref[BACK - 8 :, :LANES], scores)
    moved = pltpu.roll(scores, EDGE, 1)
    lane = lax.broadcasted_iota(jnp.int32, (1, frames), 1)
    kept = jnp.where(high & (lane >= frames - REACH), scores[0:1], scores_ref[...])
    final_scores_ref[...] = jnp.where(low & (lane < REACH), moved[7:8], kept)


def unpack_kernel(n, factor, mine_ref, other_ref, squeeze_ref, first_ref, second_ref, third_ref, final_ref, both):
    both[...] = (mine_ref[...].astype(F32) + other_ref[...].astype(F32)) * factor
    for base, ref in zip(PACK, (first_ref, second_ref, third_ref, squeeze_ref)):
        count = ref.shape[0]
        for h in range(ref.shape[1] // LANES):
            ref[:, h * LANES : (h + 1) * LANES] = both[base + h * count : base + (h + 1) * count, :]
    count = final_ref.shape[1]
    at = here()[0] * count
    at = at - jnp.minimum(lax.div(at, LANES), PK * C2 // LANES - 2) * LANES
    pair = jnp.concatenate([both[PACK[4] : PACK[4] + 1, :], both[PACK[4] + 1 : PACK[4] + 2, :]], axis=1)
    pair = pltpu.roll(jnp.broadcast_to(pair, (8, 2 * LANES)), 2 * LANES - at, 1)
    final_ref[...] = pair[0:1, :count]


def sds(shape, dtype):
    return jax.ShapeDtypeStruct(shape, dtype)


def hbm(array):
    return pltpu.with_memory_space_constraint(array, pltpu.HBM)


def vmem(shape, dtype):
    return pltpu.VMEM(shape, dtype)


VMEM = pl.BlockSpec(memory_space=pltpu.VMEM)
HBM = pl.BlockSpec(memory_space=pltpu.HBM)


def params(mib):
    return pltpu.CompilerParams(vmem_limit_bytes=mib * 1024 * 1024)


def cost(flops, nbytes):
    return pl.CostEstimate(flops=flops, bytes_accessed=nbytes, transcendentals=0)


def shards(
    features,
    score_cotangent,
    projection_weight,
    squeeze_weight,
    first_weight,
    second_weight,
    third_weight,
    final_weight,
):
    n, cores = lax.axis_size("seq"), lax.axis_size("dp")
    frames, feat = features.shape[1:]
    width = projection_weight.shape[1]
    packed = n == 16 and cores == 2
    rows = features.reshape(frames, feat)
    along = []
    for i in range(0, cores * n, n):
        down = [(i + j + 1, i + j) for j in range(n - 1)]
        along += down if i // n % 2 == 0 else [(target, source) for source, target in down]
    for i in range(0, (cores // 2) * 2 * n, 2 * n):
        along += [(i, i + n), (i + 2 * n - 1, i + n - 1)]
    along = sorted(along)
    returning = sorted((target, source) for source, target in along)

    edge = pl.pallas_call(
        edge_kernel,
        in_specs=[HBM, HBM],
        out_specs=VMEM,
        out_shape=vmem((EDGE, feat), BF16),
        scratch_shapes=[pltpu.VMEM((EDGE, feat), BF16), pltpu.VMEM((1, frames), F32), pltpu.SemaphoreType.DMA((2,))],
        name="edge",
    )(hbm(rows), hbm(score_cotangent))
    edge = lax.ppermute(edge, ("dp", "seq"), along)

    sources = (
        rows,
        projection_weight,
        squeeze_weight,
        score_cotangent,
        first_weight,
        second_weight,
        third_weight,
    )
    rows, projection, squeeze, cot, first, second, third, projected, hidden, squeezed, final = pl.pallas_call(
        functools.partial(project_kernel, len(sources)),
        in_specs=[HBM] * (1 + len(sources)),
        out_specs=[VMEM] * (len(sources) + 4),
        out_shape=[
            *[vmem(a.shape, a.dtype) for a in sources],
            vmem((frames, width), BF16),
            vmem((frames, width), BF16),
            vmem((frames, C0), F32),
            vmem((1, PK * C2), BF16),
        ],
        scratch_shapes=[pltpu.VMEM((PK * C2,), BF16), pltpu.SemaphoreType.DMA((len(sources) + 1,))],
        compiler_params=params(8),
        cost_estimate=cost(2 * frames * width * (feat + C0), 2 * feat * width),
        name="project",
    )(hbm(final_weight), *[hbm(a) for a in sources])

    if packed:
        grad_shapes = [sds((2, 4, 2, PACKED, LANES), BF16)]
        scratch = [pltpu.VMEM((n, PACKED - PACK[1], LANES), F32)]
    else:
        grad_shapes = [
            sds((C0, width), F32),
            sds(first_weight.shape, F32),
            sds(second_weight.shape, F32),
            sds(third_weight.shape, F32),
            sds((1, PK * C2), F32),
        ]
        scratch = []
    own_scores, after, delta, edge_projected, *grads = pl.pallas_call(
        functools.partial(head_kernel, n, packed),
        in_specs=[VMEM] * 10,
        out_specs=[VMEM] * (4 + len(grad_shapes)),
        out_shape=[
            sds((1, frames), F32),
            sds((1, LANES), F32),
            sds((frames + EDGE, C0), BF16),
            sds((EDGE, width), BF16),
            *grad_shapes,
        ],
        scratch_shapes=scratch,
        compiler_params=params(20),
        cost_estimate=cost(10**9, 4 * 10**6),
        name="head",
    )(
        squeezed,
        edge,
        cot,
        hidden,
        projection,
        squeeze,
        first,
        second,
        third,
        final,
    )

    def features_back():
        own_grad, back = pl.pallas_call(
            feature_kernel,
            in_specs=[VMEM] * 8,
            out_specs=[VMEM] * 2,
            out_shape=[sds((frames, feat), F32), sds((BACK, feat), F32)],
            compiler_params=params(8),
            cost_estimate=cost(2 * frames * width * (feat + C0), 2 * feat * width),
            name="feature",
        )(rows, edge, projected, edge_projected, delta, after, squeeze, projection)
        back = lax.ppermute(back, ("dp", "seq"), returning)
        return own_grad, back

    def assembled(own_grad, back):
        feature_grad, scores = pl.pallas_call(
            functools.partial(assemble_kernel, n),
            in_specs=[VMEM] * 3,
            out_specs=[VMEM] * 2,
            out_shape=[sds((frames, feat), F32), sds((1, frames), F32)],
            compiler_params=params(4),
            cost_estimate=cost(frames * feat, 8 * frames * feat),
            name="assemble",
        )(own_grad, own_scores, back)
        return feature_grad[None], scores

    factor = 1.0 / math.sqrt(cores * n * frames)
    if not packed:
        shares = []
        for term in grads[:4] + [grads[4].reshape(PK * C2)]:
            part = lax.psum_scatter(term * factor, "seq", scatter_dimension=0, tiled=True)
            shares.append(lax.psum(part.astype(BF16), "dp").astype(F32))
        feature_grad, scores = assembled(*features_back())
        return (scores, feature_grad, *shares)

    def added(*terms):
        total = terms[0].astype(F32)
        for term in terms[1:]:
            total = total + term.astype(F32)
        return total.astype(BF16)

    def mixed(zero, one):
        return [(i, i ^ zero) for i in range(n)] + [(n + i, n + (i ^ one)) for i in range(n)]

    swap = [(0, 1), (1, 0)]
    (payload,) = grads
    came = lax.ppermute(payload[1], "dp", swap)
    own_grad, back = features_back()
    came, own_grad = lax.optimization_barrier((came, own_grad))
    held = added(payload[0], came)
    moved = [lax.ppermute(held[j], ("dp", "seq"), mixed(j, (j >> 1) | ((j & 1) << 1))) for j in (1, 3, 2)]
    held, back = lax.optimization_barrier((added(held[0], *moved), back))
    held = added(
        lax.ppermute(held[1], ("dp", "seq"), mixed(12, 8)), lax.ppermute(held[0], ("dp", "seq"), mixed(0, 4))
    )
    feature_grad, scores = assembled(own_grad, back)
    held, feature_grad, scores = lax.optimization_barrier((held, feature_grad, scores))
    other = lax.ppermute(held, "dp", swap)
    shapes = [
        (C0 // n, width),
        (HK * C0 // n, C1),
        (HK * C1 // n, C2),
        (HK * C2 // n, C2),
        (1, PK * C2 // n),
    ]
    *shares, final = pl.pallas_call(
        functools.partial(unpack_kernel, n, factor),
        in_specs=[VMEM, VMEM],
        out_specs=[VMEM] * 5,
        out_shape=[sds(shape, F32) for shape in shapes],
        scratch_shapes=[pltpu.VMEM((PACKED, LANES), F32)],
        compiler_params=params(4),
        name="unpack",
    )(held, other)
    return (scores, feature_grad, *shares, final.reshape(PK * C2 // n))


def solution(mesh):
    placed = (P("dp", "seq", None), P("dp", "seq"), P(), P(), P(), P(), P(), P())
    return jax.shard_map(
        shards,
        mesh=mesh,
        in_specs=placed,
        out_specs=(
            P("dp", "seq"),
            P("dp", "seq", None),
            P("seq", None),
            P("seq", None),
            P("seq", None),
            P("seq", None),
            P("seq"),
        ),
        check_vma=False,
    )
```

```python
import functools
import math

import jax
import jax.numpy as jnp
from jax import lax
from jax.experimental import pallas as pl
from jax.experimental.pallas import tpu as pltpu
from jax.sharding import PartitionSpec as P

C0 = 64
C1 = 128
C2 = 256
HK = 5
PK = 3
EDGE = 32
REACH = 12
MORE = 8
BACK = 16
LANES = 128

EPSILON = 1e-05
SLOPE = 0.1
BF16 = jnp.bfloat16
F32 = jnp.float32
NT = (((1,), (1,)), ((), ()))
TN = (((0,), (0,)), ((), ()))


def normalize(values):
    average = jnp.mean(values, axis=-1, keepdims=True)
    centred = values - average
    variance = jnp.mean(centred * centred, axis=-1, keepdims=True)
    inverse = lax.rsqrt(variance + EPSILON)
    return (centred * inverse, inverse)


def normalize_back(upstream, normed, inverse):
    first_mean = jnp.mean(upstream, axis=-1, keepdims=True)
    second_mean = jnp.mean(upstream * normed, axis=-1, keepdims=True)
    return (upstream - first_mean - normed * second_mean) * inverse


def leaky_pair(values):
    cumulative = 0.5 * (1.0 + lax.erf(values * math.sqrt(0.5)))
    density = jnp.exp(-0.5 * values * values) * (1.0 / math.sqrt(2.0 * math.pi))
    unit = SLOPE * values + (1.0 - SLOPE) * (values * cumulative)
    slope = SLOPE + (1.0 - SLOPE) * (cumulative + values * density)
    return unit, slope


def dot(a, b, dims=(((1,), (0,)), ((), ()))):
    return lax.dot_general(a, b, dims, preferred_element_type=F32)


def forward_rows(rows, projection, squeeze):
    normed, _ = normalize(rows.astype(F32))
    projected = dot(normed.astype(BF16), projection).astype(BF16)
    wide = projected.astype(F32)
    average = jnp.mean(wide, axis=-1, keepdims=True)
    centred = wide - average
    inverse = lax.rsqrt(jnp.mean(centred * centred, axis=-1, keepdims=True) + EPSILON)
    sums = dot(jnp.ones((8, squeeze.shape[1]), BF16), squeeze, NT)[0:1]
    squeezed = (dot(projected, squeeze, NT) - average * sums) * inverse
    return projected, (centred * inverse).astype(BF16), squeezed


def here():
    return lax.axis_index("seq"), lax.rem(lax.axis_index("dp"), 2)


def in_parts(values):
    high = values.astype(BF16).astype(F32)
    middle = (values - high).astype(BF16).astype(F32)
    return jnp.concatenate([high, middle, values - high - middle, jnp.zeros_like(values)], axis=0)


def edge_kernel(rows_ref, cot_ref, out_ref, held, cot_held, sems):
    frames, feat = rows_ref.shape
    _, odd = here()
    start = pl.multiple_of(odd * (frames - EDGE), 16)
    copies = [
        pltpu.make_async_copy(cot_ref, cot_held, sems.at[0]),
        pltpu.make_async_copy(rows_ref.at[pl.ds(start, EDGE)], held, sems.at[1]),
    ]
    for copy in copies:
        copy.start()
    copies[0].wait()
    cot = cot_held[...]
    stack = jnp.concatenate([in_parts(cot)] * (EDGE // 4), axis=0)
    row = lax.broadcasted_iota(jnp.int32, (EDGE, frames), 0)
    carries = (row < MORE) & (odd == 1) | (row >= EDGE - MORE) & (odd == 0)
    copies[1].wait()
    out_ref[:, frames:] = held[:, frames:]
    out_ref[:, :frames] = jnp.where(carries, stack, held[:, :frames].astype(F32)).astype(BF16)


def project_kernel(count, final_ref, *refs):
    sources, held = refs[:count], refs[count : 2 * count]
    final_out, final_held = refs[-3], refs[-2]
    final_copy = pltpu.make_async_copy(final_ref, final_held, refs[-1].at[count])
    projected_ref, hidden_ref, squeezed_ref, _, _, sems = refs[2 * count :]
    copies = [pltpu.make_async_copy(a, b, sems.at[i]) for i, (a, b) in enumerate(zip(sources, held))]
    for copy in copies:
        copy.start()
    final_copy.start()
    for copy in copies[:3]:
        copy.wait()
    projected, hidden, squeezed = forward_rows(held[0][...], held[1][...], held[2][...])
    projected_ref[...] = projected
    hidden_ref[...] = hidden
    squeezed_ref[...] = squeezed
    for copy in copies[3:]:
        copy.wait()
    final_copy.wait()
    final_out[...] = final_held[...].reshape(final_out.shape)


def shifted(values, taps, sign):
    count = values.shape[0]
    pieces = []
    for k in range(taps):
        amount = (-sign * (k - (taps - 1) // 2)) % count
        moved = values if amount == 0 else pltpu.roll(values, amount, 0)
        pieces.append(moved.astype(BF16))
    return pieces


PACK = (264, 160, 0, 240, 284)
PACKED = 288


def final_rows(s, n):
    return min(s * (PK * C2 // n) // LANES, PK * C2 // LANES - 2)


def pieces_of(n, count, rows):
    found = []
    for s in range(n):
        at = s * count
        while at < (s + 1) * count:
            tap, row = divmod(at, rows)
            length = min(rows - row, (s + 1) * count - at)
            found.append((s, tap, row, at - s * count, length))
            at += length
    return found


def head_kernel(
    n,
    packed,
    squeezed_ref,
    edge_ref,
    cot_ref,
    hidden_ref,
    projection_ref,
    squeeze_ref,
    first_ref,
    second_ref,
    third_ref,
    final_ref,
    scores_ref,
    edge_scores_ref,
    delta_ref,
    edge_projected_ref,
    *outs,
):
    frames = squeezed_ref.shape[0]
    total = EDGE + frames
    seq, odd = here()
    row = lax.broadcasted_iota(jnp.int32, (total, LANES), 0)
    frame = row - jnp.where(row >= frames, odd * total, 0)
    before = jnp.where((odd == 1) & (seq > 0), REACH, 0)
    after = jnp.where((odd == 0) & (seq < n - 1), REACH, 0)
    inside = (frame >= -2 * before) & (frame < frames + 2 * after)
    first = jnp.where((odd == 0) & (seq > 0), REACH, -before)
    last = jnp.where((odd == 1) & (seq < n - 1), -REACH, after)
    window = (frame >= first) & (frame < frames + last)

    def mask(values, where):
        width = values.shape[1]
        if width <= LANES:
            return jnp.where(where[:, :width], values, 0.0)
        return jnp.concatenate(
            [jnp.where(where, values[:, i : i + LANES], 0.0) for i in range(0, width, LANES)], axis=1
        )

    edge_projected, edge_hidden, edge_squeezed = forward_rows(
        edge_ref[...], projection_ref[...], squeeze_ref[...]
    )
    edge_projected_ref[...] = edge_projected
    squeezed = jnp.concatenate([squeezed_ref[...], edge_squeezed], axis=0)

    parts = edge_ref[:, :LANES].astype(F32)
    parts = jnp.where(odd == 0, parts[EDGE - MORE :], parts[:MORE])
    parts = parts[0:1] + parts[1:2] + parts[2:3]
    columns = jnp.concatenate([cot_ref[...], parts, jnp.zeros((6, LANES), F32)], axis=0).T
    cot = jnp.concatenate(
        [
            jnp.broadcast_to(columns[:, 0:1], (frames, LANES)),
            jnp.broadcast_to(
                jnp.where(odd == 0, columns[:EDGE, 1:2], columns[frames - EDGE :, 1:2]), (EDGE, LANES)
            ),
        ],
        axis=0,
    )
    cot = mask(cot, inside)

    weights = (first_ref, second_ref, third_ref)
    act = squeezed
    inputs, slopes = [], []
    for ref in weights:
        unit, slope = leaky_pair(act)
        unit = mask(unit, inside)
        slopes.append(slope)
        inputs.append(mask(unit, window).astype(BF16))
        width = unit.shape[1]
        pieces = shifted(unit, HK, 1)
        if width % LANES == 0:
            act = dot(jnp.concatenate(pieces, axis=1), ref[...])
        else:
            act = jnp.zeros((total, ref.shape[1]), F32)
            for k, piece in enumerate(pieces):
                act = act + dot(piece, ref[k * width : (k + 1) * width, :])
    unit, slope = leaky_pair(act)
    final_in = mask(unit, inside).astype(BF16).astype(F32)
    taps = shifted(final_in, PK, 1)
    for ref, rows in ((scores_ref, slice(0, frames)), (edge_scores_ref, slice(total - LANES, total))):
        scores = jnp.zeros((1, rows.stop - rows.start), F32)
        for k in range(PK):
            scores = scores + dot(final_ref[:, k * C2 : (k + 1) * C2], taps[k][rows], NT)
        ref[...] = scores

    upstream = [jnp.zeros((total, LANES), F32)] * (C2 // LANES)
    final_grad = []
    final_in = mask(final_in, window)
    for k in range(PK):
        amount = (k - 1) % total
        moved = cot if amount == 0 else pltpu.roll(cot, amount, 0)
        for h in range(C2 // LANES):
            lanes = slice(k * C2 + h * LANES, k * C2 + (h + 1) * LANES)
            upstream[h] = upstream[h] + moved * final_ref[:, lanes].astype(F32)
            final_grad.append(
                jnp.sum(moved * final_in[:, h * LANES : (h + 1) * LANES], axis=0, keepdims=True)
            )
    upstream = jnp.concatenate(upstream, axis=1)
    slopes.append(slope)
    if packed:
        payload_ref, scratch = outs
        mine = [seq ^ s for s in range(n)]

        def block(s):
            q, z = mine[s] & 3, mine[s] >> 2
            holder = (z ^ (z >> 1)) & 1
            return holder ^ odd, jnp.where(holder == 0, q, (q >> 1) | ((q & 1) << 1)), z >> 1

    def keep(layer, tap, grad):
        channels, cols = grad.shape
        if not packed:
            outs[layer + 1][tap * channels : (tap + 1) * channels, :] = grad
            return
        count = HK * channels // n
        for s, at, start, offset, length in pieces_of(n, count, channels):
            if at != tap:
                continue
            for h in range(cols // LANES):
                piece = grad[start : start + length, h * LANES : (h + 1) * LANES]
                first_row = PACK[layer] + h * count + offset
                if layer == 2:
                    payload_ref[(*block(s), slice(first_row, first_row + length))] = piece.astype(BF16)
                else:
                    scratch[s, first_row - PACK[1] : first_row - PACK[1] + length, :] = piece

    for layer in (2, 1, 0):
        delta = mask(upstream * slopes[layer + 1], inside)
        pieces = shifted(delta, HK, -1)
        rows = inputs[layer].T
        ref = weights[layer]
        width = ref.shape[0] // HK
        upstream = jnp.zeros((total, width), F32)
        for k, piece in enumerate(pieces):
            upstream = upstream + dot(piece, ref[k * width : (k + 1) * width, :], NT)
        for k, piece in enumerate(pieces):
            keep(layer, k, dot(rows, piece))
    delta = mask(upstream * slopes[0], inside)
    delta_ref[...] = delta.astype(BF16)
    hidden = jnp.concatenate([hidden_ref[...], edge_hidden], axis=0)
    squeeze_grad = dot(mask(delta, window).astype(BF16), hidden, TN)

    if not packed:
        outs[0][...] = squeeze_grad
        for i, part in enumerate(final_grad):
            outs[4][:, i * LANES : (i + 1) * LANES] = part
        return

    count = C0 // n
    for s in range(n):
        for h in range(squeeze_grad.shape[1] // LANES):
            first_row = PACK[3] - PACK[1] + h * count
            scratch[s, first_row : first_row + count, :] = squeeze_grad[
                s * count : (s + 1) * count, h * LANES : (h + 1) * LANES
            ]
        row = final_rows(s, n)
        first_row = PACK[4] - PACK[1]
        scratch[s, first_row : first_row + 1, :] = final_grad[row]
        scratch[s, first_row + 1 : first_row + 2, :] = final_grad[row + 1]
        scratch[s, first_row + 2 :, :] = jnp.zeros((PACKED - PACK[4] - 2, LANES), F32)
        payload_ref[(*block(s), slice(PACK[1], PACKED))] = scratch[s].astype(BF16)


def feature_kernel(
    rows_ref, edge_ref, projected_ref, edge_projected_ref, delta_ref, edge_scores_ref, squeeze_ref, projection_ref, out_ref, back_ref
):
    hidden_upstream = dot(delta_ref[...], squeeze_ref[...])
    projected = jnp.concatenate([projected_ref[...], edge_projected_ref[...]], axis=0)
    hidden_normed, hidden_inverse = normalize(projected.astype(F32))
    projected_grad = normalize_back(hidden_upstream, hidden_normed, hidden_inverse).astype(BF16)
    normed_grad = dot(projected_grad, projection_ref[...], NT)
    rows = jnp.concatenate([rows_ref[...], edge_ref[...]], axis=0)
    normed, inverse = normalize(rows.astype(F32))
    grad = normalize_back(normed_grad, normed, inverse)
    out_ref[...] = grad[:-EDGE]
    gone = jnp.where(here()[1] == 0, grad[-EDGE : BACK - EDGE], grad[-BACK:])
    row = lax.broadcasted_iota(jnp.int32, (BACK, LANES), 0)
    spare = jnp.where(here()[1] == 0, row, BACK - 1 - row) >= REACH
    back_ref[:, LANES:] = gone[:, LANES:].astype(BF16)
    parts = jnp.concatenate([in_parts(edge_scores_ref[...])] * (BACK // 4), axis=0)
    back_ref[:, :LANES] = jnp.where(spare, parts, gone[:, :LANES]).astype(BF16)


def assemble_kernel(n, own_ref, scores_ref, back_ref, grad_ref, final_scores_ref):
    frames = own_ref.shape[0]
    seq, odd = here()
    low, high = (odd == 0) & (seq > 0), (odd == 1) & (seq < n - 1)
    grad_ref[BACK : frames - BACK, :] = own_ref[BACK : frames - BACK, :]
    row = lax.broadcasted_iota(jnp.int32, (BACK, own_ref.shape[1]), 0)
    came = back_ref[...].astype(F32)
    grad_ref[:BACK, :] = jnp.where(low & (row < REACH), came, own_ref[:BACK, :])
    grad_ref[frames - BACK :, :] = jnp.where(high & (row >= BACK - REACH), came, own_ref[frames - BACK :, :])
    parts = jnp.where(odd == 0, came[BACK - 4 :, :LANES], came[:4, :LANES])
    scores = jnp.broadcast_to(parts[0:1] + parts[1:2] + parts[2:3], (8, LANES))
    moved = pltpu.roll(scores, EDGE, 1)
    lane = lax.broadcasted_iota(jnp.int32, (1, frames), 1)
    kept = jnp.where(high & (lane >= frames - REACH), scores[0:1], scores_ref[...])
    final_scores_ref[...] = jnp.where(low & (lane < REACH), moved[0:1], kept)


def unpack_kernel(n, factor, mine_ref, other_ref, squeeze_ref, first_ref, second_ref, third_ref, final_ref, both):
    both[...] = (mine_ref[...].astype(F32) + other_ref[...].astype(F32)) * factor
    for base, ref in zip(PACK, (first_ref, second_ref, third_ref, squeeze_ref)):
        count = ref.shape[0]
        for h in range(ref.shape[1] // LANES):
            ref[:, h * LANES : (h + 1) * LANES] = both[base + h * count : base + (h + 1) * count, :]
    count = final_ref.shape[1]
    at = here()[0] * count
    at = at - jnp.minimum(lax.div(at, LANES), PK * C2 // LANES - 2) * LANES
    pair = jnp.concatenate([both[PACK[4] : PACK[4] + 1, :], both[PACK[4] + 1 : PACK[4] + 2, :]], axis=1)
    pair = pltpu.roll(jnp.broadcast_to(pair, (8, 2 * LANES)), 2 * LANES - at, 1)
    final_ref[...] = pair[0:1, :count]


def sds(shape, dtype):
    return jax.ShapeDtypeStruct(shape, dtype)


def hbm(array):
    return pltpu.with_memory_space_constraint(array, pltpu.HBM)


def vmem(shape, dtype):
    return pltpu.VMEM(shape, dtype)


VMEM = pl.BlockSpec(memory_space=pltpu.VMEM)
HBM = pl.BlockSpec(memory_space=pltpu.HBM)


def params(mib):
    return pltpu.CompilerParams(vmem_limit_bytes=mib * 1024 * 1024)


def cost(flops, nbytes):
    return pl.CostEstimate(flops=flops, bytes_accessed=nbytes, transcendentals=0)


def shards(
    features,
    score_cotangent,
    projection_weight,
    squeeze_weight,
    first_weight,
    second_weight,
    third_weight,
    final_weight,
):
    n, cores = lax.axis_size("seq"), lax.axis_size("dp")
    frames, feat = features.shape[1:]
    width = projection_weight.shape[1]
    packed = n == 16 and cores == 2
    rows = features.reshape(frames, feat)
    along = []
    for i in range(0, cores * n, n):
        down = [(i + j + 1, i + j) for j in range(n - 1)]
        along += down if i // n % 2 == 0 else [(target, source) for source, target in down]
    for i in range(0, (cores // 2) * 2 * n, 2 * n):
        along += [(i, i + n), (i + 2 * n - 1, i + n - 1)]
    along = sorted(along)
    returning = sorted((target, source) for source, target in along)

    edge = pl.pallas_call(
        edge_kernel,
        in_specs=[HBM, HBM],
        out_specs=VMEM,
        out_shape=vmem((EDGE, feat), BF16),
        scratch_shapes=[pltpu.VMEM((EDGE, feat), BF16), pltpu.VMEM((1, frames), F32), pltpu.SemaphoreType.DMA((2,))],
        name="edge",
    )(hbm(rows), hbm(score_cotangent))
    edge = lax.ppermute(edge, ("dp", "seq"), along)

    sources = (
        rows,
        projection_weight,
        squeeze_weight,
        score_cotangent,
        first_weight,
        second_weight,
        third_weight,
    )
    rows, projection, squeeze, cot, first, second, third, projected, hidden, squeezed, final = pl.pallas_call(
        functools.partial(project_kernel, len(sources)),
        in_specs=[HBM] * (1 + len(sources)),
        out_specs=[VMEM] * (len(sources) + 4),
        out_shape=[
            *[vmem(a.shape, a.dtype) for a in sources],
            vmem((frames, width), BF16),
            vmem((frames, width), BF16),
            vmem((frames, C0), F32),
            vmem((1, PK * C2), BF16),
        ],
        scratch_shapes=[pltpu.VMEM((PK * C2,), BF16), pltpu.SemaphoreType.DMA((len(sources) + 1,))],
        compiler_params=params(8),
        cost_estimate=cost(2 * frames * width * (feat + C0), 2 * feat * width),
        name="project",
    )(hbm(final_weight), *[hbm(a) for a in sources])

    if packed:
        grad_shapes = [sds((2, 4, 2, PACKED, LANES), BF16)]
        scratch = [pltpu.VMEM((n, PACKED - PACK[1], LANES), F32)]
    else:
        grad_shapes = [
            sds((C0, width), F32),
            sds(first_weight.shape, F32),
            sds(second_weight.shape, F32),
            sds(third_weight.shape, F32),
            sds((1, PK * C2), F32),
        ]
        scratch = []
    own_scores, after, delta, edge_projected, *grads = pl.pallas_call(
        functools.partial(head_kernel, n, packed),
        in_specs=[VMEM] * 10,
        out_specs=[VMEM] * (4 + len(grad_shapes)),
        out_shape=[
            sds((1, frames), F32),
            sds((1, LANES), F32),
            sds((frames + EDGE, C0), BF16),
            sds((EDGE, width), BF16),
            *grad_shapes,
        ],
        scratch_shapes=scratch,
        compiler_params=params(20),
        cost_estimate=cost(10**9, 4 * 10**6),
        name="head",
    )(
        squeezed,
        edge,
        cot,
        hidden,
        projection,
        squeeze,
        first,
        second,
        third,
        final,
    )

    def features_back():
        own_grad, back = pl.pallas_call(
            feature_kernel,
            in_specs=[VMEM] * 8,
            out_specs=[VMEM] * 2,
            out_shape=[sds((frames, feat), F32), sds((BACK, feat), BF16)],
            compiler_params=params(8),
            cost_estimate=cost(2 * frames * width * (feat + C0), 2 * feat * width),
            name="feature",
        )(rows, edge, projected, edge_projected, delta, after, squeeze, projection)
        back = lax.ppermute(back, ("dp", "seq"), returning)
        return own_grad, back

    def assembled(own_grad, back):
        feature_grad, scores = pl.pallas_call(
            functools.partial(assemble_kernel, n),
            in_specs=[VMEM] * 3,
            out_specs=[VMEM] * 2,
            out_shape=[sds((frames, feat), F32), sds((1, frames), F32)],
            compiler_params=params(4),
            cost_estimate=cost(frames * feat, 8 * frames * feat),
            name="assemble",
        )(own_grad, own_scores, back)
        return feature_grad[None], scores

    factor = 1.0 / math.sqrt(cores * n * frames)
    if not packed:
        shares = []
        for term in grads[:4] + [grads[4].reshape(PK * C2)]:
            part = lax.psum_scatter(term * factor, "seq", scatter_dimension=0, tiled=True)
            shares.append(lax.psum(part.astype(BF16), "dp").astype(F32))
        feature_grad, scores = assembled(*features_back())
        return (scores, feature_grad, *shares)

    def added(*terms):
        total = terms[0].astype(F32)
        for term in terms[1:]:
            total = total + term.astype(F32)
        return total.astype(BF16)

    def mixed(zero, one):
        return [(i, i ^ zero) for i in range(n)] + [(n + i, n + (i ^ one)) for i in range(n)]

    swap = [(0, 1), (1, 0)]
    (payload,) = grads
    came = lax.ppermute(payload[1], "dp", swap)
    own_grad, back = features_back()
    came, own_grad = lax.optimization_barrier((came, own_grad))
    held = [added(payload[0, j], came[j]) for j in range(4)]
    moved = [lax.ppermute(held[j], ("dp", "seq"), mixed(j, (j >> 1) | ((j & 1) << 1))) for j in (1, 3, 2)]
    held = [added(held[0][i], *(part[i] for part in moved)) for i in range(2)]
    held, back = lax.optimization_barrier((held, back))
    held = added(
        lax.ppermute(held[1], ("dp", "seq"), mixed(12, 8)), lax.ppermute(held[0], ("dp", "seq"), mixed(0, 4))
    )
    feature_grad, scores = assembled(own_grad, back)
    held, feature_grad, scores = lax.optimization_barrier((held, feature_grad, scores))
    other = lax.ppermute(held, "dp", swap)
    shapes = [
        (C0 // n, width),
        (HK * C0 // n, C1),
        (HK * C1 // n, C2),
        (HK * C2 // n, C2),
        (1, PK * C2 // n),
    ]
    *shares, final = pl.pallas_call(
        functools.partial(unpack_kernel, n, factor),
        in_specs=[VMEM, VMEM],
        out_specs=[VMEM] * 5,
        out_shape=[sds(shape, F32) for shape in shapes],
        scratch_shapes=[pltpu.VMEM((PACKED, LANES), F32)],
        compiler_params=params(4),
        name="unpack",
    )(held, other)
    return (scores, feature_grad, *shares, final.reshape(PK * C2 // n))


def solution(mesh):
    placed = (P("dp", "seq", None), P("dp", "seq"), P(), P(), P(), P(), P(), P())
    return jax.shard_map(
        shards,
        mesh=mesh,
        in_specs=placed,
        out_specs=(
            P("dp", "seq"),
            P("dp", "seq", None),
            P("seq", None),
            P("seq", None),
            P("seq", None),
            P("seq", None),
            P("seq"),
        ),
        check_vma=False,
    )
```

```python
import functools
import math

import jax
import jax.numpy as jnp
from jax import lax
from jax.experimental import pallas as pl
from jax.experimental.pallas import tpu as pltpu
from jax.sharding import PartitionSpec as P

C0 = 64
C1 = 128
C2 = 256
HK = 5
PK = 3
EDGE = 32
REACH = 12
MORE = 8
BACK = 16
LANES = 128

EPSILON = 1e-05
SLOPE = 0.1
BF16 = jnp.bfloat16
F32 = jnp.float32
NT = (((1,), (1,)), ((), ()))
TN = (((0,), (0,)), ((), ()))


def normalize(values):
    average = jnp.mean(values, axis=-1, keepdims=True)
    centred = values - average
    variance = jnp.mean(centred * centred, axis=-1, keepdims=True)
    inverse = lax.rsqrt(variance + EPSILON)
    return (centred * inverse, inverse)


def normalize_back(upstream, normed, inverse):
    first_mean = jnp.mean(upstream, axis=-1, keepdims=True)
    second_mean = jnp.mean(upstream * normed, axis=-1, keepdims=True)
    return (upstream - first_mean - normed * second_mean) * inverse


def leaky_pair(values):
    cumulative = 0.5 * (1.0 + lax.erf(values * math.sqrt(0.5)))
    density = jnp.exp(-0.5 * values * values) * (1.0 / math.sqrt(2.0 * math.pi))
    unit = SLOPE * values + (1.0 - SLOPE) * (values * cumulative)
    slope = SLOPE + (1.0 - SLOPE) * (cumulative + values * density)
    return unit, slope


def dot(a, b, dims=(((1,), (0,)), ((), ()))):
    return lax.dot_general(a, b, dims, preferred_element_type=F32)


def forward_rows(rows, projection, squeeze):
    normed, _ = normalize(rows.astype(F32))
    projected = dot(normed.astype(BF16), projection).astype(BF16)
    wide = projected.astype(F32)
    average = jnp.mean(wide, axis=-1, keepdims=True)
    centred = wide - average
    inverse = lax.rsqrt(jnp.mean(centred * centred, axis=-1, keepdims=True) + EPSILON)
    sums = dot(jnp.ones((8, squeeze.shape[1]), BF16), squeeze, NT)[0:1]
    squeezed = (dot(projected, squeeze, NT) - average * sums) * inverse
    return projected, (centred * inverse).astype(BF16), squeezed


def here():
    return lax.axis_index("seq"), lax.rem(lax.axis_index("dp"), 2)


def in_parts(values):
    high = values.astype(BF16).astype(F32)
    middle = (values - high).astype(BF16).astype(F32)
    return jnp.concatenate([high, middle, values - high - middle, jnp.zeros_like(values)], axis=0)


def edge_kernel(rows_ref, cot_ref, out_ref, held, cot_held, sems):
    frames, feat = rows_ref.shape
    _, odd = here()
    start = pl.multiple_of(odd * (frames - EDGE), 16)
    copies = [
        pltpu.make_async_copy(cot_ref, cot_held, sems.at[0]),
        pltpu.make_async_copy(rows_ref.at[pl.ds(start, EDGE)], held, sems.at[1]),
    ]
    for copy in copies:
        copy.start()
    copies[0].wait()
    cot = cot_held[...]
    stack = jnp.concatenate([in_parts(cot)] * (EDGE // 4), axis=0)
    row = lax.broadcasted_iota(jnp.int32, (EDGE, frames), 0)
    carries = (row < MORE) & (odd == 1) | (row >= EDGE - MORE) & (odd == 0)
    copies[1].wait()
    out_ref[:, frames:] = held[:, frames:]
    out_ref[:, :frames] = jnp.where(carries, stack, held[:, :frames].astype(F32)).astype(BF16)


def project_kernel(count, final_ref, *refs):
    sources, held = refs[:count], refs[count : 2 * count]
    final_out, final_held = refs[-3], refs[-2]
    final_copy = pltpu.make_async_copy(final_ref, final_held, refs[-1].at[count])
    projected_ref, hidden_ref, squeezed_ref, _, _, sems = refs[2 * count :]
    copies = [pltpu.make_async_copy(a, b, sems.at[i]) for i, (a, b) in enumerate(zip(sources, held))]
    for copy in copies:
        copy.start()
    final_copy.start()
    for copy in copies[:3]:
        copy.wait()
    projected, hidden, squeezed = forward_rows(held[0][...], held[1][...], held[2][...])
    projected_ref[...] = projected
    hidden_ref[...] = hidden
    squeezed_ref[...] = squeezed
    for copy in copies[3:]:
        copy.wait()
    final_copy.wait()
    final_out[...] = final_held[...].reshape(final_out.shape)


def shifted(values, taps, sign):
    count = values.shape[0]
    pieces = []
    for k in range(taps):
        amount = (-sign * (k - (taps - 1) // 2)) % count
        moved = values if amount == 0 else pltpu.roll(values, amount, 0)
        pieces.append(moved.astype(BF16))
    return pieces


PACK = (264, 160, 0, 240, 284)
PACKED = 288


def final_rows(s, n):
    return min(s * (PK * C2 // n) // LANES, PK * C2 // LANES - 2)


def pieces_of(n, count, rows):
    found = []
    for s in range(n):
        at = s * count
        while at < (s + 1) * count:
            tap, row = divmod(at, rows)
            length = min(rows - row, (s + 1) * count - at)
            found.append((s, tap, row, at - s * count, length))
            at += length
    return found


def head_kernel(
    n,
    packed,
    squeezed_ref,
    edge_ref,
    cot_ref,
    hidden_ref,
    projection_ref,
    squeeze_ref,
    first_ref,
    second_ref,
    third_ref,
    final_ref,
    scores_ref,
    edge_scores_ref,
    delta_ref,
    edge_projected_ref,
    *outs,
):
    frames = squeezed_ref.shape[0]
    total = EDGE + frames
    seq, odd = here()
    row = lax.broadcasted_iota(jnp.int32, (total, LANES), 0)
    frame = row - jnp.where(row >= frames, odd * total, 0)
    before = jnp.where((odd == 1) & (seq > 0), REACH, 0)
    after = jnp.where((odd == 0) & (seq < n - 1), REACH, 0)
    inside = (frame >= -2 * before) & (frame < frames + 2 * after)
    first = jnp.where((odd == 0) & (seq > 0), REACH, -before)
    last = jnp.where((odd == 1) & (seq < n - 1), -REACH, after)
    window = (frame >= first) & (frame < frames + last)

    def mask(values, where):
        width = values.shape[1]
        if width <= LANES:
            return jnp.where(where[:, :width], values, 0.0)
        return jnp.concatenate(
            [jnp.where(where, values[:, i : i + LANES], 0.0) for i in range(0, width, LANES)], axis=1
        )

    edge_projected, edge_hidden, edge_squeezed = forward_rows(
        edge_ref[...], projection_ref[...], squeeze_ref[...]
    )
    edge_projected_ref[...] = edge_projected
    squeezed = jnp.concatenate([squeezed_ref[...], edge_squeezed], axis=0)

    parts = edge_ref[:, :LANES].astype(F32)
    parts = jnp.where(odd == 0, parts[EDGE - MORE :], parts[:MORE])
    parts = parts[0:1] + parts[1:2] + parts[2:3]
    columns = jnp.concatenate([cot_ref[...], parts, jnp.zeros((6, LANES), F32)], axis=0).T
    cot = jnp.concatenate(
        [
            jnp.broadcast_to(columns[:, 0:1], (frames, LANES)),
            jnp.broadcast_to(
                jnp.where(odd == 0, columns[:EDGE, 1:2], columns[frames - EDGE :, 1:2]), (EDGE, LANES)
            ),
        ],
        axis=0,
    )
    cot = mask(cot, inside)

    weights = (first_ref, second_ref, third_ref)
    act = squeezed
    inputs, slopes = [], []
    for ref in weights:
        unit, slope = leaky_pair(act)
        unit = mask(unit, inside)
        slopes.append(slope)
        inputs.append(mask(unit, window).astype(BF16))
        width = unit.shape[1]
        pieces = shifted(unit, HK, 1)
        if width % LANES == 0:
            act = dot(jnp.concatenate(pieces, axis=1), ref[...])
        else:
            act = jnp.zeros((total, ref.shape[1]), F32)
            for k, piece in enumerate(pieces):
                act = act + dot(piece, ref[k * width : (k + 1) * width, :])
    unit, slope = leaky_pair(act)
    final_in = mask(unit, inside).astype(BF16).astype(F32)
    taps = shifted(final_in, PK, 1)
    for ref, rows in ((scores_ref, slice(0, frames)), (edge_scores_ref, slice(total - LANES, total))):
        scores = jnp.zeros((1, rows.stop - rows.start), F32)
        for k in range(PK):
            scores = scores + dot(final_ref[:, k * C2 : (k + 1) * C2], taps[k][rows], NT)
        ref[...] = scores

    upstream = [jnp.zeros((total, LANES), F32)] * (C2 // LANES)
    final_grad = []
    final_in = mask(final_in, window)
    for k in range(PK):
        amount = (k - 1) % total
        moved = cot if amount == 0 else pltpu.roll(cot, amount, 0)
        for h in range(C2 // LANES):
            lanes = slice(k * C2 + h * LANES, k * C2 + (h + 1) * LANES)
            upstream[h] = upstream[h] + moved * final_ref[:, lanes].astype(F32)
            final_grad.append(
                jnp.sum(moved * final_in[:, h * LANES : (h + 1) * LANES], axis=0, keepdims=True)
            )
    upstream = jnp.concatenate(upstream, axis=1)
    slopes.append(slope)
    if packed:
        payload_ref, scratch = outs
        mine = [seq ^ s for s in range(n)]

        def block(s):
            q, z = mine[s] & 3, mine[s] >> 2
            holder = (z ^ (z >> 1)) & 1
            return holder ^ odd, jnp.where(holder == 0, q, (q >> 1) | ((q & 1) << 1)), z >> 1

    def keep(layer, tap, grad):
        channels, cols = grad.shape
        if not packed:
            outs[layer + 1][tap * channels : (tap + 1) * channels, :] = grad
            return
        count = HK * channels // n
        for s, at, start, offset, length in pieces_of(n, count, channels):
            if at != tap:
                continue
            for h in range(cols // LANES):
                piece = grad[start : start + length, h * LANES : (h + 1) * LANES]
                first_row = PACK[layer] + h * count + offset
                if layer == 2:
                    payload_ref[(*block(s), slice(first_row, first_row + length))] = piece.astype(BF16)
                else:
                    scratch[s, first_row - PACK[1] : first_row - PACK[1] + length, :] = piece

    for layer in (2, 1, 0):
        delta = mask(upstream * slopes[layer + 1], inside)
        pieces = shifted(delta, HK, -1)
        rows = inputs[layer].T
        ref = weights[layer]
        width = ref.shape[0] // HK
        upstream = jnp.zeros((total, width), F32)
        for k, piece in enumerate(pieces):
            upstream = upstream + dot(piece, ref[k * width : (k + 1) * width, :], NT)
        for k, piece in enumerate(pieces):
            keep(layer, k, dot(rows, piece))
    delta = mask(upstream * slopes[0], inside)
    delta_ref[...] = delta.astype(BF16)
    hidden = jnp.concatenate([hidden_ref[...], edge_hidden], axis=0)
    squeeze_grad = dot(mask(delta, window).astype(BF16), hidden, TN)

    if not packed:
        outs[0][...] = squeeze_grad
        for i, part in enumerate(final_grad):
            outs[4][:, i * LANES : (i + 1) * LANES] = part
        return

    count = C0 // n
    for s in range(n):
        for h in range(squeeze_grad.shape[1] // LANES):
            first_row = PACK[3] - PACK[1] + h * count
            scratch[s, first_row : first_row + count, :] = squeeze_grad[
                s * count : (s + 1) * count, h * LANES : (h + 1) * LANES
            ]
        row = final_rows(s, n)
        first_row = PACK[4] - PACK[1]
        scratch[s, first_row : first_row + 1, :] = final_grad[row]
        scratch[s, first_row + 1 : first_row + 2, :] = final_grad[row + 1]
        scratch[s, first_row + 2 :, :] = jnp.zeros((PACKED - PACK[4] - 2, LANES), F32)
        payload_ref[(*block(s), slice(PACK[1], PACKED))] = scratch[s].astype(BF16)


def feature_kernel(
    rows_ref, edge_ref, projected_ref, edge_projected_ref, delta_ref, edge_scores_ref, squeeze_ref, projection_ref, out_ref, back_ref
):
    hidden_upstream = dot(delta_ref[...], squeeze_ref[...])
    projected = jnp.concatenate([projected_ref[...], edge_projected_ref[...]], axis=0)
    hidden_normed, hidden_inverse = normalize(projected.astype(F32))
    projected_grad = normalize_back(hidden_upstream, hidden_normed, hidden_inverse).astype(BF16)
    normed_grad = dot(projected_grad, projection_ref[...], NT)
    rows = jnp.concatenate([rows_ref[...], edge_ref[...]], axis=0)
    normed, inverse = normalize(rows.astype(F32))
    grad = normalize_back(normed_grad, normed, inverse)
    out_ref[...] = grad[:-EDGE]
    gone = jnp.where(here()[1] == 0, grad[-EDGE : BACK - EDGE], grad[-BACK:])
    row = lax.broadcasted_iota(jnp.int32, (BACK, LANES), 0)
    spare = jnp.where(here()[1] == 0, row, BACK - 1 - row) >= REACH
    back_ref[:, LANES:] = gone[:, LANES:].astype(BF16)
    parts = jnp.concatenate([in_parts(edge_scores_ref[...])] * (BACK // 4), axis=0)
    back_ref[:, :LANES] = jnp.where(spare, parts, gone[:, :LANES]).astype(BF16)


def assemble_kernel(n, own_ref, scores_ref, back_ref, grad_ref, final_scores_ref):
    frames = own_ref.shape[0]
    seq, odd = here()
    low, high = (odd == 0) & (seq > 0), (odd == 1) & (seq < n - 1)
    grad_ref[BACK : frames - BACK, :] = own_ref[BACK : frames - BACK, :]
    row = lax.broadcasted_iota(jnp.int32, (BACK, own_ref.shape[1]), 0)
    came = back_ref[...].astype(F32)
    grad_ref[:BACK, :] = jnp.where(low & (row < REACH), came, own_ref[:BACK, :])
    grad_ref[frames - BACK :, :] = jnp.where(high & (row >= BACK - REACH), came, own_ref[frames - BACK :, :])
    parts = jnp.where(odd == 0, came[BACK - 4 :, :LANES], came[:4, :LANES])
    scores = jnp.broadcast_to(parts[0:1] + parts[1:2] + parts[2:3], (8, LANES))
    moved = pltpu.roll(scores, EDGE, 1)
    lane = lax.broadcasted_iota(jnp.int32, (1, frames), 1)
    kept = jnp.where(high & (lane >= frames - REACH), scores[0:1], scores_ref[...])
    final_scores_ref[...] = jnp.where(low & (lane < REACH), moved[0:1], kept)


def unpack_kernel(n, factor, mine_ref, other_ref, squeeze_ref, first_ref, second_ref, third_ref, final_ref, both):
    both[...] = (mine_ref[...].astype(F32) + other_ref[...].astype(F32)) * factor
    for base, ref in zip(PACK, (first_ref, second_ref, third_ref, squeeze_ref)):
        count = ref.shape[0]
        for h in range(ref.shape[1] // LANES):
            ref[:, h * LANES : (h + 1) * LANES] = both[base + h * count : base + (h + 1) * count, :]
    count = final_ref.shape[1]
    at = here()[0] * count
    at = at - jnp.minimum(lax.div(at, LANES), PK * C2 // LANES - 2) * LANES
    pair = jnp.concatenate([both[PACK[4] : PACK[4] + 1, :], both[PACK[4] + 1 : PACK[4] + 2, :]], axis=1)
    pair = pltpu.roll(jnp.broadcast_to(pair, (8, 2 * LANES)), 2 * LANES - at, 1)
    final_ref[...] = pair[0:1, :count]


def sds(shape, dtype):
    return jax.ShapeDtypeStruct(shape, dtype)


def hbm(array):
    return pltpu.with_memory_space_constraint(array, pltpu.HBM)


def vmem(shape, dtype):
    return pltpu.VMEM(shape, dtype)


VMEM = pl.BlockSpec(memory_space=pltpu.VMEM)
HBM = pl.BlockSpec(memory_space=pltpu.HBM)


def params(mib):
    return pltpu.CompilerParams(vmem_limit_bytes=mib * 1024 * 1024)


def cost(flops, nbytes):
    return pl.CostEstimate(flops=flops, bytes_accessed=nbytes, transcendentals=0)


def shards(
    features,
    score_cotangent,
    projection_weight,
    squeeze_weight,
    first_weight,
    second_weight,
    third_weight,
    final_weight,
):
    n, cores = lax.axis_size("seq"), lax.axis_size("dp")
    frames, feat = features.shape[1:]
    width = projection_weight.shape[1]
    packed = n == 16 and cores == 2
    rows = features.reshape(frames, feat)
    along = []
    for i in range(0, cores * n, n):
        down = [(i + j + 1, i + j) for j in range(n - 1)]
        along += down if i // n % 2 == 0 else [(target, source) for source, target in down]
    for i in range(0, (cores // 2) * 2 * n, 2 * n):
        along += [(i, i + n), (i + 2 * n - 1, i + n - 1)]
    along = sorted(along)
    returning = sorted((target, source) for source, target in along)

    edge = pl.pallas_call(
        edge_kernel,
        in_specs=[HBM, HBM],
        out_specs=VMEM,
        out_shape=vmem((EDGE, feat), BF16),
        scratch_shapes=[pltpu.VMEM((EDGE, feat), BF16), pltpu.VMEM((1, frames), F32), pltpu.SemaphoreType.DMA((2,))],
        name="edge",
    )(hbm(rows), hbm(score_cotangent))
    edge = lax.ppermute(edge, ("dp", "seq"), along)

    sources = (
        rows,
        projection_weight,
        squeeze_weight,
        score_cotangent,
        first_weight,
        second_weight,
        third_weight,
    )
    rows, projection, squeeze, cot, first, second, third, projected, hidden, squeezed, final = pl.pallas_call(
        functools.partial(project_kernel, len(sources)),
        in_specs=[HBM] * (1 + len(sources)),
        out_specs=[VMEM] * (len(sources) + 4),
        out_shape=[
            *[vmem(a.shape, a.dtype) for a in sources],
            vmem((frames, width), BF16),
            vmem((frames, width), BF16),
            vmem((frames, C0), F32),
            vmem((1, PK * C2), BF16),
        ],
        scratch_shapes=[pltpu.VMEM((PK * C2,), BF16), pltpu.SemaphoreType.DMA((len(sources) + 1,))],
        compiler_params=params(8),
        cost_estimate=cost(2 * frames * width * (feat + C0), 2 * feat * width),
        name="project",
    )(hbm(final_weight), *[hbm(a) for a in sources])

    if packed:
        grad_shapes = [sds((2, 4, 2, PACKED, LANES), BF16)]
        scratch = [pltpu.VMEM((n, PACKED - PACK[1], LANES), F32)]
    else:
        grad_shapes = [
            sds((C0, width), F32),
            sds(first_weight.shape, F32),
            sds(second_weight.shape, F32),
            sds(third_weight.shape, F32),
            sds((1, PK * C2), F32),
        ]
        scratch = []
    own_scores, after, delta, edge_projected, *grads = pl.pallas_call(
        functools.partial(head_kernel, n, packed),
        in_specs=[VMEM] * 10,
        out_specs=[VMEM] * (4 + len(grad_shapes)),
        out_shape=[
            sds((1, frames), F32),
            sds((1, LANES), F32),
            sds((frames + EDGE, C0), BF16),
            sds((EDGE, width), BF16),
            *grad_shapes,
        ],
        scratch_shapes=scratch,
        compiler_params=params(20),
        cost_estimate=cost(10**9, 4 * 10**6),
        name="head",
    )(
        squeezed,
        edge,
        cot,
        hidden,
        projection,
        squeeze,
        first,
        second,
        third,
        final,
    )

    def features_back():
        own_grad, back = pl.pallas_call(
            feature_kernel,
            in_specs=[VMEM] * 8,
            out_specs=[VMEM] * 2,
            out_shape=[sds((frames, feat), F32), sds((BACK, feat), BF16)],
            compiler_params=params(8),
            cost_estimate=cost(2 * frames * width * (feat + C0), 2 * feat * width),
            name="feature",
        )(rows, edge, projected, edge_projected, delta, after, squeeze, projection)
        back = lax.ppermute(back, ("dp", "seq"), returning)
        return own_grad, back

    def assembled(own_grad, back):
        feature_grad, scores = pl.pallas_call(
            functools.partial(assemble_kernel, n),
            in_specs=[VMEM] * 3,
            out_specs=[VMEM] * 2,
            out_shape=[sds((frames, feat), F32), sds((1, frames), F32)],
            compiler_params=params(4),
            cost_estimate=cost(frames * feat, 8 * frames * feat),
            name="assemble",
        )(own_grad, own_scores, back)
        return feature_grad[None], scores

    factor = 1.0 / math.sqrt(cores * n * frames)
    if not packed:
        shares = []
        for term in grads[:4] + [grads[4].reshape(PK * C2)]:
            part = lax.psum_scatter(term * factor, "seq", scatter_dimension=0, tiled=True)
            shares.append(lax.psum(part.astype(BF16), "dp").astype(F32))
        feature_grad, scores = assembled(*features_back())
        return (scores, feature_grad, *shares)

    def added(*terms):
        total = terms[0].astype(F32)
        for term in terms[1:]:
            total = total + term.astype(F32)
        return total.astype(BF16)

    def mixed(zero, one):
        return [(i, i ^ zero) for i in range(n)] + [(n + i, n + (i ^ one)) for i in range(n)]

    swap = [(0, 1), (1, 0)]
    (payload,) = grads
    came = lax.ppermute(payload[1], "dp", swap)
    own_grad, back = features_back()
    held = [added(payload[0, j], came[j]) for j in range(4)]
    moved = [lax.ppermute(held[j], ("dp", "seq"), mixed(j, (j >> 1) | ((j & 1) << 1))) for j in (1, 3, 2)]
    held = [added(held[0][i], *(part[i] for part in moved)) for i in range(2)]
    held, back, own_grad = lax.optimization_barrier((held, back, own_grad))
    held = added(
        lax.ppermute(held[1], ("dp", "seq"), mixed(12, 8)), lax.ppermute(held[0], ("dp", "seq"), mixed(0, 4))
    )
    feature_grad, scores = assembled(own_grad, back)
    held, feature_grad, scores = lax.optimization_barrier((held, feature_grad, scores))
    other = lax.ppermute(held, "dp", swap)
    shapes = [
        (C0 // n, width),
        (HK * C0 // n, C1),
        (HK * C1 // n, C2),
        (HK * C2 // n, C2),
        (1, PK * C2 // n),
    ]
    *shares, final = pl.pallas_call(
        functools.partial(unpack_kernel, n, factor),
        in_specs=[VMEM, VMEM],
        out_specs=[VMEM] * 5,
        out_shape=[sds(shape, F32) for shape in shapes],
        scratch_shapes=[pltpu.VMEM((PACKED, LANES), F32)],
        compiler_params=params(4),
        name="unpack",
    )(held, other)
    return (scores, feature_grad, *shares, final.reshape(PK * C2 // n))


def solution(mesh):
    placed = (P("dp", "seq", None), P("dp", "seq"), P(), P(), P(), P(), P(), P())
    return jax.shard_map(
        shards,
        mesh=mesh,
        in_specs=placed,
        out_specs=(
            P("dp", "seq"),
            P("dp", "seq", None),
            P("seq", None),
            P("seq", None),
            P("seq", None),
            P("seq", None),
            P("seq"),
        ),
        check_vma=False,
    )
```

```python
import functools
import math

import jax
import jax.numpy as jnp
from jax import lax
from jax.experimental import pallas as pl
from jax.experimental.pallas import tpu as pltpu
from jax.sharding import PartitionSpec as P

C0 = 64
C1 = 128
C2 = 256
HK = 5
PK = 3
EDGE = 32
REACH = 12
MORE = 8
BACK = 16
LANES = 128

EPSILON = 1e-05
SLOPE = 0.1
BF16 = jnp.bfloat16
F32 = jnp.float32
NT = (((1,), (1,)), ((), ()))
TN = (((0,), (0,)), ((), ()))


def normalize(values):
    average = jnp.mean(values, axis=-1, keepdims=True)
    centred = values - average
    variance = jnp.mean(centred * centred, axis=-1, keepdims=True)
    inverse = lax.rsqrt(variance + EPSILON)
    return (centred * inverse, inverse)


def normalize_back(upstream, normed, inverse):
    first_mean = jnp.mean(upstream, axis=-1, keepdims=True)
    second_mean = jnp.mean(upstream * normed, axis=-1, keepdims=True)
    return (upstream - first_mean - normed * second_mean) * inverse


def leaky_pair(values):
    cumulative = 0.5 * (1.0 + lax.erf(values * math.sqrt(0.5)))
    density = jnp.exp(-0.5 * values * values) * (1.0 / math.sqrt(2.0 * math.pi))
    unit = SLOPE * values + (1.0 - SLOPE) * (values * cumulative)
    slope = SLOPE + (1.0 - SLOPE) * (cumulative + values * density)
    return unit, slope


def dot(a, b, dims=(((1,), (0,)), ((), ()))):
    return lax.dot_general(a, b, dims, preferred_element_type=F32)


def forward_rows(rows, projection, squeeze, sums):
    normed, _ = normalize(rows.astype(F32))
    projected = dot(normed.astype(BF16), projection).astype(BF16)
    wide = projected.astype(F32)
    average = jnp.mean(wide, axis=-1, keepdims=True)
    centred = wide - average
    inverse = lax.rsqrt(jnp.mean(centred * centred, axis=-1, keepdims=True) + EPSILON)
    squeezed = (dot(projected, squeeze, NT) - average * sums) * inverse
    return projected, (centred * inverse).astype(BF16), squeezed


def here():
    return lax.axis_index("seq"), lax.rem(lax.axis_index("dp"), 2)


def in_parts(values):
    high = values.astype(BF16).astype(F32)
    middle = (values - high).astype(BF16).astype(F32)
    return jnp.concatenate([high, middle, values - high - middle, jnp.zeros_like(values)], axis=0)


def edge_kernel(rows_ref, cot_ref, out_ref, held, cot_held, sems):
    frames, feat = rows_ref.shape
    _, odd = here()
    start = pl.multiple_of(odd * (frames - EDGE), 16)
    copies = [
        pltpu.make_async_copy(cot_ref, cot_held, sems.at[0]),
        pltpu.make_async_copy(rows_ref.at[pl.ds(start, EDGE)], held, sems.at[1]),
    ]
    for copy in copies:
        copy.start()
    copies[0].wait()
    cot = cot_held[...]
    stack = jnp.concatenate([in_parts(cot)] * (EDGE // 4), axis=0)
    row = lax.broadcasted_iota(jnp.int32, (EDGE, frames), 0)
    carries = (row < MORE) & (odd == 1) | (row >= EDGE - MORE) & (odd == 0)
    copies[1].wait()
    out_ref[:, frames:] = held[:, frames:]
    out_ref[:, :frames] = jnp.where(carries, stack, held[:, :frames].astype(F32)).astype(BF16)


def project_kernel(count, final_ref, *refs):
    sources, held = refs[:count], refs[count : 2 * count]
    final_out, final_held = refs[-3], refs[-2]
    final_copy = pltpu.make_async_copy(final_ref, final_held, refs[-1].at[count])
    projected_ref, hidden_ref, squeezed_ref, sums_ref, _, _, sems = refs[2 * count :]
    copies = [pltpu.make_async_copy(a, b, sems.at[i]) for i, (a, b) in enumerate(zip(sources, held))]
    for copy in copies:
        copy.start()
    final_copy.start()
    for copy in copies[:3]:
        copy.wait()
    sums = dot(jnp.ones((8, held[2].shape[1]), BF16), held[2][...], NT)
    sums_ref[...] = sums
    projected, hidden, squeezed = forward_rows(held[0][...], held[1][...], held[2][...], sums[0:1])
    projected_ref[...] = projected
    hidden_ref[...] = hidden
    squeezed_ref[...] = squeezed
    for copy in copies[3:]:
        copy.wait()
    final_copy.wait()
    final_out[...] = final_held[...].reshape(final_out.shape)


def shifted(values, taps, sign):
    count = values.shape[0]
    pieces = []
    for k in range(taps):
        amount = (-sign * (k - (taps - 1) // 2)) % count
        moved = values if amount == 0 else pltpu.roll(values, amount, 0)
        pieces.append(moved.astype(BF16))
    return pieces


PACK = (264, 160, 0, 240, 284)
PACKED = 288


def final_rows(s, n):
    return min(s * (PK * C2 // n) // LANES, PK * C2 // LANES - 2)


def pieces_of(n, count, rows):
    found = []
    for s in range(n):
        at = s * count
        while at < (s + 1) * count:
            tap, row = divmod(at, rows)
            length = min(rows - row, (s + 1) * count - at)
            found.append((s, tap, row, at - s * count, length))
            at += length
    return found


def head_kernel(
    n,
    packed,
    squeezed_ref,
    sums_ref,
    edge_ref,
    cot_ref,
    hidden_ref,
    projection_ref,
    squeeze_ref,
    first_ref,
    second_ref,
    third_ref,
    final_ref,
    scores_ref,
    edge_scores_ref,
    delta_ref,
    edge_projected_ref,
    *outs,
):
    frames = squeezed_ref.shape[0]
    total = EDGE + frames
    seq, odd = here()
    row = lax.broadcasted_iota(jnp.int32, (total, LANES), 0)
    frame = row - jnp.where(row >= frames, odd * total, 0)
    before = jnp.where((odd == 1) & (seq > 0), REACH, 0)
    after = jnp.where((odd == 0) & (seq < n - 1), REACH, 0)
    inside = (frame >= -2 * before) & (frame < frames + 2 * after)
    first = jnp.where((odd == 0) & (seq > 0), REACH, -before)
    last = jnp.where((odd == 1) & (seq < n - 1), -REACH, after)
    window = (frame >= first) & (frame < frames + last)

    def mask(values, where):
        width = values.shape[1]
        if width <= LANES:
            return jnp.where(where[:, :width], values, 0.0)
        return jnp.concatenate(
            [jnp.where(where, values[:, i : i + LANES], 0.0) for i in range(0, width, LANES)], axis=1
        )

    edge_projected, edge_hidden, edge_squeezed = forward_rows(
        edge_ref[...], projection_ref[...], squeeze_ref[...], sums_ref[0:1, :]
    )
    edge_projected_ref[...] = edge_projected
    squeezed = jnp.concatenate([squeezed_ref[...], edge_squeezed], axis=0)

    parts = edge_ref[:, :LANES].astype(F32)
    parts = jnp.where(odd == 0, parts[EDGE - MORE :], parts[:MORE])
    parts = parts[0:1] + parts[1:2] + parts[2:3]
    columns = jnp.concatenate([cot_ref[...], parts, jnp.zeros((6, LANES), F32)], axis=0).T
    cot = jnp.concatenate(
        [
            jnp.broadcast_to(columns[:, 0:1], (frames, LANES)),
            jnp.broadcast_to(
                jnp.where(odd == 0, columns[:EDGE, 1:2], columns[frames - EDGE :, 1:2]), (EDGE, LANES)
            ),
        ],
        axis=0,
    )
    cot = mask(cot, inside)

    weights = (first_ref, second_ref, third_ref)
    act = squeezed
    inputs, slopes = [], []
    for ref in weights:
        unit, slope = leaky_pair(act)
        unit = mask(unit, inside)
        slopes.append(slope)
        inputs.append(mask(unit, window).astype(BF16))
        width = unit.shape[1]
        pieces = shifted(unit, HK, 1)
        if width % LANES == 0:
            act = dot(jnp.concatenate(pieces, axis=1), ref[...])
        else:
            act = jnp.zeros((total, ref.shape[1]), F32)
            for k, piece in enumerate(pieces):
                act = act + dot(piece, ref[k * width : (k + 1) * width, :])
    unit, slope = leaky_pair(act)
    final_in = mask(unit, inside).astype(BF16).astype(F32)
    taps = shifted(final_in, PK, 1)
    for ref, rows in ((scores_ref, slice(0, frames)), (edge_scores_ref, slice(total - LANES, total))):
        scores = jnp.zeros((1, rows.stop - rows.start), F32)
        for k in range(PK):
            scores = scores + dot(final_ref[:, k * C2 : (k + 1) * C2], taps[k][rows], NT)
        ref[...] = scores

    upstream = [jnp.zeros((total, LANES), F32)] * (C2 // LANES)
    final_grad = []
    final_in = mask(final_in, window)
    for k in range(PK):
        amount = (k - 1) % total
        moved = cot if amount == 0 else pltpu.roll(cot, amount, 0)
        for h in range(C2 // LANES):
            lanes = slice(k * C2 + h * LANES, k * C2 + (h + 1) * LANES)
            upstream[h] = upstream[h] + moved * final_ref[:, lanes].astype(F32)
            final_grad.append(
                jnp.sum(moved * final_in[:, h * LANES : (h + 1) * LANES], axis=0, keepdims=True)
            )
    upstream = jnp.concatenate(upstream, axis=1)
    slopes.append(slope)
    if packed:
        payload_ref, scratch = outs
        mine = [seq ^ s for s in range(n)]

        def block(s):
            q, z = mine[s] & 3, mine[s] >> 2
            holder = (z ^ (z >> 1)) & 1
            return holder ^ odd, jnp.where(holder == 0, q, (q >> 1) | ((q & 1) << 1)), z >> 1

    def keep(layer, tap, grad):
        channels, cols = grad.shape
        if not packed:
            outs[layer + 1][tap * channels : (tap + 1) * channels, :] = grad
            return
        count = HK * channels // n
        for s, at, start, offset, length in pieces_of(n, count, channels):
            if at != tap:
                continue
            for h in range(cols // LANES):
                piece = grad[start : start + length, h * LANES : (h + 1) * LANES]
                first_row = PACK[layer] + h * count + offset
                if layer == 2:
                    payload_ref[(*block(s), slice(first_row, first_row + length))] = piece.astype(BF16)
                else:
                    scratch[s, first_row - PACK[1] : first_row - PACK[1] + length, :] = piece

    for layer in (2, 1, 0):
        delta = mask(upstream * slopes[layer + 1], inside)
        pieces = shifted(delta, HK, -1)
        rows = inputs[layer].T
        ref = weights[layer]
        width = ref.shape[0] // HK
        whole = jnp.concatenate([ref[k * width : (k + 1) * width, :] for k in range(HK)], axis=1)
        upstream = dot(jnp.concatenate(pieces, axis=1), whole, NT)
        for k, piece in enumerate(pieces):
            keep(layer, k, dot(rows, piece))
    delta = mask(upstream * slopes[0], inside)
    delta_ref[...] = delta.astype(BF16)
    hidden = jnp.concatenate([hidden_ref[...], edge_hidden], axis=0)
    squeeze_grad = dot(mask(delta, window).astype(BF16), hidden, TN)

    if not packed:
        outs[0][...] = squeeze_grad
        for i, part in enumerate(final_grad):
            outs[4][:, i * LANES : (i + 1) * LANES] = part
        return

    count = C0 // n
    for s in range(n):
        for h in range(squeeze_grad.shape[1] // LANES):
            first_row = PACK[3] - PACK[1] + h * count
            scratch[s, first_row : first_row + count, :] = squeeze_grad[
                s * count : (s + 1) * count, h * LANES : (h + 1) * LANES
            ]
        row = final_rows(s, n)
        first_row = PACK[4] - PACK[1]
        scratch[s, first_row : first_row + 1, :] = final_grad[row]
        scratch[s, first_row + 1 : first_row + 2, :] = final_grad[row + 1]
        scratch[s, first_row + 2 :, :] = jnp.zeros((PACKED - PACK[4] - 2, LANES), F32)
        payload_ref[(*block(s), slice(PACK[1], PACKED))] = scratch[s].astype(BF16)


def feature_kernel(
    rows_ref, edge_ref, projected_ref, edge_projected_ref, delta_ref, edge_scores_ref, squeeze_ref, projection_ref, out_ref, back_ref
):
    hidden_upstream = dot(delta_ref[...], squeeze_ref[...])
    projected = jnp.concatenate([projected_ref[...], edge_projected_ref[...]], axis=0)
    hidden_normed, hidden_inverse = normalize(projected.astype(F32))
    projected_grad = normalize_back(hidden_upstream, hidden_normed, hidden_inverse).astype(BF16)
    normed_grad = dot(projected_grad, projection_ref[...], NT)
    rows = jnp.concatenate([rows_ref[...], edge_ref[...]], axis=0)
    normed, inverse = normalize(rows.astype(F32))
    grad = normalize_back(normed_grad, normed, inverse)
    out_ref[...] = grad[:-EDGE]
    gone = jnp.where(here()[1] == 0, grad[-EDGE : BACK - EDGE], grad[-BACK:])
    row = lax.broadcasted_iota(jnp.int32, (BACK, LANES), 0)
    spare = jnp.where(here()[1] == 0, row, BACK - 1 - row) >= REACH
    back_ref[:, LANES:] = gone[:, LANES:].astype(BF16)
    parts = jnp.concatenate([in_parts(edge_scores_ref[...])] * (BACK // 4), axis=0)
    back_ref[:, :LANES] = jnp.where(spare, parts, gone[:, :LANES]).astype(BF16)


def assemble_kernel(n, own_ref, scores_ref, back_ref, grad_ref, final_scores_ref):
    frames = own_ref.shape[0]
    seq, odd = here()
    low, high = (odd == 0) & (seq > 0), (odd == 1) & (seq < n - 1)
    grad_ref[BACK : frames - BACK, :] = own_ref[BACK : frames - BACK, :]
    row = lax.broadcasted_iota(jnp.int32, (BACK, own_ref.shape[1]), 0)
    came = back_ref[...].astype(F32)
    grad_ref[:BACK, :] = jnp.where(low & (row < REACH), came, own_ref[:BACK, :])
    grad_ref[frames - BACK :, :] = jnp.where(high & (row >= BACK - REACH), came, own_ref[frames - BACK :, :])
    parts = jnp.where(odd == 0, came[BACK - 4 :, :LANES], came[:4, :LANES])
    scores = jnp.broadcast_to(parts[0:1] + parts[1:2] + parts[2:3], (8, LANES))
    moved = pltpu.roll(scores, EDGE, 1)
    lane = lax.broadcasted_iota(jnp.int32, (1, frames), 1)
    kept = jnp.where(high & (lane >= frames - REACH), scores[0:1], scores_ref[...])
    final_scores_ref[...] = jnp.where(low & (lane < REACH), moved[0:1], kept)


def unpack_kernel(n, factor, mine_ref, other_ref, squeeze_ref, first_ref, second_ref, third_ref, final_ref, both):
    both[...] = (mine_ref[...].astype(F32) + other_ref[...].astype(F32)) * factor
    for base, ref in zip(PACK, (first_ref, second_ref, third_ref, squeeze_ref)):
        count = ref.shape[0]
        for h in range(ref.shape[1] // LANES):
            ref[:, h * LANES : (h + 1) * LANES] = both[base + h * count : base + (h + 1) * count, :]
    count = final_ref.shape[1]
    at = here()[0] * count
    at = at - jnp.minimum(lax.div(at, LANES), PK * C2 // LANES - 2) * LANES
    pair = jnp.concatenate([both[PACK[4] : PACK[4] + 1, :], both[PACK[4] + 1 : PACK[4] + 2, :]], axis=1)
    pair = pltpu.roll(jnp.broadcast_to(pair, (8, 2 * LANES)), lax.rem(2 * LANES - at, 2 * LANES), 1)
    final_ref[...] = pair[0:1, :count]


def sds(shape, dtype):
    return jax.ShapeDtypeStruct(shape, dtype)


def hbm(array):
    return pltpu.with_memory_space_constraint(array, pltpu.HBM)


def vmem(shape, dtype):
    return pltpu.VMEM(shape, dtype)


VMEM = pl.BlockSpec(memory_space=pltpu.VMEM)
HBM = pl.BlockSpec(memory_space=pltpu.HBM)


def params(mib):
    return pltpu.CompilerParams(vmem_limit_bytes=mib * 1024 * 1024)


def cost(flops, nbytes):
    return pl.CostEstimate(flops=flops, bytes_accessed=nbytes, transcendentals=0)


def shards(
    features,
    score_cotangent,
    projection_weight,
    squeeze_weight,
    first_weight,
    second_weight,
    third_weight,
    final_weight,
):
    n, cores = lax.axis_size("seq"), lax.axis_size("dp")
    frames, feat = features.shape[1:]
    width = projection_weight.shape[1]
    packed = n == 16 and cores == 2
    rows = features.reshape(frames, feat)
    along = []
    for i in range(0, cores * n, n):
        down = [(i + j + 1, i + j) for j in range(n - 1)]
        along += down if i // n % 2 == 0 else [(target, source) for source, target in down]
    for i in range(0, (cores // 2) * 2 * n, 2 * n):
        along += [(i, i + n), (i + 2 * n - 1, i + n - 1)]
    along = sorted(along)
    returning = sorted((target, source) for source, target in along)

    edge = pl.pallas_call(
        edge_kernel,
        in_specs=[HBM, HBM],
        out_specs=VMEM,
        out_shape=vmem((EDGE, feat), BF16),
        scratch_shapes=[pltpu.VMEM((EDGE, feat), BF16), pltpu.VMEM((1, frames), F32), pltpu.SemaphoreType.DMA((2,))],
        name="edge",
    )(hbm(rows), hbm(score_cotangent))
    edge = lax.ppermute(edge, ("dp", "seq"), along)

    sources = (
        rows,
        projection_weight,
        squeeze_weight,
        score_cotangent,
        first_weight,
        second_weight,
        third_weight,
    )
    rows, projection, squeeze, cot, first, second, third, projected, hidden, squeezed, sums, final = pl.pallas_call(
        functools.partial(project_kernel, len(sources)),
        in_specs=[HBM] * (1 + len(sources)),
        out_specs=[VMEM] * (len(sources) + 5),
        out_shape=[
            *[vmem(a.shape, a.dtype) for a in sources],
            vmem((frames, width), BF16),
            vmem((frames, width), BF16),
            vmem((frames, C0), F32),
            vmem((8, C0), F32),
            vmem((1, PK * C2), BF16),
        ],
        scratch_shapes=[pltpu.VMEM((PK * C2,), BF16), pltpu.SemaphoreType.DMA((len(sources) + 1,))],
        compiler_params=params(8),
        cost_estimate=cost(2 * frames * width * (feat + C0), 2 * feat * width),
        name="project",
    )(hbm(final_weight), *[hbm(a) for a in sources])

    if packed:
        grad_shapes = [sds((2, 4, 2, PACKED, LANES), BF16)]
        scratch = [pltpu.VMEM((n, PACKED - PACK[1], LANES), F32)]
    else:
        grad_shapes = [
            sds((C0, width), F32),
            sds(first_weight.shape, F32),
            sds(second_weight.shape, F32),
            sds(third_weight.shape, F32),
            sds((1, PK * C2), F32),
        ]
        scratch = []
    own_scores, after, delta, edge_projected, *grads = pl.pallas_call(
        functools.partial(head_kernel, n, packed),
        in_specs=[VMEM] * 11,
        out_specs=[VMEM] * (4 + len(grad_shapes)),
        out_shape=[
            sds((1, frames), F32),
            sds((1, LANES), F32),
            sds((frames + EDGE, C0), BF16),
            sds((EDGE, width), BF16),
            *grad_shapes,
        ],
        scratch_shapes=scratch,
        compiler_params=params(20),
        cost_estimate=cost(10**9, 4 * 10**6),
        name="head",
    )(
        squeezed,
        sums,
        edge,
        cot,
        hidden,
        projection,
        squeeze,
        first,
        second,
        third,
        final,
    )

    def features_back():
        own_grad, back = pl.pallas_call(
            feature_kernel,
            in_specs=[VMEM] * 8,
            out_specs=[VMEM] * 2,
            out_shape=[sds((frames, feat), F32), sds((BACK, feat), BF16)],
            compiler_params=params(8),
            cost_estimate=cost(2 * frames * width * (feat + C0), 2 * feat * width),
            name="feature",
        )(rows, edge, projected, edge_projected, delta, after, squeeze, projection)
        back = lax.ppermute(back, ("dp", "seq"), returning)
        return own_grad, back

    def assembled(own_grad, back):
        feature_grad, scores = pl.pallas_call(
            functools.partial(assemble_kernel, n),
            in_specs=[VMEM] * 3,
            out_specs=[VMEM] * 2,
            out_shape=[sds((frames, feat), F32), sds((1, frames), F32)],
            compiler_params=params(4),
            cost_estimate=cost(frames * feat, 8 * frames * feat),
            name="assemble",
        )(own_grad, own_scores, back)
        return feature_grad[None], scores

    factor = 1.0 / math.sqrt(cores * n * frames)
    if not packed:
        shares = []
        for term in grads[:4] + [grads[4].reshape(PK * C2)]:
            part = lax.psum_scatter(term * factor, "seq", scatter_dimension=0, tiled=True)
            shares.append(lax.psum(part.astype(BF16), "dp").astype(F32))
        feature_grad, scores = assembled(*features_back())
        return (scores, feature_grad, *shares)

    def added(*terms):
        total = terms[0].astype(F32)
        for term in terms[1:]:
            total = total + term.astype(F32)
        return total.astype(BF16)

    def mixed(zero, one):
        return [(i, i ^ zero) for i in range(n)] + [(n + i, n + (i ^ one)) for i in range(n)]

    swap = [(0, 1), (1, 0)]
    (payload,) = grads
    came = lax.ppermute(payload[1], "dp", swap)
    own_grad, back = features_back()
    held = [added(payload[0, j], came[j]) for j in range(4)]
    moved = [lax.ppermute(held[j], ("dp", "seq"), mixed(j, (j >> 1) | ((j & 1) << 1))) for j in (1, 3, 2)]
    held = [added(held[0][i], *(part[i] for part in moved)) for i in range(2)]
    held, back, own_grad = lax.optimization_barrier((held, back, own_grad))
    held = added(
        lax.ppermute(held[1], ("dp", "seq"), mixed(12, 8)), lax.ppermute(held[0], ("dp", "seq"), mixed(0, 4))
    )
    feature_grad, scores = assembled(own_grad, back)
    held, feature_grad, scores = lax.optimization_barrier((held, feature_grad, scores))
    other = lax.ppermute(held, "dp", swap)
    shapes = [
        (C0 // n, width),
        (HK * C0 // n, C1),
        (HK * C1 // n, C2),
        (HK * C2 // n, C2),
        (1, PK * C2 // n),
    ]
    *shares, final = pl.pallas_call(
        functools.partial(unpack_kernel, n, factor),
        in_specs=[VMEM, VMEM],
        out_specs=[VMEM] * 5,
        out_shape=[sds(shape, F32) for shape in shapes],
        scratch_shapes=[pltpu.VMEM((PACKED, LANES), F32)],
        compiler_params=params(4),
        name="unpack",
    )(held, other)
    return (scores, feature_grad, *shares, final.reshape(PK * C2 // n))


def solution(mesh):
    placed = (P("dp", "seq", None), P("dp", "seq"), P(), P(), P(), P(), P(), P())
    return jax.shard_map(
        shards,
        mesh=mesh,
        in_specs=placed,
        out_specs=(
            P("dp", "seq"),
            P("dp", "seq", None),
            P("seq", None),
            P("seq", None),
            P("seq", None),
            P("seq", None),
            P("seq"),
        ),
        check_vma=False,
    )
```

```python
import functools
import math

import jax
import jax.numpy as jnp
from jax import lax
from jax.experimental import pallas as pl
from jax.experimental.pallas import tpu as pltpu
from jax.sharding import PartitionSpec as P

C0 = 64
C1 = 128
C2 = 256
HK = 5
PK = 3
EDGE = 32
REACH = 12
MORE = 8
BACK = 16
LANES = 128

EPSILON = 1e-05
SLOPE = 0.1
BF16 = jnp.bfloat16
F32 = jnp.float32
NT = (((1,), (1,)), ((), ()))
TN = (((0,), (0,)), ((), ()))


def normalize(values):
    average = jnp.mean(values, axis=-1, keepdims=True)
    centred = values - average
    variance = jnp.mean(centred * centred, axis=-1, keepdims=True)
    inverse = lax.rsqrt(variance + EPSILON)
    return (centred * inverse, inverse)


def normalize_back(upstream, normed, inverse):
    first_mean = jnp.mean(upstream, axis=-1, keepdims=True)
    second_mean = jnp.mean(upstream * normed, axis=-1, keepdims=True)
    return (upstream - first_mean - normed * second_mean) * inverse


def leaky_pair(values):
    cumulative = 0.5 * (1.0 + lax.erf(values * math.sqrt(0.5)))
    density = jnp.exp(-0.5 * values * values) * (1.0 / math.sqrt(2.0 * math.pi))
    unit = SLOPE * values + (1.0 - SLOPE) * (values * cumulative)
    slope = SLOPE + (1.0 - SLOPE) * (cumulative + values * density)
    return unit, slope


def dot(a, b, dims=(((1,), (0,)), ((), ()))):
    return lax.dot_general(a, b, dims, preferred_element_type=F32)


def forward_rows(rows, projection, squeeze, sums):
    normed, _ = normalize(rows.astype(F32))
    projected = dot(normed.astype(BF16), projection).astype(BF16)
    wide = projected.astype(F32)
    average = jnp.mean(wide, axis=-1, keepdims=True)
    centred = wide - average
    inverse = lax.rsqrt(jnp.mean(centred * centred, axis=-1, keepdims=True) + EPSILON)
    squeezed = (dot(projected, squeeze, NT) - average * sums) * inverse
    return projected, (centred * inverse).astype(BF16), squeezed


def here():
    return lax.axis_index("seq"), lax.rem(lax.axis_index("dp"), 2)


def in_parts(values):
    high = values.astype(BF16).astype(F32)
    middle = (values - high).astype(BF16).astype(F32)
    return jnp.concatenate([high, middle, values - high - middle, jnp.zeros_like(values)], axis=0)


def edge_kernel(rows_ref, cot_ref, out_ref, held, cot_held, sems):
    frames, feat = rows_ref.shape
    _, odd = here()
    start = pl.multiple_of(odd * (frames - EDGE), 16)
    copies = [
        pltpu.make_async_copy(cot_ref, cot_held, sems.at[0]),
        pltpu.make_async_copy(rows_ref.at[pl.ds(start, EDGE)], held, sems.at[1]),
    ]
    for copy in copies:
        copy.start()
    copies[0].wait()
    cot = cot_held[...]
    stack = jnp.concatenate([in_parts(cot)] * (EDGE // 4), axis=0)
    row = lax.broadcasted_iota(jnp.int32, (EDGE, frames), 0)
    carries = (row < MORE) & (odd == 1) | (row >= EDGE - MORE) & (odd == 0)
    copies[1].wait()
    out_ref[:, frames:] = held[:, frames:]
    out_ref[:, :frames] = jnp.where(carries, stack, held[:, :frames].astype(F32)).astype(BF16)


def project_kernel(count, final_ref, *refs):
    sources, held = refs[:count], refs[count : 2 * count]
    final_out, final_held = refs[-3], refs[-2]
    final_copy = pltpu.make_async_copy(final_ref, final_held, refs[-1].at[count])
    projected_ref, hidden_ref, squeezed_ref, sums_ref, _, _, sems = refs[2 * count :]
    copies = [pltpu.make_async_copy(a, b, sems.at[i]) for i, (a, b) in enumerate(zip(sources, held))]
    for copy in copies:
        copy.start()
    final_copy.start()
    for copy in copies[:3]:
        copy.wait()
    sums = dot(jnp.ones((8, held[2].shape[1]), BF16), held[2][...], NT)
    sums_ref[...] = sums
    projected, hidden, squeezed = forward_rows(held[0][...], held[1][...], held[2][...], sums[0:1])
    projected_ref[...] = projected
    hidden_ref[...] = hidden
    squeezed_ref[...] = squeezed
    for copy in copies[3:]:
        copy.wait()
    final_copy.wait()
    final_out[...] = final_held[...].reshape(final_out.shape)


def shifted(values, taps, sign):
    count = values.shape[0]
    pieces = []
    for k in range(taps):
        amount = (-sign * (k - (taps - 1) // 2)) % count
        moved = values if amount == 0 else pltpu.roll(values, amount, 0)
        pieces.append(moved.astype(BF16))
    return pieces


PACK = (264, 160, 0, 240, 284)
PACKED = 288


ORDERS = ((1, 3, 2), (2, 1, 3))
SLOTS = [sum((k + 1) << (4 * bits) for k, bits in enumerate(order)) for order in ORDERS]


def final_rows(s, n):
    return min(s * (PK * C2 // n) // LANES, PK * C2 // LANES - 2)


def pieces_of(n, count, rows):
    found = []
    for s in range(n):
        at = s * count
        while at < (s + 1) * count:
            tap, row = divmod(at, rows)
            length = min(rows - row, (s + 1) * count - at)
            found.append((s, tap, row, at - s * count, length))
            at += length
    return found


def head_kernel(
    n,
    packed,
    squeezed_ref,
    sums_ref,
    edge_ref,
    cot_ref,
    hidden_ref,
    projection_ref,
    squeeze_ref,
    first_ref,
    second_ref,
    third_ref,
    final_ref,
    scores_ref,
    edge_scores_ref,
    delta_ref,
    edge_projected_ref,
    *outs,
):
    frames = squeezed_ref.shape[0]
    total = EDGE + frames
    seq, odd = here()
    row = lax.broadcasted_iota(jnp.int32, (total, LANES), 0)
    frame = row - jnp.where(row >= frames, odd * total, 0)
    before = jnp.where((odd == 1) & (seq > 0), REACH, 0)
    after = jnp.where((odd == 0) & (seq < n - 1), REACH, 0)
    inside = (frame >= -2 * before) & (frame < frames + 2 * after)
    first = jnp.where((odd == 0) & (seq > 0), REACH, -before)
    last = jnp.where((odd == 1) & (seq < n - 1), -REACH, after)
    window = (frame >= first) & (frame < frames + last)

    def mask(values, where):
        width = values.shape[1]
        if width <= LANES:
            return jnp.where(where[:, :width], values, 0.0)
        return jnp.concatenate(
            [jnp.where(where, values[:, i : i + LANES], 0.0) for i in range(0, width, LANES)], axis=1
        )

    edge_projected, edge_hidden, edge_squeezed = forward_rows(
        edge_ref[...], projection_ref[...], squeeze_ref[...], sums_ref[0:1, :]
    )
    edge_projected_ref[...] = edge_projected
    squeezed = jnp.concatenate([squeezed_ref[...], edge_squeezed], axis=0)

    parts = edge_ref[:, :LANES].astype(F32)
    parts = jnp.where(odd == 0, parts[EDGE - MORE :], parts[:MORE])
    parts = parts[0:1] + parts[1:2] + parts[2:3]
    columns = jnp.concatenate([cot_ref[...], parts, jnp.zeros((6, LANES), F32)], axis=0).T
    cot = jnp.concatenate(
        [
            jnp.broadcast_to(columns[:, 0:1], (frames, LANES)),
            jnp.broadcast_to(
                jnp.where(odd == 0, columns[:EDGE, 1:2], columns[frames - EDGE :, 1:2]), (EDGE, LANES)
            ),
        ],
        axis=0,
    )
    cot = mask(cot, inside)

    weights = (first_ref, second_ref, third_ref)
    act = squeezed
    inputs, slopes = [], []
    for ref in weights:
        unit, slope = leaky_pair(act)
        unit = mask(unit, inside)
        slopes.append(slope)
        inputs.append(mask(unit, window).astype(BF16))
        width = unit.shape[1]
        pieces = shifted(unit, HK, 1)
        if width % LANES == 0:
            act = dot(jnp.concatenate(pieces, axis=1), ref[...])
        else:
            act = jnp.zeros((total, ref.shape[1]), F32)
            for k, piece in enumerate(pieces):
                act = act + dot(piece, ref[k * width : (k + 1) * width, :])
    unit, slope = leaky_pair(act)
    final_in = mask(unit, inside).astype(BF16).astype(F32)
    taps = shifted(final_in, PK, 1)
    for ref, rows in ((scores_ref, slice(0, frames)), (edge_scores_ref, slice(total - LANES, total))):
        scores = jnp.zeros((1, rows.stop - rows.start), F32)
        for k in range(PK):
            scores = scores + dot(final_ref[:, k * C2 : (k + 1) * C2], taps[k][rows], NT)
        ref[...] = scores

    upstream = [jnp.zeros((total, LANES), F32)] * (C2 // LANES)
    final_grad = []
    final_in = mask(final_in, window)
    for k in range(PK):
        amount = (k - 1) % total
        moved = cot if amount == 0 else pltpu.roll(cot, amount, 0)
        for h in range(C2 // LANES):
            lanes = slice(k * C2 + h * LANES, k * C2 + (h + 1) * LANES)
            upstream[h] = upstream[h] + moved * final_ref[:, lanes].astype(F32)
            final_grad.append(
                jnp.sum(moved * final_in[:, h * LANES : (h + 1) * LANES], axis=0, keepdims=True)
            )
    upstream = jnp.concatenate(upstream, axis=1)
    slopes.append(slope)
    if packed:
        payload_ref, scratch = outs
        mine = [seq ^ s for s in range(n)]

        def block(s):
            q, z = mine[s] & 3, mine[s] >> 2
            holder = (z ^ (z >> 1)) & 1
            return holder ^ odd, (jnp.where(holder == 0, SLOTS[0], SLOTS[1]) >> (4 * q)) & 3, z >> 1

    def keep(layer, tap, grad):
        channels, cols = grad.shape
        if not packed:
            outs[layer + 1][tap * channels : (tap + 1) * channels, :] = grad
            return
        count = HK * channels // n
        for s, at, start, offset, length in pieces_of(n, count, channels):
            if at != tap:
                continue
            for h in range(cols // LANES):
                piece = grad[start : start + length, h * LANES : (h + 1) * LANES]
                first_row = PACK[layer] + h * count + offset
                if layer == 2:
                    payload_ref[(*block(s), slice(first_row, first_row + length))] = piece.astype(BF16)
                else:
                    scratch[s, first_row - PACK[1] : first_row - PACK[1] + length, :] = piece

    for layer in (2, 1, 0):
        delta = mask(upstream * slopes[layer + 1], inside)
        pieces = shifted(delta, HK, -1)
        rows = inputs[layer].T
        ref = weights[layer]
        width = ref.shape[0] // HK
        whole = jnp.concatenate([ref[k * width : (k + 1) * width, :] for k in range(HK)], axis=1)
        upstream = dot(jnp.concatenate(pieces, axis=1), whole, NT)
        for k, piece in enumerate(pieces):
            keep(layer, k, dot(rows, piece))
    delta = mask(upstream * slopes[0], inside)
    delta_ref[...] = delta.astype(BF16)
    hidden = jnp.concatenate([hidden_ref[...], edge_hidden], axis=0)
    squeeze_grad = dot(mask(delta, window).astype(BF16), hidden, TN)

    if not packed:
        outs[0][...] = squeeze_grad
        for i, part in enumerate(final_grad):
            outs[4][:, i * LANES : (i + 1) * LANES] = part
        return

    count = C0 // n
    for s in range(n):
        for h in range(squeeze_grad.shape[1] // LANES):
            first_row = PACK[3] - PACK[1] + h * count
            scratch[s, first_row : first_row + count, :] = squeeze_grad[
                s * count : (s + 1) * count, h * LANES : (h + 1) * LANES
            ]
        row = final_rows(s, n)
        first_row = PACK[4] - PACK[1]
        scratch[s, first_row : first_row + 1, :] = final_grad[row]
        scratch[s, first_row + 1 : first_row + 2, :] = final_grad[row + 1]
        scratch[s, first_row + 2 :, :] = jnp.zeros((PACKED - PACK[4] - 2, LANES), F32)
        payload_ref[(*block(s), slice(PACK[1], PACKED))] = scratch[s].astype(BF16)


def feature_kernel(
    rows_ref, edge_ref, projected_ref, edge_projected_ref, delta_ref, edge_scores_ref, squeeze_ref, projection_ref, out_ref, back_ref
):
    hidden_upstream = dot(delta_ref[...], squeeze_ref[...])
    projected = jnp.concatenate([projected_ref[...], edge_projected_ref[...]], axis=0)
    hidden_normed, hidden_inverse = normalize(projected.astype(F32))
    projected_grad = normalize_back(hidden_upstream, hidden_normed, hidden_inverse).astype(BF16)
    normed_grad = dot(projected_grad, projection_ref[...], NT)
    rows = jnp.concatenate([rows_ref[...], edge_ref[...]], axis=0)
    normed, inverse = normalize(rows.astype(F32))
    grad = normalize_back(normed_grad, normed, inverse)
    out_ref[...] = grad[:-EDGE]
    gone = jnp.where(here()[1] == 0, grad[-EDGE : BACK - EDGE], grad[-BACK:])
    row = lax.broadcasted_iota(jnp.int32, (BACK, LANES), 0)
    spare = jnp.where(here()[1] == 0, row, BACK - 1 - row) >= REACH
    back_ref[:, LANES:] = gone[:, LANES:].astype(BF16)
    parts = jnp.concatenate([in_parts(edge_scores_ref[...])] * (BACK // 4), axis=0)
    back_ref[:, :LANES] = jnp.where(spare, parts, gone[:, :LANES]).astype(BF16)


def assemble_kernel(n, own_ref, scores_ref, back_ref, grad_ref, final_scores_ref):
    frames = own_ref.shape[0]
    seq, odd = here()
    low, high = (odd == 0) & (seq > 0), (odd == 1) & (seq < n - 1)
    grad_ref[BACK : frames - BACK, :] = own_ref[BACK : frames - BACK, :]
    row = lax.broadcasted_iota(jnp.int32, (BACK, own_ref.shape[1]), 0)
    came = back_ref[...].astype(F32)
    grad_ref[:BACK, :] = jnp.where(low & (row < REACH), came, own_ref[:BACK, :])
    grad_ref[frames - BACK :, :] = jnp.where(high & (row >= BACK - REACH), came, own_ref[frames - BACK :, :])
    parts = jnp.where(odd == 0, came[BACK - 4 :, :LANES], came[:4, :LANES])
    scores = jnp.broadcast_to(parts[0:1] + parts[1:2] + parts[2:3], (8, LANES))
    moved = pltpu.roll(scores, EDGE, 1)
    lane = lax.broadcasted_iota(jnp.int32, (1, frames), 1)
    kept = jnp.where(high & (lane >= frames - REACH), scores[0:1], scores_ref[...])
    final_scores_ref[...] = jnp.where(low & (lane < REACH), moved[0:1], kept)


def unpack_kernel(n, factor, mine_ref, other_ref, squeeze_ref, first_ref, second_ref, third_ref, final_ref, both):
    both[...] = (mine_ref[...].astype(F32) + other_ref[...].astype(F32)) * factor
    for base, ref in zip(PACK, (first_ref, second_ref, third_ref, squeeze_ref)):
        count = ref.shape[0]
        for h in range(ref.shape[1] // LANES):
            ref[:, h * LANES : (h + 1) * LANES] = both[base + h * count : base + (h + 1) * count, :]
    count = final_ref.shape[1]
    at = here()[0] * count
    at = at - jnp.minimum(lax.div(at, LANES), PK * C2 // LANES - 2) * LANES
    pair = jnp.concatenate([both[PACK[4] : PACK[4] + 1, :], both[PACK[4] + 1 : PACK[4] + 2, :]], axis=1)
    pair = pltpu.roll(jnp.broadcast_to(pair, (8, 2 * LANES)), lax.rem(2 * LANES - at, 2 * LANES), 1)
    final_ref[...] = pair[0:1, :count]


def sds(shape, dtype):
    return jax.ShapeDtypeStruct(shape, dtype)


def hbm(array):
    return pltpu.with_memory_space_constraint(array, pltpu.HBM)


def vmem(shape, dtype):
    return pltpu.VMEM(shape, dtype)


VMEM = pl.BlockSpec(memory_space=pltpu.VMEM)
HBM = pl.BlockSpec(memory_space=pltpu.HBM)


def params(mib):
    return pltpu.CompilerParams(vmem_limit_bytes=mib * 1024 * 1024)


def cost(flops, nbytes):
    return pl.CostEstimate(flops=flops, bytes_accessed=nbytes, transcendentals=0)


def shards(
    features,
    score_cotangent,
    projection_weight,
    squeeze_weight,
    first_weight,
    second_weight,
    third_weight,
    final_weight,
):
    n, cores = lax.axis_size("seq"), lax.axis_size("dp")
    frames, feat = features.shape[1:]
    width = projection_weight.shape[1]
    packed = n == 16 and cores == 2
    rows = features.reshape(frames, feat)
    along = []
    for i in range(0, cores * n, n):
        down = [(i + j + 1, i + j) for j in range(n - 1)]
        along += down if i // n % 2 == 0 else [(target, source) for source, target in down]
    for i in range(0, (cores // 2) * 2 * n, 2 * n):
        along += [(i, i + n), (i + 2 * n - 1, i + n - 1)]
    along = sorted(along)
    returning = sorted((target, source) for source, target in along)

    edge = pl.pallas_call(
        edge_kernel,
        in_specs=[HBM, HBM],
        out_specs=VMEM,
        out_shape=vmem((EDGE, feat), BF16),
        scratch_shapes=[pltpu.VMEM((EDGE, feat), BF16), pltpu.VMEM((1, frames), F32), pltpu.SemaphoreType.DMA((2,))],
        name="edge",
    )(hbm(rows), hbm(score_cotangent))
    edge = lax.ppermute(edge, ("dp", "seq"), along)

    sources = (
        rows,
        projection_weight,
        squeeze_weight,
        score_cotangent,
        first_weight,
        second_weight,
        third_weight,
    )
    rows, projection, squeeze, cot, first, second, third, projected, hidden, squeezed, sums, final = pl.pallas_call(
        functools.partial(project_kernel, len(sources)),
        in_specs=[HBM] * (1 + len(sources)),
        out_specs=[VMEM] * (len(sources) + 5),
        out_shape=[
            *[vmem(a.shape, a.dtype) for a in sources],
            vmem((frames, width), BF16),
            vmem((frames, width), BF16),
            vmem((frames, C0), F32),
            vmem((8, C0), F32),
            vmem((1, PK * C2), BF16),
        ],
        scratch_shapes=[pltpu.VMEM((PK * C2,), BF16), pltpu.SemaphoreType.DMA((len(sources) + 1,))],
        compiler_params=params(8),
        cost_estimate=cost(2 * frames * width * (feat + C0), 2 * feat * width),
        name="project",
    )(hbm(final_weight), *[hbm(a) for a in sources])

    if packed:
        grad_shapes = [sds((2, 4, 2, PACKED, LANES), BF16)]
        scratch = [pltpu.VMEM((n, PACKED - PACK[1], LANES), F32)]
    else:
        grad_shapes = [
            sds((C0, width), F32),
            sds(first_weight.shape, F32),
            sds(second_weight.shape, F32),
            sds(third_weight.shape, F32),
            sds((1, PK * C2), F32),
        ]
        scratch = []
    own_scores, after, delta, edge_projected, *grads = pl.pallas_call(
        functools.partial(head_kernel, n, packed),
        in_specs=[VMEM] * 11,
        out_specs=[VMEM] * (4 + len(grad_shapes)),
        out_shape=[
            sds((1, frames), F32),
            sds((1, LANES), F32),
            sds((frames + EDGE, C0), BF16),
            sds((EDGE, width), BF16),
            *grad_shapes,
        ],
        scratch_shapes=scratch,
        compiler_params=params(20),
        cost_estimate=cost(10**9, 4 * 10**6),
        name="head",
    )(
        squeezed,
        sums,
        edge,
        cot,
        hidden,
        projection,
        squeeze,
        first,
        second,
        third,
        final,
    )

    def features_back():
        own_grad, back = pl.pallas_call(
            feature_kernel,
            in_specs=[VMEM] * 8,
            out_specs=[VMEM] * 2,
            out_shape=[sds((frames, feat), F32), sds((BACK, feat), BF16)],
            compiler_params=params(8),
            cost_estimate=cost(2 * frames * width * (feat + C0), 2 * feat * width),
            name="feature",
        )(rows, edge, projected, edge_projected, delta, after, squeeze, projection)
        back = lax.ppermute(back, ("dp", "seq"), returning)
        return own_grad, back

    def assembled(own_grad, back):
        feature_grad, scores = pl.pallas_call(
            functools.partial(assemble_kernel, n),
            in_specs=[VMEM] * 3,
            out_specs=[VMEM] * 2,
            out_shape=[sds((frames, feat), F32), sds((1, frames), F32)],
            compiler_params=params(4),
            cost_estimate=cost(frames * feat, 8 * frames * feat),
            name="assemble",
        )(own_grad, own_scores, back)
        return feature_grad[None], scores

    factor = 1.0 / math.sqrt(cores * n * frames)
    if not packed:
        shares = []
        for term in grads[:4] + [grads[4].reshape(PK * C2)]:
            part = lax.psum_scatter(term * factor, "seq", scatter_dimension=0, tiled=True)
            shares.append(lax.psum(part.astype(BF16), "dp").astype(F32))
        feature_grad, scores = assembled(*features_back())
        return (scores, feature_grad, *shares)

    def added(*terms):
        total = terms[0].astype(F32)
        for term in terms[1:]:
            total = total + term.astype(F32)
        return total.astype(BF16)

    def mixed(zero, one):
        return [(i, i ^ zero) for i in range(n)] + [(n + i, n + (i ^ one)) for i in range(n)]

    swap = [(0, 1), (1, 0)]
    (payload,) = grads
    came = lax.ppermute(payload[1], "dp", swap)
    own_grad, back = features_back()
    held = [added(payload[0, j], came[j]) for j in range(4)]
    moved = [lax.ppermute(held[1 + k], ("dp", "seq"), mixed(*pair)) for k, pair in enumerate(zip(*ORDERS))]
    held = [added(held[0][i], *(part[i] for part in moved)) for i in range(2)]
    held, back, own_grad = lax.optimization_barrier((held, back, own_grad))
    held = added(
        lax.ppermute(held[1], ("dp", "seq"), mixed(12, 8)), lax.ppermute(held[0], ("dp", "seq"), mixed(0, 4))
    )
    feature_grad, scores = assembled(own_grad, back)
    held, feature_grad, scores = lax.optimization_barrier((held, feature_grad, scores))
    other = lax.ppermute(held, "dp", swap)
    shapes = [
        (C0 // n, width),
        (HK * C0 // n, C1),
        (HK * C1 // n, C2),
        (HK * C2 // n, C2),
        (1, PK * C2 // n),
    ]
    *shares, final = pl.pallas_call(
        functools.partial(unpack_kernel, n, factor),
        in_specs=[VMEM, VMEM],
        out_specs=[VMEM] * 5,
        out_shape=[sds(shape, F32) for shape in shapes],
        scratch_shapes=[pltpu.VMEM((PACKED, LANES), F32)],
        compiler_params=params(4),
        name="unpack",
    )(held, other)
    return (scores, feature_grad, *shares, final.reshape(PK * C2 // n))


def solution(mesh):
    placed = (P("dp", "seq", None), P("dp", "seq"), P(), P(), P(), P(), P(), P())
    return jax.shard_map(
        shards,
        mesh=mesh,
        in_specs=placed,
        out_specs=(
            P("dp", "seq"),
            P("dp", "seq", None),
            P("seq", None),
            P("seq", None),
            P("seq", None),
            P("seq", None),
            P("seq"),
        ),
        check_vma=False,
    )
```

```python
import functools
import math

import jax
import jax.numpy as jnp
from jax import lax
from jax.experimental import pallas as pl
from jax.experimental.pallas import tpu as pltpu
from jax.sharding import PartitionSpec as P

C0 = 64
C1 = 128
C2 = 256
HK = 5
PK = 3
EDGE = 32
REACH = 12
MORE = 8
BACK = 16
LANES = 128

EPSILON = 1e-05
SLOPE = 0.1
BF16 = jnp.bfloat16
F32 = jnp.float32
NT = (((1,), (1,)), ((), ()))
TN = (((0,), (0,)), ((), ()))


def normalize(values):
    average = jnp.mean(values, axis=-1, keepdims=True)
    centred = values - average
    variance = jnp.mean(centred * centred, axis=-1, keepdims=True)
    inverse = lax.rsqrt(variance + EPSILON)
    return (centred * inverse, inverse)


def normalize_back(upstream, normed, inverse):
    first_mean = jnp.mean(upstream, axis=-1, keepdims=True)
    second_mean = jnp.mean(upstream * normed, axis=-1, keepdims=True)
    return (upstream - first_mean - normed * second_mean) * inverse


def leaky_pair(values):
    cumulative = 0.5 * (1.0 + lax.erf(values * math.sqrt(0.5)))
    density = jnp.exp(-0.5 * values * values) * (1.0 / math.sqrt(2.0 * math.pi))
    unit = SLOPE * values + (1.0 - SLOPE) * (values * cumulative)
    slope = SLOPE + (1.0 - SLOPE) * (cumulative + values * density)
    return unit, slope


def dot(a, b, dims=(((1,), (0,)), ((), ()))):
    return lax.dot_general(a, b, dims, preferred_element_type=F32)


def forward_rows(rows, projection, squeeze, sums):
    normed, _ = normalize(rows.astype(F32))
    projected = dot(normed.astype(BF16), projection).astype(BF16)
    wide = projected.astype(F32)
    average = jnp.mean(wide, axis=-1, keepdims=True)
    centred = wide - average
    inverse = lax.rsqrt(jnp.mean(centred * centred, axis=-1, keepdims=True) + EPSILON)
    squeezed = (dot(projected, squeeze, NT) - average * sums) * inverse
    return projected, (centred * inverse).astype(BF16), squeezed


def here():
    return lax.axis_index("seq"), lax.rem(lax.axis_index("dp"), 2)


def in_parts(values):
    high = values.astype(BF16).astype(F32)
    middle = (values - high).astype(BF16).astype(F32)
    return jnp.concatenate([high, middle, values - high - middle, jnp.zeros_like(values)], axis=0)


def edge_kernel(rows_ref, cot_ref, out_ref, held, cot_held, sems):
    frames, feat = rows_ref.shape
    _, odd = here()
    start = pl.multiple_of(odd * (frames - EDGE), 16)
    copies = [
        pltpu.make_async_copy(cot_ref, cot_held, sems.at[0]),
        pltpu.make_async_copy(rows_ref.at[pl.ds(start, EDGE)], held, sems.at[1]),
    ]
    for copy in copies:
        copy.start()
    copies[0].wait()
    cot = cot_held[...]
    stack = jnp.concatenate([in_parts(cot)] * (EDGE // 4), axis=0)
    row = lax.broadcasted_iota(jnp.int32, (EDGE, frames), 0)
    carries = (row < MORE) & (odd == 1) | (row >= EDGE - MORE) & (odd == 0)
    copies[1].wait()
    out_ref[:, frames:] = held[:, frames:]
    out_ref[:, :frames] = jnp.where(carries, stack, held[:, :frames].astype(F32)).astype(BF16)


def project_kernel(count, final_ref, *refs):
    sources, held = refs[:count], refs[count : 2 * count]
    final_out, final_held = refs[-3], refs[-2]
    final_copy = pltpu.make_async_copy(final_ref, final_held, refs[-1].at[count])
    projected_ref, hidden_ref, squeezed_ref, sums_ref, _, _, sems = refs[2 * count :]
    copies = [pltpu.make_async_copy(a, b, sems.at[i]) for i, (a, b) in enumerate(zip(sources, held))]
    for copy in copies:
        copy.start()
    final_copy.start()
    for copy in copies[:3]:
        copy.wait()
    sums = dot(jnp.ones((8, held[2].shape[1]), BF16), held[2][...], NT)
    sums_ref[...] = sums
    projected, hidden, squeezed = forward_rows(held[0][...], held[1][...], held[2][...], sums[0:1])
    projected_ref[...] = projected
    hidden_ref[...] = hidden
    squeezed_ref[...] = squeezed
    for copy in copies[3:]:
        copy.wait()
    final_copy.wait()
    final_out[...] = final_held[...].reshape(final_out.shape)


def shifted(values, taps, sign):
    count = values.shape[0]
    pieces = []
    for k in range(taps):
        amount = (-sign * (k - (taps - 1) // 2)) % count
        moved = values if amount == 0 else pltpu.roll(values, amount, 0)
        pieces.append(moved.astype(BF16))
    return pieces


PACK = (264, 160, 0, 240, 284)
PACKED = 288


ORDERS = ((1, 3, 2), (2, 1, 3))
SLOTS = [sum((k + 1) << (4 * bits) for k, bits in enumerate(order)) for order in ORDERS]


def final_rows(s, n):
    return min(s * (PK * C2 // n) // LANES, PK * C2 // LANES - 2)


def pieces_of(n, count, rows):
    found = []
    for s in range(n):
        at = s * count
        while at < (s + 1) * count:
            tap, row = divmod(at, rows)
            length = min(rows - row, (s + 1) * count - at)
            found.append((s, tap, row, at - s * count, length))
            at += length
    return found


def head_kernel(
    n,
    packed,
    squeezed_ref,
    sums_ref,
    edge_ref,
    cot_ref,
    hidden_ref,
    projection_ref,
    squeeze_ref,
    first_ref,
    second_ref,
    third_ref,
    final_ref,
    scores_ref,
    edge_scores_ref,
    delta_ref,
    edge_projected_ref,
    *outs,
):
    frames = squeezed_ref.shape[0]
    total = EDGE + frames
    seq, odd = here()
    row = lax.broadcasted_iota(jnp.int32, (total, LANES), 0)
    frame = row - jnp.where(row >= frames, odd * total, 0)
    before = jnp.where((odd == 1) & (seq > 0), REACH, 0)
    after = jnp.where((odd == 0) & (seq < n - 1), REACH, 0)
    inside = (frame >= -2 * before) & (frame < frames + 2 * after)
    first = jnp.where((odd == 0) & (seq > 0), REACH, -before)
    last = jnp.where((odd == 1) & (seq < n - 1), -REACH, after)
    window = (frame >= first) & (frame < frames + last)

    def mask(values, where):
        width = values.shape[1]
        if width <= LANES:
            return jnp.where(where[:, :width], values, 0.0)
        return jnp.concatenate(
            [jnp.where(where, values[:, i : i + LANES], 0.0) for i in range(0, width, LANES)], axis=1
        )

    edge_projected, edge_hidden, edge_squeezed = forward_rows(
        edge_ref[...], projection_ref[...], squeeze_ref[...], sums_ref[0:1, :]
    )
    edge_projected_ref[...] = edge_projected
    squeezed = jnp.concatenate([squeezed_ref[...], edge_squeezed], axis=0)

    parts = edge_ref[:, :LANES].astype(F32)
    parts = jnp.where(odd == 0, parts[EDGE - MORE :], parts[:MORE])
    parts = parts[0:1] + parts[1:2] + parts[2:3]
    columns = jnp.concatenate([cot_ref[...], parts, jnp.zeros((6, LANES), F32)], axis=0).T
    cot = jnp.concatenate(
        [
            jnp.broadcast_to(columns[:, 0:1], (frames, LANES)),
            jnp.broadcast_to(
                jnp.where(odd == 0, columns[:EDGE, 1:2], columns[frames - EDGE :, 1:2]), (EDGE, LANES)
            ),
        ],
        axis=0,
    )
    cot = mask(cot, inside)

    weights = (first_ref, second_ref, third_ref)
    act = squeezed
    inputs, slopes = [], []
    for ref in weights:
        unit, slope = leaky_pair(act)
        unit = mask(unit, inside)
        slopes.append(slope)
        inputs.append(mask(unit, window).astype(BF16))
        width = unit.shape[1]
        pieces = shifted(unit, HK, 1)
        if width % LANES == 0:
            act = dot(jnp.concatenate(pieces, axis=1), ref[...])
        else:
            act = jnp.zeros((total, ref.shape[1]), F32)
            for k, piece in enumerate(pieces):
                act = act + dot(piece, ref[k * width : (k + 1) * width, :])
    unit, slope = leaky_pair(act)
    final_in = mask(unit, inside).astype(BF16).astype(F32)
    taps = shifted(final_in, PK, 1)
    for ref, rows in ((scores_ref, slice(0, frames)), (edge_scores_ref, slice(total - LANES, total))):
        scores = jnp.zeros((1, rows.stop - rows.start), F32)
        for k in range(PK):
            scores = scores + dot(final_ref[:, k * C2 : (k + 1) * C2], taps[k][rows], NT)
        ref[...] = scores

    upstream = [jnp.zeros((total, LANES), F32)] * (C2 // LANES)
    final_grad = []
    final_in = mask(final_in, window)
    for k in range(PK):
        amount = (k - 1) % total
        moved = cot if amount == 0 else pltpu.roll(cot, amount, 0)
        for h in range(C2 // LANES):
            lanes = slice(k * C2 + h * LANES, k * C2 + (h + 1) * LANES)
            upstream[h] = upstream[h] + moved * final_ref[:, lanes].astype(F32)
            final_grad.append(
                jnp.sum(moved * final_in[:, h * LANES : (h + 1) * LANES], axis=0, keepdims=True)
            )
    upstream = jnp.concatenate(upstream, axis=1)
    slopes.append(slope)
    if packed:
        payload_ref, scratch = outs
        mine = [seq ^ s for s in range(n)]

        def block(s):
            q, z = mine[s] & 3, mine[s] >> 2
            holder = (z ^ (z >> 1)) & 1
            return holder ^ odd, (jnp.where(holder == 0, SLOTS[0], SLOTS[1]) >> (4 * q)) & 3, z >> 1

    def keep(layer, tap, grad):
        channels, cols = grad.shape
        if not packed:
            outs[layer + 1][tap * channels : (tap + 1) * channels, :] = grad
            return
        count = HK * channels // n
        for s, at, start, offset, length in pieces_of(n, count, channels):
            if at != tap:
                continue
            for h in range(cols // LANES):
                piece = grad[start : start + length, h * LANES : (h + 1) * LANES]
                first_row = PACK[layer] + h * count + offset
                if layer == 2:
                    payload_ref[(*block(s), slice(first_row, first_row + length))] = piece.astype(BF16)
                else:
                    scratch[s, first_row - PACK[1] : first_row - PACK[1] + length, :] = piece

    for layer in (2, 1, 0):
        delta = mask(upstream * slopes[layer + 1], inside)
        pieces = shifted(delta, HK, -1)
        rows = inputs[layer].T
        ref = weights[layer]
        width = ref.shape[0] // HK
        whole = jnp.concatenate([ref[k * width : (k + 1) * width, :] for k in range(HK)], axis=1)
        upstream = dot(jnp.concatenate(pieces, axis=1), whole, NT)
        grad = dot(rows, jnp.concatenate(pieces, axis=1))
        cols = grad.shape[1] // HK
        for k in range(HK):
            keep(layer, k, grad[:, k * cols : (k + 1) * cols])
    delta = mask(upstream * slopes[0], inside)
    delta_ref[...] = delta.astype(BF16)
    hidden = jnp.concatenate([hidden_ref[...], edge_hidden], axis=0)
    squeeze_grad = dot(mask(delta, window).astype(BF16), hidden, TN)

    if not packed:
        outs[0][...] = squeeze_grad
        for i, part in enumerate(final_grad):
            outs[4][:, i * LANES : (i + 1) * LANES] = part
        return

    count = C0 // n
    for s in range(n):
        for h in range(squeeze_grad.shape[1] // LANES):
            first_row = PACK[3] - PACK[1] + h * count
            scratch[s, first_row : first_row + count, :] = squeeze_grad[
                s * count : (s + 1) * count, h * LANES : (h + 1) * LANES
            ]
        row = final_rows(s, n)
        first_row = PACK[4] - PACK[1]
        scratch[s, first_row : first_row + 1, :] = final_grad[row]
        scratch[s, first_row + 1 : first_row + 2, :] = final_grad[row + 1]
        scratch[s, first_row + 2 :, :] = jnp.zeros((PACKED - PACK[4] - 2, LANES), F32)
        payload_ref[(*block(s), slice(PACK[1], PACKED))] = scratch[s].astype(BF16)


def feature_kernel(
    rows_ref, edge_ref, projected_ref, edge_projected_ref, delta_ref, edge_scores_ref, squeeze_ref, projection_ref, out_ref, back_ref
):
    hidden_upstream = dot(delta_ref[...], squeeze_ref[...])
    projected = jnp.concatenate([projected_ref[...], edge_projected_ref[...]], axis=0)
    hidden_normed, hidden_inverse = normalize(projected.astype(F32))
    projected_grad = normalize_back(hidden_upstream, hidden_normed, hidden_inverse).astype(BF16)
    normed_grad = dot(projected_grad, projection_ref[...], NT)
    rows = jnp.concatenate([rows_ref[...], edge_ref[...]], axis=0)
    normed, inverse = normalize(rows.astype(F32))
    grad = normalize_back(normed_grad, normed, inverse)
    out_ref[...] = grad[:-EDGE]
    gone = jnp.where(here()[1] == 0, grad[-EDGE : BACK - EDGE], grad[-BACK:])
    row = lax.broadcasted_iota(jnp.int32, (BACK, LANES), 0)
    spare = jnp.where(here()[1] == 0, row, BACK - 1 - row) >= REACH
    back_ref[:, LANES:] = gone[:, LANES:].astype(BF16)
    parts = jnp.concatenate([in_parts(edge_scores_ref[...])] * (BACK // 4), axis=0)
    back_ref[:, :LANES] = jnp.where(spare, parts, gone[:, :LANES]).astype(BF16)


def assemble_kernel(n, own_ref, scores_ref, back_ref, grad_ref, final_scores_ref):
    frames = own_ref.shape[0]
    seq, odd = here()
    low, high = (odd == 0) & (seq > 0), (odd == 1) & (seq < n - 1)
    grad_ref[BACK : frames - BACK, :] = own_ref[BACK : frames - BACK, :]
    row = lax.broadcasted_iota(jnp.int32, (BACK, own_ref.shape[1]), 0)
    came = back_ref[...].astype(F32)
    grad_ref[:BACK, :] = jnp.where(low & (row < REACH), came, own_ref[:BACK, :])
    grad_ref[frames - BACK :, :] = jnp.where(high & (row >= BACK - REACH), came, own_ref[frames - BACK :, :])
    parts = jnp.where(odd == 0, came[BACK - 4 :, :LANES], came[:4, :LANES])
    scores = jnp.broadcast_to(parts[0:1] + parts[1:2] + parts[2:3], (8, LANES))
    moved = pltpu.roll(scores, EDGE, 1)
    lane = lax.broadcasted_iota(jnp.int32, (1, frames), 1)
    kept = jnp.where(high & (lane >= frames - REACH), scores[0:1], scores_ref[...])
    final_scores_ref[...] = jnp.where(low & (lane < REACH), moved[0:1], kept)


def unpack_kernel(n, factor, mine_ref, other_ref, squeeze_ref, first_ref, second_ref, third_ref, final_ref, both):
    both[...] = (mine_ref[...].astype(F32) + other_ref[...].astype(F32)) * factor
    for base, ref in zip(PACK, (first_ref, second_ref, third_ref, squeeze_ref)):
        count = ref.shape[0]
        for h in range(ref.shape[1] // LANES):
            ref[:, h * LANES : (h + 1) * LANES] = both[base + h * count : base + (h + 1) * count, :]
    count = final_ref.shape[1]
    at = here()[0] * count
    at = at - jnp.minimum(lax.div(at, LANES), PK * C2 // LANES - 2) * LANES
    pair = jnp.concatenate([both[PACK[4] : PACK[4] + 1, :], both[PACK[4] + 1 : PACK[4] + 2, :]], axis=1)
    pair = pltpu.roll(jnp.broadcast_to(pair, (8, 2 * LANES)), lax.rem(2 * LANES - at, 2 * LANES), 1)
    final_ref[...] = pair[0:1, :count]


def sds(shape, dtype):
    return jax.ShapeDtypeStruct(shape, dtype)


def hbm(array):
    return pltpu.with_memory_space_constraint(array, pltpu.HBM)


def vmem(shape, dtype):
    return pltpu.VMEM(shape, dtype)


VMEM = pl.BlockSpec(memory_space=pltpu.VMEM)
HBM = pl.BlockSpec(memory_space=pltpu.HBM)


def params(mib):
    return pltpu.CompilerParams(vmem_limit_bytes=mib * 1024 * 1024)


def cost(flops, nbytes):
    return pl.CostEstimate(flops=flops, bytes_accessed=nbytes, transcendentals=0)


def shards(
    features,
    score_cotangent,
    projection_weight,
    squeeze_weight,
    first_weight,
    second_weight,
    third_weight,
    final_weight,
):
    n, cores = lax.axis_size("seq"), lax.axis_size("dp")
    frames, feat = features.shape[1:]
    width = projection_weight.shape[1]
    packed = n == 16 and cores == 2
    rows = features.reshape(frames, feat)
    along = []
    for i in range(0, cores * n, n):
        down = [(i + j + 1, i + j) for j in range(n - 1)]
        along += down if i // n % 2 == 0 else [(target, source) for source, target in down]
    for i in range(0, (cores // 2) * 2 * n, 2 * n):
        along += [(i, i + n), (i + 2 * n - 1, i + n - 1)]
    along = sorted(along)
    returning = sorted((target, source) for source, target in along)

    edge = pl.pallas_call(
        edge_kernel,
        in_specs=[HBM, HBM],
        out_specs=VMEM,
        out_shape=vmem((EDGE, feat), BF16),
        scratch_shapes=[pltpu.VMEM((EDGE, feat), BF16), pltpu.VMEM((1, frames), F32), pltpu.SemaphoreType.DMA((2,))],
        name="edge",
    )(hbm(rows), hbm(score_cotangent))
    edge = lax.ppermute(edge, ("dp", "seq"), along)

    sources = (
        rows,
        projection_weight,
        squeeze_weight,
        score_cotangent,
        first_weight,
        second_weight,
        third_weight,
    )
    rows, projection, squeeze, cot, first, second, third, projected, hidden, squeezed, sums, final = pl.pallas_call(
        functools.partial(project_kernel, len(sources)),
        in_specs=[HBM] * (1 + len(sources)),
        out_specs=[VMEM] * (len(sources) + 5),
        out_shape=[
            *[vmem(a.shape, a.dtype) for a in sources],
            vmem((frames, width), BF16),
            vmem((frames, width), BF16),
            vmem((frames, C0), F32),
            vmem((8, C0), F32),
            vmem((1, PK * C2), BF16),
        ],
        scratch_shapes=[pltpu.VMEM((PK * C2,), BF16), pltpu.SemaphoreType.DMA((len(sources) + 1,))],
        compiler_params=params(8),
        cost_estimate=cost(2 * frames * width * (feat + C0), 2 * feat * width),
        name="project",
    )(hbm(final_weight), *[hbm(a) for a in sources])

    if packed:
        grad_shapes = [sds((2, 4, 2, PACKED, LANES), BF16)]
        scratch = [pltpu.VMEM((n, PACKED - PACK[1], LANES), F32)]
    else:
        grad_shapes = [
            sds((C0, width), F32),
            sds(first_weight.shape, F32),
            sds(second_weight.shape, F32),
            sds(third_weight.shape, F32),
            sds((1, PK * C2), F32),
        ]
        scratch = []
    own_scores, after, delta, edge_projected, *grads = pl.pallas_call(
        functools.partial(head_kernel, n, packed),
        in_specs=[VMEM] * 11,
        out_specs=[VMEM] * (4 + len(grad_shapes)),
        out_shape=[
            sds((1, frames), F32),
            sds((1, LANES), F32),
            sds((frames + EDGE, C0), BF16),
            sds((EDGE, width), BF16),
            *grad_shapes,
        ],
        scratch_shapes=scratch,
        compiler_params=params(20),
        cost_estimate=cost(10**9, 4 * 10**6),
        name="head",
    )(
        squeezed,
        sums,
        edge,
        cot,
        hidden,
        projection,
        squeeze,
        first,
        second,
        third,
        final,
    )

    def features_back():
        own_grad, back = pl.pallas_call(
            feature_kernel,
            in_specs=[VMEM] * 8,
            out_specs=[VMEM] * 2,
            out_shape=[sds((frames, feat), F32), sds((BACK, feat), BF16)],
            compiler_params=params(8),
            cost_estimate=cost(2 * frames * width * (feat + C0), 2 * feat * width),
            name="feature",
        )(rows, edge, projected, edge_projected, delta, after, squeeze, projection)
        back = lax.ppermute(back, ("dp", "seq"), returning)
        return own_grad, back

    def assembled(own_grad, back):
        feature_grad, scores = pl.pallas_call(
            functools.partial(assemble_kernel, n),
            in_specs=[VMEM] * 3,
            out_specs=[VMEM] * 2,
            out_shape=[sds((frames, feat), F32), sds((1, frames), F32)],
            compiler_params=params(4),
            cost_estimate=cost(frames * feat, 8 * frames * feat),
            name="assemble",
        )(own_grad, own_scores, back)
        return feature_grad[None], scores

    factor = 1.0 / math.sqrt(cores * n * frames)
    if not packed:
        shares = []
        for term in grads[:4] + [grads[4].reshape(PK * C2)]:
            part = lax.psum_scatter(term * factor, "seq", scatter_dimension=0, tiled=True)
            shares.append(lax.psum(part.astype(BF16), "dp").astype(F32))
        feature_grad, scores = assembled(*features_back())
        return (scores, feature_grad, *shares)

    def added(*terms):
        total = terms[0].astype(F32)
        for term in terms[1:]:
            total = total + term.astype(F32)
        return total.astype(BF16)

    def mixed(zero, one):
        return [(i, i ^ zero) for i in range(n)] + [(n + i, n + (i ^ one)) for i in range(n)]

    swap = [(0, 1), (1, 0)]
    (payload,) = grads
    came = lax.ppermute(payload[1], "dp", swap)
    own_grad, back = features_back()
    came, own_grad = lax.optimization_barrier((came, own_grad))
    held = [added(payload[0, j], came[j]) for j in range(4)]
    moved = [lax.ppermute(held[1 + k], ("dp", "seq"), mixed(*pair)) for k, pair in enumerate(zip(*ORDERS))]
    held = [added(held[0][i], *(part[i] for part in moved)) for i in range(2)]
    held, back = lax.optimization_barrier((held, back))
    held = added(
        lax.ppermute(held[1], ("dp", "seq"), mixed(12, 8)), lax.ppermute(held[0], ("dp", "seq"), mixed(0, 4))
    )
    feature_grad, scores = assembled(own_grad, back)
    held, feature_grad, scores = lax.optimization_barrier((held, feature_grad, scores))
    other = lax.ppermute(held, "dp", swap)
    shapes = [
        (C0 // n, width),
        (HK * C0 // n, C1),
        (HK * C1 // n, C2),
        (HK * C2 // n, C2),
        (1, PK * C2 // n),
    ]
    *shares, final = pl.pallas_call(
        functools.partial(unpack_kernel, n, factor),
        in_specs=[VMEM, VMEM],
        out_specs=[VMEM] * 5,
        out_shape=[sds(shape, F32) for shape in shapes],
        scratch_shapes=[pltpu.VMEM((PACKED, LANES), F32)],
        compiler_params=params(4),
        name="unpack",
    )(held, other)
    return (scores, feature_grad, *shares, final.reshape(PK * C2 // n))


def solution(mesh):
    placed = (P("dp", "seq", None), P("dp", "seq"), P(), P(), P(), P(), P(), P())
    return jax.shard_map(
        shards,
        mesh=mesh,
        in_specs=placed,
        out_specs=(
            P("dp", "seq"),
            P("dp", "seq", None),
            P("seq", None),
            P("seq", None),
            P("seq", None),
            P("seq", None),
            P("seq"),
        ),
        check_vma=False,
    )
```
